32 devices in a mesh: seq: 16 (over z, y, x), tp: 2 (over core).
Axes of the slice: x: 2, y: 2, z: 4, core: 2. Of those that a mesh axis runs over, the one named last changes fastest.
Arguments:
- tokens: float32 [4096, 768], P('seq'), may hold values from -6 to 6
- cotangent: float32 [4096, 768], P('seq'), may hold values from -6 to 6
- norm1_gain: float32 [768], replicated, may hold values from 0.5 to 1.5
- norm1_bias: float32 [768], replicated, may hold values from -1.75 to 1.75
- query_weight: float32 [768, 768], P(None, 'tp'), may hold values from -0.21875 to 0.21875
- query_bias: float32 [768], P('tp'), may hold values from -1.75 to 1.75
- key_weight: float32 [768, 768], P(None, 'tp'), may hold values from -0.21875 to 0.21875
- key_bias: float32 [768], P('tp'), may hold values from -1.75 to 1.75
- value_weight: float32 [768, 768], P(None, 'tp'), may hold values from -0.21875 to 0.21875
- value_bias: float32 [768], P('tp'), may hold values from -1.75 to 1.75
- shift_kernel: float32 [4, 768], P(None, 'tp'), may hold values from -3 to 3
- log_step: float32 [768], P('tp'), as said below
- state_rate: float32 [64, 768], P(None, 'tp'), may hold values from 1 to 64
- state_out: float32 [64, 768], P(None, 'tp'), may hold values from -0.75 to 0.75
- skip_gain: float32 [768], P('tp'), may hold values from -4 to 4
- out_weight: float32 [768, 768], P('tp'), may hold values from -0.21875 to 0.21875
- out_bias: float32 [768], replicated, may hold values from -1.75 to 1.75
- norm2_gain: float32 [768], replicated, may hold values from 0.5 to 1.5
- norm2_bias: float32 [768], replicated, may hold values from -1.75 to 1.75
- up_weight: float32 [768, 3072], P(None, 'tp'), may hold values from -0.21875 to 0.21875
- up_bias: float32 [3072], P('tp'), may hold values from -1.75 to 1.75
- down_weight: float32 [3072, 768], P('tp'), may hold values from -0.109375 to 0.109375
- down_bias: float32 [768], replicated, may hold values from -1.75 to 1.75
Outputs:
- block_out: float32 [4096, 768], P('seq')
- input_grad: float32 [4096, 768], P('seq')
- grad_norm1_gain: float32 [768], replicated
- grad_norm1_bias: float32 [768], replicated
- grad_query_weight: float32 [768, 768], P(None, 'tp')
- grad_query_bias: float32 [768], P('tp')
- grad_key_weight: float32 [768, 768], P(None, 'tp')
- grad_key_bias: float32 [768], P('tp')
- grad_value_weight: float32 [768, 768], P(None, 'tp')
- grad_value_bias: float32 [768], P('tp')
- grad_shift_kernel: float32 [4, 768], P(None, 'tp')
- grad_log_step: float32 [768], P('tp')
- grad_state_rate: float32 [64, 768], P(None, 'tp')
- grad_state_out: float32 [64, 768], P(None, 'tp')
- grad_skip_gain: float32 [768], P('tp')
- grad_out_weight: float32 [768, 768], P('tp')
- grad_out_bias: float32 [768], replicated
- grad_norm2_gain: float32 [768], replicated
- grad_norm2_bias: float32 [768], replicated
- grad_up_weight: float32 [768, 3072], P(None, 'tp')
- grad_up_bias: float32 [3072], P('tp')
- grad_down_weight: float32 [3072, 768], P('tp')
- grad_down_bias: float32 [768], replicated
The draws below stay inside these ranges and needn't reach their ends.
Inputs may be any that keep to these rules, and one draw needn't show every extreme that they name: `log_step`: uniform between log(0.05 / 2048) and log(0.005).
All inputs are finite; a program needn't handle non-finite values.
Results may differ from the reference program's by a relative error of at most 0.0003.
Values sent between devices are 32-bit elements; how exact they have to be, the bound alone decides.
A program may use at most 256 MiB of HBM per device.

```python
import math
import jax
import jax.numpy as jnp
from jax import lax

D = 768
FF = 3072
STATE = 64
SHIFT = 4
SEQS = 2
TOKENS = 4096
LENGTH = 2048


def draw_log_step(key, part):
    key = jax.random.fold_in(key, 7)
    spread = jax.random.uniform(key, (D,), jnp.float32)
    low_end = jnp.log(0.05 / LENGTH)
    return low_end + spread * (jnp.log(0.005) - low_end)


def shard_levels(stream_key, dims, shards, smallest, largest):
    factor_of, own = 1.0, jax.random.fold_in(stream_key, 6)
    for axis_at, parts in shards:
        heights = jnp.exp(jax.random.uniform(jax.random.fold_in(own, axis_at), (parts,), jnp.float32, smallest / len(shards), largest / len(shards)))
        factor_of = factor_of * jnp.repeat(heights, dims[axis_at] // parts).reshape([-1 if axis == axis_at else 1 for axis in range(len(dims))])
    return factor_of


def bell_draw(stream_key, dims, scale, limit, pieces=(), held_as=jnp.bfloat16):
    drawn = scale * jax.random.normal(stream_key, dims, jnp.float32)
    if pieces:
        drawn = drawn * shard_levels(stream_key, dims, pieces, -0.22, 0.18)
    return jnp.clip(drawn, -limit, limit).astype(held_as)


def setup_inputs(seed: int = 0) -> dict:
    key_list = jax.random.split(jax.random.key(seed), 24)
    tokens = bell_draw(key_list[0], (TOKENS, D), 1.0, 6.0, ((0, 16),), jnp.float32)
    cotangent = bell_draw(key_list[1], (TOKENS, D), 1.0, 6.0, ((0, 16),), jnp.float32)
    norm1_gain = jnp.clip(1.0 + 0.1 * jax.random.normal(key_list[2], (D,), jnp.float32), 0.5, 1.5)
    norm1_bias = bell_draw(key_list[3], (D,), 0.3, 1.75, (), jnp.float32)
    query_weight = bell_draw(key_list[4], (D, D), D ** -0.5, 0.21875, ((1, 2),), jnp.float32)
    query_bias = bell_draw(key_list[5], (D,), 0.3, 1.75, ((0, 2),), jnp.float32)
    key_weight = bell_draw(key_list[6], (D, D), D ** -0.5, 0.21875, ((1, 2),), jnp.float32)
    key_bias = bell_draw(key_list[7], (D,), 0.3, 1.75, ((0, 2),), jnp.float32)
    value_weight = bell_draw(key_list[8], (D, D), D ** -0.5, 0.21875, ((1, 2),), jnp.float32)
    value_bias = bell_draw(key_list[9], (D,), 0.3, 1.75, ((0, 2),), jnp.float32)
    shift_kernel = bell_draw(key_list[10], (SHIFT, D), 0.5, 3.0, ((1, 2),), jnp.float32)
    log_step = draw_log_step(jax.random.fold_in(key_list[23], 71), 0)
    state_rate = jnp.clip(jnp.exp(math.log(64.0) - 4.158883 * jax.random.uniform(key_list[12], (STATE, D), jnp.float32) ** shard_levels(key_list[12], (STATE, D), ((1, 2),), -0.2, 0.2)), 1.0, 64.0)
    state_out = bell_draw(key_list[13], (STATE, D), STATE ** -0.5, 0.75, ((1, 2),), jnp.float32)
    skip_gain = bell_draw(key_list[14], (D,), 1.0, 4.0, ((0, 2),), jnp.float32)
    out_weight = bell_draw(key_list[15], (D, D), D ** -0.5, 0.21875, ((0, 2),), jnp.float32)
    out_bias = bell_draw(key_list[16], (D,), 0.3, 1.75, (), jnp.float32)
    norm2_gain = jnp.clip(1.0 + 0.1 * jax.random.normal(key_list[17], (D,), jnp.float32), 0.5, 1.5)
    norm2_bias = bell_draw(key_list[18], (D,), 0.3, 1.75, (), jnp.float32)
    up_weight = bell_draw(key_list[19], (D, FF), D ** -0.5, 0.21875, ((1, 2),), jnp.float32)
    up_bias = bell_draw(key_list[20], (FF,), 0.3, 1.75, ((0, 2),), jnp.float32)
    down_weight = bell_draw(key_list[21], (FF, D), FF ** -0.5, 0.109375, ((0, 2),), jnp.float32)
    down_bias = bell_draw(key_list[22], (D,), 0.3, 1.75, (), jnp.float32)
    return dict(tokens=tokens, cotangent=cotangent, norm1_gain=norm1_gain, norm1_bias=norm1_bias, query_weight=query_weight, query_bias=query_bias, key_weight=key_weight, key_bias=key_bias, value_weight=value_weight, value_bias=value_bias, shift_kernel=shift_kernel, log_step=log_step, state_rate=state_rate, state_out=state_out, skip_gain=skip_gain, out_weight=out_weight, out_bias=out_bias, norm2_gain=norm2_gain, norm2_bias=norm2_bias, up_weight=up_weight, up_bias=up_bias, down_weight=down_weight, down_bias=down_bias)


@jax.custom_vjp
def low(v):
    return lax.optimization_barrier(v.astype(jnp.bfloat16)).astype(jnp.float32)

@jax.custom_vjp
def low_back(v):
    return v

def low_keep(v):
    return (low(v), None)

def low_pass(kept, grad):
    return (grad,)

def back_keep(v):
    return (v, None)

def back_low(kept, grad):
    return (low(grad),)
low.defvjp(low_keep, low_pass)
low_back.defvjp(back_keep, back_low)
EPSILON = 1e-05
HIGHEST = lax.Precision.HIGHEST
block_rows = 32

def matmul(left, right):
    return jnp.dot(left, right, precision=HIGHEST, preferred_element_type=jnp.float32)

def layer_norm(values, gain, bias):
    centered = values - lax.optimization_barrier(jnp.mean(values, axis=-1, keepdims=True))
    spread = lax.optimization_barrier(jnp.mean(centered * centered, axis=-1, keepdims=True))
    return centered * lax.rsqrt(spread + EPSILON) * gain + bias

def stretch_states(inputs, in_coef, decay_rate, carry_state, lower_ones):
    length = inputs.shape[0]
    places = jnp.arange(length).astype(jnp.float32)[:, None, None]
    growth = jnp.exp(decay_rate[None] * places)
    scaled = growth * (in_coef[None] * inputs[:, None, :])
    summed = matmul(lower_ones, scaled.reshape(length, -1)).reshape(scaled.shape)
    return summed / growth + jnp.exp(-decay_rate[None] * (places + 1.0)) * carry_state[None]

def shift_mix(key_rows, shift_kernel):
    grouped = key_rows.reshape(SEQS, LENGTH, D)
    padded = jnp.pad(grouped, ((0, 0), (SHIFT - 1, 0), (0, 0)))
    total_rows = jnp.zeros_like(grouped)
    for offset in range(SHIFT):
        total_rows = total_rows + shift_kernel[offset] * padded[:, SHIFT - 1 - offset:SHIFT - 1 - offset + LENGTH]
    return total_rows.reshape(TOKENS, D)

def diagonal_ssm(mixed, log_step, state_rate, state_out, skip_gain):
    decay_rate = jnp.exp(log_step)[None, :] * state_rate
    in_coef = jnp.sqrt(-jnp.expm1(-2.0 * decay_rate))
    lower_ones = jnp.tril(jnp.ones((block_rows, block_rows), jnp.float32))
    blocks = mixed.reshape(SEQS, LENGTH // block_rows, block_rows, D).transpose(1, 0, 2, 3)

    def one_sequence(token_block, state_carry):
        return stretch_states(token_block, in_coef, decay_rate, state_carry, lower_ones)

    def advance(state_carry, token_block):
        states = jax.vmap(one_sequence)(token_block, state_carry)
        return (states[:, -1], lax.optimization_barrier(jnp.sum(states * state_out[None, None], axis=2)))
    _, outputs = lax.scan(jax.checkpoint(advance), jnp.zeros((SEQS, STATE, D), jnp.float32), blocks)
    return outputs.transpose(1, 0, 2, 3).reshape(TOKENS, D) + skip_gain * mixed

def forward(tokens, norm1_gain, norm1_bias, query_weight, query_bias, key_weight, key_bias, value_weight, value_bias, shift_kernel, log_step, state_rate, state_out, skip_gain, out_weight, out_bias, norm2_gain, norm2_bias, up_weight, up_bias, down_weight, down_bias):
    normed = layer_norm(tokens, norm1_gain, norm1_bias)
    queries = matmul(normed, query_weight) + query_bias
    key_rows = matmul(normed, key_weight) + key_bias
    value_rows = matmul(normed, value_weight) + value_bias
    mixed = shift_mix(key_rows, shift_kernel) * value_rows
    ssm_out = diagonal_ssm(mixed, log_step, state_rate, state_out, skip_gain)
    middle = tokens + matmul(queries * ssm_out, out_weight) + out_bias
    normed2 = layer_norm(middle, norm2_gain, norm2_bias)
    activated = jax.nn.gelu(matmul(normed2, up_weight) + up_bias)
    return middle + matmul(activated, down_weight) + down_bias

def reference(tokens, cotangent, norm1_gain, norm1_bias, query_weight, query_bias, key_weight, key_bias, value_weight, value_bias, shift_kernel, log_step, state_rate, state_out, skip_gain, out_weight, out_bias, norm2_gain, norm2_bias, up_weight, up_bias, down_weight, down_bias):
    block_out, pullback = jax.vjp(forward, tokens, norm1_gain, norm1_bias, query_weight, query_bias, key_weight, key_bias, value_weight, value_bias, shift_kernel, log_step, state_rate, state_out, skip_gain, out_weight, out_bias, norm2_gain, norm2_bias, up_weight, up_bias, down_weight, down_bias)
    grads = pullback(cotangent)
    return (block_out, grads[0], grads[1], grads[2], grads[3], grads[4], grads[5], grads[6], grads[7], grads[8], grads[9], grads[10], grads[11], grads[12], grads[13], grads[14], grads[15], grads[16], grads[17], grads[18], grads[19], grads[20], grads[21])
```

```python
import functools

import jax
import jax.numpy as jnp
from jax import lax
from jax.experimental import pallas as pl
from jax.experimental.pallas import tpu as pltpu
from jax.sharding import PartitionSpec as P

SHIFT = 4
SEQS = 2
STATE = 64
LANES = 128
CHUNK = 32

EPSILON = 1e-05
F32 = jnp.float32
PRECISION = lax.Precision.HIGH


def shape(*dims):
    return jax.ShapeDtypeStruct(dims, F32)


def fold_states(values):
    return jnp.sum(values.reshape(STATE // 8, 8, LANES), axis=0)


def scan_kernel(mixed_ref, decay_ref, out_coef_ref, out_ref, end_ref, starts_ref, part_ref):
    decay, out_coef = decay_ref[...], out_coef_ref[...]

    def chunk(k, state):
        starts_ref[k] = state
        base = pl.multiple_of(k * CHUNK, CHUNK)
        for j in range(CHUNK):
            state = decay * state + mixed_ref[pl.ds(base + j, 1), :]
            part_ref[j] = fold_states(out_coef * state)
        out_ref[pl.ds(base, CHUNK), :] = jnp.sum(part_ref[...], axis=1)
        return state

    end_ref[...] = lax.fori_loop(0, mixed_ref.shape[0] // CHUNK, chunk, jnp.zeros_like(decay))


def carry_kernel(incoming_ref, decay_ref, out_coef_ref, local_ref, local_starts_ref, out_ref, starts_ref, part_ref):
    decay, out_coef = decay_ref[...], out_coef_ref[...]

    def chunk(k, state):
        starts_ref[k] = local_starts_ref[k] + state
        base = pl.multiple_of(k * CHUNK, CHUNK)
        for j in range(CHUNK):
            state = decay * state
            part_ref[j] = fold_states(out_coef * state)
        rows = pl.ds(base, CHUNK)
        out_ref[rows, :] = local_ref[rows, :] + jnp.sum(part_ref[...], axis=1)
        return state

    lax.fori_loop(0, local_ref.shape[0] // CHUNK, chunk, incoming_ref[...])


def adjoint_end_kernel(grad_ref, decay_ref, end_ref):
    decay = decay_ref[...]
    count = grad_ref.shape[0] // CHUNK

    def chunk(i, adjoint):
        base = pl.multiple_of((count - 1 - i) * CHUNK, CHUNK)
        for j in range(CHUNK - 1, -1, -1):
            adjoint = decay * adjoint + grad_ref[pl.ds(base + j, 1), :]
        return adjoint

    end_ref[...] = lax.fori_loop(0, count, chunk, jnp.zeros_like(decay))


def adjoint_kernel(
    grad_ref, mixed_ref, decay_ref, out_coef_ref, incoming_ref, starts_ref, out_ref, coef_ref, slope_ref, part_ref, state_ref
):
    decay = decay_ref[...]
    count = grad_ref.shape[0] // CHUNK
    coef_ref[...] = jnp.zeros_like(decay)
    slope_ref[...] = jnp.zeros_like(decay)

    def chunk(i, adjoint):
        k = count - 1 - i
        base = pl.multiple_of(k * CHUNK, CHUNK)
        state = starts_ref[k]
        for j in range(CHUNK):
            state_ref[j] = state
            state = decay * state + mixed_ref[pl.ds(base + j, 1), :]
        out_coef = out_coef_ref[...]
        coef, slope = coef_ref[...], slope_ref[...]
        for j in range(CHUNK - 1, -1, -1):
            adjoint = decay * adjoint + grad_ref[pl.ds(base + j, 1), :]
            part_ref[j] = fold_states(out_coef * adjoint)
            coef = coef + adjoint * mixed_ref[pl.ds(base + j, 1), :]
            slope = slope + adjoint * state_ref[j]
        coef_ref[...] = coef
        slope_ref[...] = slope
        out_ref[pl.ds(base, CHUNK), :] = jnp.sum(part_ref[...], axis=1)
        return adjoint

    lax.fori_loop(0, count, chunk, incoming_ref[...])


def state_call(kernel, args, outs, scratch, name):
    def spec(dims):
        lead = len(dims) - 1
        return pl.BlockSpec(tuple(dims[:-1]) + (LANES,), lambda i: (0,) * lead + (i,))

    return pl.pallas_call(
        kernel,
        grid=(args[0].shape[-1] // LANES,),
        in_specs=[spec(a.shape) for a in args],
        out_specs=[spec(o.shape) for o in outs],
        out_shape=outs,
        scratch_shapes=[pltpu.VMEM(dims, F32) for dims in scratch],
        compiler_params=pltpu.CompilerParams(vmem_limit_bytes=32 * 2**20),
        name=name,
    )(*args)


def within_sequence(value, shift, span):
    count = lax.axis_size("seq")
    pairs = [(i, i + shift) for i in range(count) if 0 <= i % span + shift < span]
    return lax.ppermute(value, "seq", pairs)


def carried(ends, device_decay, span, direction):
    total = None
    arrived = [within_sequence(ends, direction * k, span) for k in range(1, span)]
    for value in reversed(arrived):
        total = value if total is None else total * device_decay + value
    return jnp.zeros_like(ends) if total is None else total


def over_cores(value):
    count = lax.axis_size("tp")
    total = value
    for shift in range(1, count):
        total = total + lax.ppermute(value, "tp", [(i, (i + shift) % count) for i in range(count)])
    return total


def matmul(left, right):
    return jnp.dot(left, right, precision=PRECISION, preferred_element_type=F32)


def matmul_tn(left, right):
    return lax.dot_general(left, right, (((0,), (0,)), ((), ())), precision=PRECISION, preferred_element_type=F32)


def matmul_nt(left, right):
    return lax.dot_general(left, right, (((1,), (1,)), ((), ())), precision=PRECISION, preferred_element_type=F32)


def layer_norm(values, gain, bias):
    centered = values - jnp.mean(values, axis=-1, keepdims=True)
    spread = jnp.mean(centered * centered, axis=-1, keepdims=True)
    return centered * lax.rsqrt(spread + EPSILON) * gain + bias


def decay_terms(log_step, state_rate):
    decay_rate = jnp.exp(log_step)[None, :] * state_rate
    return (jnp.exp(-decay_rate), jnp.sqrt(-jnp.expm1(-2.0 * decay_rate)))


def on_device(
    tokens,
    cotangent,
    norm1_gain,
    norm1_bias,
    query_weight,
    query_bias,
    key_weight,
    key_bias,
    value_weight,
    value_bias,
    shift_kernel,
    log_step,
    state_rate,
    state_out,
    skip_gain,
    out_weight,
    out_bias,
    norm2_gain,
    norm2_bias,
    up_weight,
    up_bias,
    down_weight,
    down_bias,
):
    tok_rows = tokens.shape[0]
    width_local = query_weight.shape[1]
    span = lax.axis_size("seq") // SEQS
    chunks = tok_rows // CHUNK
    normed, norm1_pull = jax.vjp(layer_norm, tokens, norm1_gain, norm1_bias)
    queries = matmul(normed, query_weight) + query_bias
    key_rows = matmul(normed, key_weight) + key_bias
    value_rows = matmul(normed, value_weight) + value_bias
    tail_rows = within_sequence(key_rows[tok_rows - (SHIFT - 1) :], 1, span)
    extended = jnp.concatenate([tail_rows, key_rows], axis=0)
    behind = [extended[SHIFT - 1 - j : SHIFT - 1 - j + tok_rows] for j in range(SHIFT)]
    shifted = sum(shift_kernel[j] * behind[j] for j in range(SHIFT))
    mixed = shifted * value_rows
    decay_rate = jnp.exp(log_step)[None, :] * state_rate
    (decay_factor, in_coef), decay_pull = jax.vjp(decay_terms, log_step, state_rate)
    device_decay = jnp.exp(-decay_rate * tok_rows)
    out_coef = in_coef * state_out
    tok_shape, state_shape = shape(tok_rows, width_local), shape(STATE, width_local)
    starts_shape = shape(chunks, STATE, width_local)
    part_scratch = (CHUNK, 8, LANES)
    local_out, local_end, local_starts = state_call(
        scan_kernel,
        (mixed, decay_factor, out_coef),
        [tok_shape, state_shape, starts_shape],
        [part_scratch],
        "ssm_scan",
    )
    incoming = carried(local_end, device_decay, span, 1)
    scanned, starts = state_call(
        carry_kernel,
        (incoming, decay_factor, out_coef, local_out, local_starts),
        [tok_shape, starts_shape],
        [part_scratch],
        "ssm_carry",
    )
    ssm_out = scanned + skip_gain * mixed
    gated = queries * ssm_out
    middle = tokens + over_cores(matmul(gated, out_weight)) + out_bias
    normed2, norm2_pull = jax.vjp(layer_norm, middle, norm2_gain, norm2_bias)
    activated, gelu_pull = jax.vjp(jax.nn.gelu, matmul(normed2, up_weight) + up_bias)
    (grad_pre,) = gelu_pull(matmul_nt(cotangent, down_weight))
    grad_normed2 = over_cores(matmul_nt(grad_pre, up_weight))
    block_out = middle + over_cores(matmul(activated, down_weight)) + down_bias
    grad_down_weight = matmul_tn(activated, cotangent)
    grad_down_bias = jnp.sum(cotangent, axis=0)
    grad_up_weight = matmul_tn(normed2, grad_pre)
    grad_up_bias = jnp.sum(grad_pre, axis=0)
    grad_mid_norm, grad_norm2_gain, grad_norm2_bias = norm2_pull(grad_normed2)
    grad_middle = cotangent + grad_mid_norm
    grad_out_bias = jnp.sum(grad_middle, axis=0)
    grad_gated = matmul_nt(grad_middle, out_weight)
    grad_queries = grad_gated * ssm_out
    grad_ssm = grad_gated * queries
    grad_skip_gain = jnp.sum(grad_ssm * mixed, axis=0)
    (local_first,) = state_call(
        adjoint_end_kernel, (grad_ssm, decay_factor), [state_shape], [], "ssm_adjoint_end"
    )
    incoming_adjoint = carried(local_first, device_decay, span, -1)
    scanned_grad, coef_sum, slope_sum = state_call(
        adjoint_kernel,
        (grad_ssm, mixed, decay_factor, out_coef, incoming_adjoint, starts),
        [tok_shape, state_shape, state_shape],
        [part_scratch, (CHUNK, STATE, LANES)],
        "ssm_adjoint",
    )
    grad_mixed = scanned_grad + skip_gain * grad_ssm
    grad_state_out = in_coef * coef_sum
    grad_log_step, grad_state_rate = decay_pull((out_coef * slope_sum, state_out * coef_sum))
    grad_shifted = grad_mixed * value_rows
    grad_values = grad_mixed * shifted
    head_rows = within_sequence(grad_shifted[: SHIFT - 1], -1, span)
    grad_extended = jnp.concatenate([grad_shifted, head_rows], axis=0)
    grad_keys = sum(shift_kernel[j] * grad_extended[j : j + tok_rows] for j in range(SHIFT))
    grad_shift_kernel = jnp.stack([jnp.sum(grad_shifted * behind[j], axis=0) for j in range(SHIFT)])
    grad_out_weight = matmul_tn(gated, grad_middle)
    grad_query_weight = matmul_tn(normed, grad_queries)
    grad_key_weight = matmul_tn(normed, grad_keys)
    grad_value_weight = matmul_tn(normed, grad_values)
    grad_query_bias = jnp.sum(grad_queries, axis=0)
    grad_key_bias = jnp.sum(grad_keys, axis=0)
    grad_value_bias = jnp.sum(grad_values, axis=0)
    local_normed = (
        matmul_nt(grad_queries, query_weight)
        + matmul_nt(grad_keys, key_weight)
        + matmul_nt(grad_values, value_weight)
    )
    grad_normed = over_cores(local_normed)
    grad_in_norm, grad_norm1_gain, grad_norm1_bias = norm1_pull(grad_normed)
    input_grad = grad_middle + grad_in_norm
    (
        grad_norm1_gain,
        grad_norm1_bias,
        grad_query_weight,
        grad_query_bias,
        grad_key_weight,
        grad_key_bias,
        grad_value_weight,
        grad_value_bias,
        grad_shift_kernel,
        grad_log_step,
        grad_state_rate,
        grad_state_out,
        grad_skip_gain,
        grad_out_weight,
        grad_out_bias,
        grad_norm2_gain,
        grad_norm2_bias,
        grad_up_weight,
        grad_up_bias,
        grad_down_weight,
        grad_down_bias,
    ) = lax.psum(
        (
            grad_norm1_gain,
            grad_norm1_bias,
            grad_query_weight,
            grad_query_bias,
            grad_key_weight,
            grad_key_bias,
            grad_value_weight,
            grad_value_bias,
            grad_shift_kernel,
            grad_log_step,
            grad_state_rate,
            grad_state_out,
            grad_skip_gain,
            grad_out_weight,
            grad_out_bias,
            grad_norm2_gain,
            grad_norm2_bias,
            grad_up_weight,
            grad_up_bias,
            grad_down_weight,
            grad_down_bias,
        ),
        "seq",
    )
    return (
        block_out,
        input_grad,
        grad_norm1_gain,
        grad_norm1_bias,
        grad_query_weight,
        grad_query_bias,
        grad_key_weight,
        grad_key_bias,
        grad_value_weight,
        grad_value_bias,
        grad_shift_kernel,
        grad_log_step,
        grad_state_rate,
        grad_state_out,
        grad_skip_gain,
        grad_out_weight,
        grad_out_bias,
        grad_norm2_gain,
        grad_norm2_bias,
        grad_up_weight,
        grad_up_bias,
        grad_down_weight,
        grad_down_bias,
    )


def solution(mesh):
    return jax.shard_map(
        on_device,
        mesh=mesh,
        in_specs=(
            P("seq", None),
            P("seq", None),
            P(),
            P(),
            P(None, "tp"),
            P("tp"),
            P(None, "tp"),
            P("tp"),
            P(None, "tp"),
            P("tp"),
            P(None, "tp"),
            P("tp"),
            P(None, "tp"),
            P(None, "tp"),
            P("tp"),
            P("tp", None),
            P(),
            P(),
            P(),
            P(None, "tp"),
            P("tp"),
            P("tp", None),
            P(),
        ),
        out_specs=(
            P("seq", None),
            P("seq", None),
            P(),
            P(),
            P(None, "tp"),
            P("tp"),
            P(None, "tp"),
            P("tp"),
            P(None, "tp"),
            P("tp"),
            P(None, "tp"),
            P("tp"),
            P(None, "tp"),
            P(None, "tp"),
            P("tp"),
            P("tp", None),
            P(),
            P(),
            P(),
            P(None, "tp"),
            P("tp"),
            P("tp", None),
            P(),
        ),
        check_vma=False,
    )
```

```python
import functools

import jax
import jax.numpy as jnp
from jax import lax
from jax.experimental import pallas as pl
from jax.experimental.pallas import tpu as pltpu
from jax.sharding import PartitionSpec as P

SHIFT = 4
SEQS = 2
STATE = 64
LANES = 128
CHUNK = 32
PIECE_ROWS = 24
LAG = 2

EPSILON = 1e-05
F32 = jnp.float32
PRECISION = lax.Precision.HIGH


def shape(*dims):
    return jax.ShapeDtypeStruct(dims, F32)


def fold_states(values):
    return jnp.sum(values.reshape(STATE // 8, 8, LANES), axis=0)


def scan_kernel(mixed_ref, decay_ref, out_coef_ref, out_ref, end_ref, starts_ref, part_ref):
    decay, out_coef = decay_ref[...], out_coef_ref[...]

    def chunk(k, state):
        starts_ref[k] = state
        base = pl.multiple_of(k * CHUNK, CHUNK)
        for j in range(CHUNK):
            state = decay * state + mixed_ref[pl.ds(base + j, 1), :]
            part_ref[j] = fold_states(out_coef * state)
        out_ref[pl.ds(base, CHUNK), :] = jnp.sum(part_ref[...], axis=1)
        return state

    end_ref[...] = lax.fori_loop(0, mixed_ref.shape[0] // CHUNK, chunk, jnp.zeros_like(decay))


def carry_kernel(incoming_ref, decay_ref, out_coef_ref, local_ref, local_starts_ref, out_ref, starts_ref, part_ref):
    decay, out_coef = decay_ref[...], out_coef_ref[...]

    def chunk(k, state):
        starts_ref[k] = local_starts_ref[k] + state
        base = pl.multiple_of(k * CHUNK, CHUNK)
        for j in range(CHUNK):
            state = decay * state
            part_ref[j] = fold_states(out_coef * state)
        rows = pl.ds(base, CHUNK)
        out_ref[rows, :] = local_ref[rows, :] + jnp.sum(part_ref[...], axis=1)
        return state

    lax.fori_loop(0, local_ref.shape[0] // CHUNK, chunk, incoming_ref[...])


def adjoint_end_kernel(grad_ref, decay_ref, end_ref):
    decay = decay_ref[...]
    count = grad_ref.shape[0] // CHUNK

    def chunk(i, adjoint):
        base = pl.multiple_of((count - 1 - i) * CHUNK, CHUNK)
        for j in range(CHUNK - 1, -1, -1):
            adjoint = decay * adjoint + grad_ref[pl.ds(base + j, 1), :]
        return adjoint

    end_ref[...] = lax.fori_loop(0, count, chunk, jnp.zeros_like(decay))


def adjoint_kernel(
    grad_ref, mixed_ref, decay_ref, out_coef_ref, incoming_ref, starts_ref, out_ref, coef_ref, slope_ref, part_ref, state_ref
):
    decay = decay_ref[...]
    count = grad_ref.shape[0] // CHUNK
    coef_ref[...] = jnp.zeros_like(decay)
    slope_ref[...] = jnp.zeros_like(decay)

    def chunk(i, adjoint):
        k = count - 1 - i
        base = pl.multiple_of(k * CHUNK, CHUNK)
        state = starts_ref[k]
        for j in range(CHUNK):
            state_ref[j] = state
            state = decay * state + mixed_ref[pl.ds(base + j, 1), :]
        out_coef = out_coef_ref[...]
        coef, slope = coef_ref[...], slope_ref[...]
        for j in range(CHUNK - 1, -1, -1):
            adjoint = decay * adjoint + grad_ref[pl.ds(base + j, 1), :]
            part_ref[j] = fold_states(out_coef * adjoint)
            coef = coef + adjoint * mixed_ref[pl.ds(base + j, 1), :]
            slope = slope + adjoint * state_ref[j]
        coef_ref[...] = coef
        slope_ref[...] = slope
        out_ref[pl.ds(base, CHUNK), :] = jnp.sum(part_ref[...], axis=1)
        return adjoint

    lax.fori_loop(0, count, chunk, incoming_ref[...])


def state_call(kernel, args, outs, scratch, name):
    def spec(dims):
        lead = len(dims) - 1
        return pl.BlockSpec(tuple(dims[:-1]) + (LANES,), lambda i: (0,) * lead + (i,))

    return pl.pallas_call(
        kernel,
        grid=(args[0].shape[-1] // LANES,),
        in_specs=[spec(a.shape) for a in args],
        out_specs=[spec(o.shape) for o in outs],
        out_shape=outs,
        scratch_shapes=[pltpu.VMEM(dims, F32) for dims in scratch],
        compiler_params=pltpu.CompilerParams(vmem_limit_bytes=32 * 2**20),
        name=name,
    )(*args)


def within_sequence(value, shift, span):
    count = lax.axis_size("seq")
    pairs = [(i, i + shift) for i in range(count) if 0 <= i % span + shift < span]
    return lax.ppermute(value, "seq", pairs)


def carried(ends, device_decay, span, direction):
    total = None
    arrived = [within_sequence(ends, direction * k, span) for k in range(1, span)]
    for value in reversed(arrived):
        total = value if total is None else total * device_decay + value
    return jnp.zeros_like(ends) if total is None else total


def over_cores(value):
    count = lax.axis_size("tp")
    total = value
    for shift in range(1, count):
        total = total + lax.ppermute(value, "tp", [(i, (i + shift) % count) for i in range(count)])
    return total


MESH = pl.DeviceIdType.MESH


def is_far(i):
    return lax.rem(i, 4) == 2


def sum_kernel(
    length, pieces, rows, lag, own_ref, out_ref, sum_ref, got_ref, load_sem, store_sem, chain_send, chain_recv,
    z_send, z_recv, side_send, side_recv
):
    me = lax.axis_index("seq")
    place, quarter = me // 4, lax.rem(me, 4)
    x, y = lax.rem(quarter, 2), quarter // 2
    x_peer, y_peer = me + 1 - 2 * x, me + 2 - 4 * y
    quarter_x, quarter_y, quarter_d = quarter + 1 - 2 * x, quarter + 2 - 4 * y, 3 - quarter
    first = lag * (length - 1)
    started = (place, length - 1 - place)
    ahead = (me + 4, me - 4)
    behind = (me - 4, me + 4)

    loads = [pltpu.make_async_copy(own_ref.at[d], sum_ref.at[d], load_sem.at[d]) for d in range(2)]
    for load in loads:
        load.start()
    barrier = pltpu.get_barrier_semaphore()

    def greet(peer):
        pl.semaphore_signal(barrier, inc=1, device_id={"seq": peer}, device_id_type=MESH)

    greet(x_peer)
    greet(y_peer)
    pl.when(place > 0)(lambda: greet(me - 4))
    pl.when(place < length - 1)(lambda: greet(me + 4))
    pl.semaphore_wait(barrier, 2 + (place > 0).astype(jnp.int32) + (place < length - 1).astype(jnp.int32))
    for load in loads:
        load.wait()

    def remote(source, target, send, recv, peer):
        return pltpu.make_async_remote_copy(
            src_ref=source,
            dst_ref=target,
            send_sem=send,
            recv_sem=recv,
            device_id={"seq": peer},
            device_id_type=MESH,
        )

    def at(i):
        return pl.ds(pl.multiple_of(i * rows, 8), rows)

    def chain_copy(d, i):
        return remote(
            sum_ref.at[d, at(i)], got_ref.at[d, at(i)], chain_send.at[d, i], chain_recv.at[d, i], ahead[d]
        )

    def z_copy(d, i, k):
        ref = out_ref.at[(quarter, quarter_x, quarter_y, quarter_d)[k], d, at(i)]
        return remote(ref, ref, z_send.at[d, i, k], z_recv.at[d, i, k], behind[d])

    def side_copy(d, i, k):
        even = lax.rem(i, 2) == 0
        source = (quarter, quarter, jnp.where(even, quarter_x, quarter_y))[k]
        peer = (x_peer, y_peer, jnp.where(even, y_peer, x_peer))[k]
        ref = out_ref.at[source, d, at(i)]
        return remote(ref, ref, side_send.at[d, i, k], side_recv.at[d, i, k], peer)

    def chain_step(d, i):
        @pl.when(started[d] > 0)
        def _():
            chain_copy(d, i).wait_recv()
            sum_ref[d, at(i)] = sum_ref[d, at(i)] + got_ref[d, at(i)]

        @pl.when(started[d] < length - 1)
        def _():
            chain_copy(d, i).start()

        @pl.when(started[d] == length - 1)
        def _():
            store = pltpu.make_async_copy(sum_ref.at[d, at(i)], out_ref.at[quarter, d, at(i)], store_sem.at[d, i])
            store.start()
            store.wait()

    def kind(d, i):
        remaining = length - 1 - started[d]
        far = is_far(i)
        sideways = jnp.logical_or(jnp.logical_not(far), remaining == 0)
        onward = jnp.logical_and(far, remaining < length - 1)
        return remaining, sideways, onward

    def own_step(d, i):
        remaining, sideways, _ = kind(d, i)

        @pl.when(remaining > 0)
        def _():
            z_copy(d, i, 0).wait_recv()

        @pl.when(remaining < length - 1)
        def _():
            z_copy(d, i, 0).start()

        @pl.when(sideways)
        def _():
            side_copy(d, i, 0).start()
            side_copy(d, i, 1).start()

    def side_step(d, i):
        _, sideways, onward = kind(d, i)

        @pl.when(sideways)
        def _():
            side_copy(d, i, 0).wait_recv()
            side_copy(d, i, 1).wait_recv()
            side_copy(d, i, 2).start()

        @pl.when(jnp.logical_not(sideways))
        def _():
            z_copy(d, i, 1).wait_recv()
            z_copy(d, i, 2).wait_recv()

        @pl.when(onward)
        def _():
            z_copy(d, i, 1).start()
            z_copy(d, i, 2).start()

    def last_step(d, i):
        _, sideways, onward = kind(d, i)

        @pl.when(sideways)
        def _():
            side_copy(d, i, 2).wait_recv()

        @pl.when(jnp.logical_not(sideways))
        def _():
            z_copy(d, i, 3).wait_recv()

        @pl.when(onward)
        def _():
            z_copy(d, i, 3).start()

    def tick(t, _):
        for step, late in ((last_step, first + 2 * lag), (side_step, first + lag), (chain_step, 0), (own_step, first)):
            for d in range(2):
                passed = started[d] if step is chain_step else length - 1 - started[d]
                i = t - late - lag * passed
                pl.when(jnp.logical_and(i >= 0, i < pieces))(functools.partial(step, d, i))
        return 0

    lax.fori_loop(0, 2 * first + 2 * lag + pieces, tick, 0)

    def drain(i, _):
        for d in range(2):
            remaining, sideways, onward = kind(d, i)
            pl.when(remaining > 0)(lambda: chain_copy(d, i).wait_send())
            pl.when(remaining < length - 1)(lambda: z_copy(d, i, 0).wait_send())

            @pl.when(onward)
            def _():
                for k in range(1, 4):
                    z_copy(d, i, k).wait_send()

            @pl.when(sideways)
            def _():
                for k in range(3):
                    side_copy(d, i, k).wait_send()

        return 0

    lax.fori_loop(0, pieces, drain, 0)


def summed_quarters(own, pieces, lag):
    _, total, columns = own.shape
    length = lax.axis_size("seq") // 4
    sems = [(2,), (2, pieces), (2, pieces), (2, pieces), (2, pieces, 4), (2, pieces, 4), (2, pieces, 3), (2, pieces, 3)]
    return pl.pallas_call(
        functools.partial(sum_kernel, length, pieces, total // pieces, lag),
        out_shape=shape(4, 2, total, columns),
        in_specs=[pl.BlockSpec(memory_space=pl.ANY)],
        out_specs=pl.BlockSpec(memory_space=pltpu.HBM),
        scratch_shapes=[pltpu.VMEM((2, total, columns), F32)] * 2 + [pltpu.SemaphoreType.DMA(dims) for dims in sems],
        compiler_params=pltpu.CompilerParams(collective_id=0, has_side_effects=True, vmem_limit_bytes=32 * 2**20),
        cost_estimate=pl.CostEstimate(flops=total * columns * 2, bytes_accessed=total * columns * 64, transcendentals=0),
        name="gradient_sums",
    )(own)


def swapped(value, bit):
    return lax.ppermute(value, "seq", [(i, i ^ bit) for i in range(lax.axis_size("seq"))])


def half(value, axis, which):
    size = value.shape[axis] // 2
    return lax.dynamic_slice_in_dim(value, which * size, size, axis)


def halved_sum(value, bit, mine):
    return half(value, 0, mine) + swapped(half(value, 0, 1 - mine), bit)


def matmul(left, right):
    return jnp.dot(left, right, precision=PRECISION, preferred_element_type=F32)


def matmul_tn(left, right):
    return lax.dot_general(left, right, (((0,), (0,)), ((), ())), precision=PRECISION, preferred_element_type=F32)


def matmul_nt(left, right):
    return lax.dot_general(left, right, (((1,), (1,)), ((), ())), precision=PRECISION, preferred_element_type=F32)


def layer_norm(values, gain, bias):
    centered = values - jnp.mean(values, axis=-1, keepdims=True)
    spread = jnp.mean(centered * centered, axis=-1, keepdims=True)
    return centered * lax.rsqrt(spread + EPSILON) * gain + bias


def decay_terms(log_step, state_rate):
    decay_rate = jnp.exp(log_step)[None, :] * state_rate
    return (jnp.exp(-decay_rate), jnp.sqrt(-jnp.expm1(-2.0 * decay_rate)))


def on_device(
    tokens,
    cotangent,
    norm1_gain,
    norm1_bias,
    query_weight,
    query_bias,
    key_weight,
    key_bias,
    value_weight,
    value_bias,
    shift_kernel,
    log_step,
    state_rate,
    state_out,
    skip_gain,
    out_weight,
    out_bias,
    norm2_gain,
    norm2_bias,
    up_weight,
    up_bias,
    down_weight,
    down_bias,
):
    tok_rows = tokens.shape[0]
    width_local = query_weight.shape[1]
    span = lax.axis_size("seq") // SEQS
    chunks = tok_rows // CHUNK
    x, y = lax.axis_index("seq") % 2, lax.axis_index("seq") // 2 % 2
    normed, norm1_pull = jax.vjp(layer_norm, tokens, norm1_gain, norm1_bias)
    queries = matmul(normed, query_weight) + query_bias
    key_rows = matmul(normed, key_weight) + key_bias
    value_rows = matmul(normed, value_weight) + value_bias
    tail_rows = within_sequence(key_rows[tok_rows - (SHIFT - 1) :], 1, span)
    extended = jnp.concatenate([tail_rows, key_rows], axis=0)
    behind = [extended[SHIFT - 1 - j : SHIFT - 1 - j + tok_rows] for j in range(SHIFT)]
    shifted = sum(shift_kernel[j] * behind[j] for j in range(SHIFT))
    mixed = shifted * value_rows
    decay_rate = jnp.exp(log_step)[None, :] * state_rate
    (decay_factor, in_coef), decay_pull = jax.vjp(decay_terms, log_step, state_rate)
    device_decay = jnp.exp(-decay_rate * tok_rows)
    out_coef = in_coef * state_out
    tok_shape, state_shape = shape(tok_rows, width_local), shape(STATE, width_local)
    starts_shape = shape(chunks, STATE, width_local)
    part_scratch = (CHUNK, 8, LANES)
    local_out, local_end, local_starts = state_call(
        scan_kernel,
        (mixed, decay_factor, out_coef),
        [tok_shape, state_shape, starts_shape],
        [part_scratch],
        "ssm_scan",
    )
    incoming = carried(local_end, device_decay, span, 1)
    scanned, starts = state_call(
        carry_kernel,
        (incoming, decay_factor, out_coef, local_out, local_starts),
        [tok_shape, starts_shape],
        [part_scratch],
        "ssm_carry",
    )
    ssm_out = scanned + skip_gain * mixed
    gated = queries * ssm_out
    middle = tokens + over_cores(matmul(gated, out_weight)) + out_bias
    normed2, norm2_pull = jax.vjp(layer_norm, middle, norm2_gain, norm2_bias)
    activated, gelu_pull = jax.vjp(jax.nn.gelu, matmul(normed2, up_weight) + up_bias)
    (grad_pre,) = gelu_pull(matmul_nt(cotangent, down_weight))
    grad_normed2 = over_cores(matmul_nt(grad_pre, up_weight))
    block_out = middle + over_cores(matmul(activated, down_weight)) + down_bias
    grad_down_bias = jnp.sum(cotangent, axis=0)
    grad_up_bias = jnp.sum(grad_pre, axis=0)
    down_half = matmul_tn(half(activated, 1, x), cotangent) + matmul_tn(
        swapped(half(activated, 1, 1 - x), 1), swapped(cotangent, 1)
    )
    up_half = matmul_tn(normed2, half(grad_pre, 1, y)) + matmul_tn(
        swapped(normed2, 2), swapped(half(grad_pre, 1, 1 - y), 2)
    )
    down_quarter = halved_sum(down_half, 2, y)
    up_quarter = halved_sum(up_half, 1, x)
    grad_mid_norm, grad_norm2_gain, grad_norm2_bias = norm2_pull(grad_normed2)
    grad_middle = cotangent + grad_mid_norm
    grad_out_bias = jnp.sum(grad_middle, axis=0)
    grad_gated = matmul_nt(grad_middle, out_weight)
    grad_queries = grad_gated * ssm_out
    grad_ssm = grad_gated * queries
    grad_skip_gain = jnp.sum(grad_ssm * mixed, axis=0)
    (local_first,) = state_call(
        adjoint_end_kernel, (grad_ssm, decay_factor), [state_shape], [], "ssm_adjoint_end"
    )
    incoming_adjoint = carried(local_first, device_decay, span, -1)
    scanned_grad, coef_sum, slope_sum = state_call(
        adjoint_kernel,
        (grad_ssm, mixed, decay_factor, out_coef, incoming_adjoint, starts),
        [tok_shape, state_shape, state_shape],
        [part_scratch, (CHUNK, STATE, LANES)],
        "ssm_adjoint",
    )
    grad_mixed = scanned_grad + skip_gain * grad_ssm
    grad_state_out = in_coef * coef_sum
    grad_log_step, grad_state_rate = decay_pull((out_coef * slope_sum, state_out * coef_sum))
    grad_shifted = grad_mixed * value_rows
    grad_values = grad_mixed * shifted
    head_rows = within_sequence(grad_shifted[: SHIFT - 1], -1, span)
    grad_extended = jnp.concatenate([grad_shifted, head_rows], axis=0)
    grad_keys = sum(shift_kernel[j] * grad_extended[j : j + tok_rows] for j in range(SHIFT))
    grad_shift_kernel = jnp.stack([jnp.sum(grad_shifted * behind[j], axis=0) for j in range(SHIFT)])
    grad_query_bias = jnp.sum(grad_queries, axis=0)
    grad_key_bias = jnp.sum(grad_keys, axis=0)
    grad_value_bias = jnp.sum(grad_values, axis=0)
    local_normed = (
        matmul_nt(grad_queries, query_weight)
        + matmul_nt(grad_keys, key_weight)
        + matmul_nt(grad_values, value_weight)
    )
    grad_normed = over_cores(local_normed)
    grad_in_norm, grad_norm1_gain, grad_norm1_bias = norm1_pull(grad_normed)
    input_grad = grad_middle + grad_in_norm
    query_key = matmul_tn(normed, jnp.where(x == 0, grad_queries, grad_keys)) + matmul_tn(
        swapped(normed, 1), swapped(jnp.where(x == 0, grad_keys, grad_queries), 1)
    )
    value_out = matmul_tn(jnp.where(y == 0, normed, grad_middle), jnp.where(y == 0, grad_values, gated)) + matmul_tn(
        swapped(jnp.where(y == 0, grad_middle, normed), 2), swapped(jnp.where(y == 0, gated, grad_values), 2)
    )
    small = (
        grad_norm1_gain,
        grad_norm1_bias,
        grad_norm2_gain,
        grad_norm2_bias,
        grad_out_bias,
        grad_down_bias,
        grad_up_bias,
        grad_query_bias,
        grad_key_bias,
        grad_value_bias,
        grad_skip_gain,
        grad_log_step,
        grad_shift_kernel,
        grad_state_rate,
        grad_state_out,
    )
    small_rows = jnp.concatenate([part.reshape(-1, width_local) for part in small], axis=0)
    small_count = small_rows.shape[0]
    small_size = -(-small_count // 32) * 8
    small_rows = jnp.pad(small_rows, ((0, 4 * small_size - small_count), (0, 0)))
    small_quarter = halved_sum(halved_sum(small_rows, 1, x), 2, y)
    mixer_quarter = jnp.concatenate(
        [halved_sum(query_key, 2, y), halved_sum(value_out, 1, x), small_quarter], axis=0
    )
    mixer_rows = mixer_quarter.shape[0] // 2
    feed_rows = up_quarter.shape[0]
    piece_rows = PIECE_ROWS
    pieces = -(-(feed_rows + -(-mixer_rows // 2)) // piece_rows)
    spare = 2 * (pieces * piece_rows - feed_rows) - mixer_rows
    mixer_wide = jnp.concatenate([mixer_quarter[:mixer_rows], mixer_quarter[mixer_rows:]], axis=1)
    mixer_wide = jnp.pad(mixer_wide, ((0, spare), (0, 0)))
    own = jnp.concatenate(
        [jnp.stack([up_quarter, down_quarter]), mixer_wide.reshape(2, -1, mixer_wide.shape[1])], axis=1
    )
    sums = summed_quarters(own, pieces, LAG)
    width = sums.shape[-1]
    feed = sums[:, :, :feed_rows].reshape(2, 2, 2, feed_rows, width)
    grad_up_weight = feed[:, :, 0].transpose(1, 2, 0, 3).reshape(2 * feed_rows, 2 * width)
    grad_down_weight = feed[:, :, 1].transpose(1, 0, 2, 3).reshape(4 * feed_rows, width)
    rest = sums[:, :, feed_rows:].reshape(4, -1, width)[:, :mixer_rows]
    rest = jnp.concatenate([rest[..., :width_local], rest[..., width_local:]], axis=1)
    rest = rest.reshape(2, 2, 2 * mixer_rows, width_local)
    projection = 2 * (width // 4)
    grad_query_weight = rest[:, 0, :projection].reshape(-1, width_local)
    grad_key_weight = rest[:, 1, :projection].reshape(-1, width_local)
    grad_value_weight = rest[0, :, projection : 2 * projection].reshape(-1, width_local)
    grad_out_weight = rest[1, :, projection : 2 * projection].reshape(-1, width_local).T
    flat = rest[:, :, 2 * projection :].transpose(1, 0, 2, 3).reshape(-1, width_local)
    unpacked = []
    start = 0
    for part in small:
        count = part.size // width_local
        unpacked.append(flat[start : start + count].reshape(part.shape))
        start += count
    (
        grad_norm1_gain,
        grad_norm1_bias,
        grad_norm2_gain,
        grad_norm2_bias,
        grad_out_bias,
        grad_down_bias,
        grad_up_bias,
        grad_query_bias,
        grad_key_bias,
        grad_value_bias,
        grad_skip_gain,
        grad_log_step,
        grad_shift_kernel,
        grad_state_rate,
        grad_state_out,
    ) = unpacked
    return (
        block_out,
        input_grad,
        grad_norm1_gain,
        grad_norm1_bias,
        grad_query_weight,
        grad_query_bias,
        grad_key_weight,
        grad_key_bias,
        grad_value_weight,
        grad_value_bias,
        grad_shift_kernel,
        grad_log_step,
        grad_state_rate,
        grad_state_out,
        grad_skip_gain,
        grad_out_weight,
        grad_out_bias,
        grad_norm2_gain,
        grad_norm2_bias,
        grad_up_weight,
        grad_up_bias,
        grad_down_weight,
        grad_down_bias,
    )


def solution(mesh):
    return jax.shard_map(
        on_device,
        mesh=mesh,
        in_specs=(
            P("seq", None),
            P("seq", None),
            P(),
            P(),
            P(None, "tp"),
            P("tp"),
            P(None, "tp"),
            P("tp"),
            P(None, "tp"),
            P("tp"),
            P(None, "tp"),
            P("tp"),
            P(None, "tp"),
            P(None, "tp"),
            P("tp"),
            P("tp", None),
            P(),
            P(),
            P(),
            P(None, "tp"),
            P("tp"),
            P("tp", None),
            P(),
        ),
        out_specs=(
            P("seq", None),
            P("seq", None),
            P(),
            P(),
            P(None, "tp"),
            P("tp"),
            P(None, "tp"),
            P("tp"),
            P(None, "tp"),
            P("tp"),
            P(None, "tp"),
            P("tp"),
            P(None, "tp"),
            P(None, "tp"),
            P("tp"),
            P("tp", None),
            P(),
            P(),
            P(),
            P(None, "tp"),
            P("tp"),
            P("tp", None),
            P(),
        ),
        check_vma=False,
    )
```

```python
import functools

import jax
import jax.numpy as jnp
from jax import lax
from jax.experimental import pallas as pl
from jax.experimental.pallas import tpu as pltpu
from jax.sharding import PartitionSpec as P

SHIFT = 4
SEQS = 2
STATE = 64
LANES = 128
CHUNK = 32
PIECE_ROWS = 24
LAG = 2

EPSILON = 1e-05
F32 = jnp.float32
PRECISION = lax.Precision.HIGH


def shape(*dims):
    return jax.ShapeDtypeStruct(dims, F32)


def fold_states(values):
    return jnp.sum(values.reshape(STATE // 8, 8, LANES), axis=0)


def cut(block):
    return pl.ds(block * LANES, LANES)


class Sequence:
    def __init__(self, span, backward):
        self.me = lax.axis_index("seq")
        self.span = span
        self.place = lax.rem(self.me, span)
        self.start = self.me - self.place
        self.groups = span // 4
        self.quarter, self.group = lax.rem(self.place, 4), self.place // 4
        if backward:
            self.rank, self.turn = 3 - self.quarter, self.groups - 1 - self.group
        else:
            self.rank, self.turn = self.quarter, self.group
        self.backward = backward

    def greet(self):
        barrier = pltpu.get_barrier_semaphore()
        for k in range(1, self.span):
            peer = self.start + lax.rem(self.place + k, self.span)
            pl.semaphore_signal(barrier, inc=1, device_id={"seq": peer}, device_id_type=pl.DeviceIdType.MESH)
        pl.semaphore_wait(barrier, self.span - 1)

    def remote(self, source, target, send, recv, peer):
        return pltpu.make_async_remote_copy(
            src_ref=source,
            dst_ref=target,
            send_sem=send,
            recv_sem=recv,
            device_id={"seq": peer},
            device_id_type=pl.DeviceIdType.MESH,
        )

    def end_copy(self, b, k, ends_ref, sems):
        other = lax.rem(self.quarter + k, 4)
        peer = self.me - self.quarter + other
        ref = ends_ref.at[self.rank, :, cut(b)]
        return self.remote(ref, ref, sems[0].at[b, k - 1], sems[1].at[b, k - 1], peer)

    def total_copy(self, b, k, totals_ref, sems):
        peer = self.me - 4 * k if self.backward else self.me + 4 * k
        ref = totals_ref.at[self.turn, :, cut(b)]
        return self.remote(ref, ref, sems[2].at[b, k - 1], sems[3].at[b, k - 1], peer)

    def send_end(self, b, end, ends_ref, sems):
        ends_ref[self.rank, :, cut(b)] = end
        for k in range(1, 4):
            self.end_copy(b, k, ends_ref, sems).start()

    def group_total(self, b, decay, ends_ref, totals_ref, sems):
        for k in range(1, 4):
            self.end_copy(b, k, ends_ref, sems).wait_recv()
        before = jnp.zeros_like(decay)
        total = ends_ref[0, :, cut(b)]
        for r in range(3):
            before = jnp.where(self.rank > r, before * decay + ends_ref[r, :, cut(b)], before)
            total = total * decay + ends_ref[r + 1, :, cut(b)]
        if self.groups > 1:
            totals_ref[self.turn, :, cut(b)] = total
            for k in range(1, self.groups):
                pl.when(self.turn + k < self.groups)(lambda: self.total_copy(b, k, totals_ref, sems).start())
        return before

    def carried(self, b, decay, before, totals_ref, sems):
        if self.groups == 1:
            return before
        square = decay * decay
        fourth = square * square
        carry = jnp.zeros_like(decay)
        for h in range(self.groups - 1):
            for k in range(1, self.groups - h):
                pl.when(self.turn == h + k)(lambda: self.total_copy(b, k, totals_ref, sems).wait_recv())
        for h in range(self.groups - 1):
            carry = jnp.where(self.turn > h, carry * fourth + totals_ref[h, :, cut(b)], carry)
        for r in range(3):
            carry = jnp.where(self.rank > r, carry * decay, carry)
        return before + carry

    def drain(self, blocks, ends_ref, totals_ref, sems):
        for b in range(blocks):
            for k in range(1, 4):
                self.end_copy(b, k, ends_ref, sems).wait_send()
            for k in range(1, self.groups):
                pl.when(self.turn + k < self.groups)(lambda: self.total_copy(b, k, totals_ref, sems).wait_send())


def mixer_kernel(
    span, query_ref, key_ref, value_ref, taps_ref, skip_ref, decay_ref, out_coef_ref, device_decay_ref,
    gated_ref, out_ref, mixed_ref, shifted_ref, starts_ref, halo_ref,
    keys_ref, rows_ref, part_ref, ends_ref, totals_ref, end_send, end_recv, total_send, total_recv, halo_send, halo_recv
):
    tokens, width = key_ref.shape
    blocks = width // LANES
    seq = Sequence(span, False)
    sems = (end_send, end_recv, total_send, total_recv)
    keys_ref[pl.ds(8, tokens), :] = key_ref[...]
    seq.greet()

    def halo_copy(peer):
        return seq.remote(key_ref.at[pl.ds(tokens - 8, 8)], halo_ref, halo_send.at[0], halo_recv.at[0], peer)

    first, last = seq.place == 0, seq.place == span - 1
    pl.when(jnp.logical_not(last))(lambda: halo_copy(seq.me + 1).start())

    def mix(start, count):
        total = taps_ref[0:1, :] * keys_ref[pl.ds(8 + start, count), :]
        for j in range(1, SHIFT):
            total = total + taps_ref[j : j + 1, :] * keys_ref[pl.ds(8 + start - j, count), :]
        shifted_ref[pl.ds(start, count), :] = total
        mixed = total * value_ref[pl.ds(start, count), :]
        mixed_ref[pl.ds(start, count), :] = mixed
        for b in range(blocks):
            rows_ref[b, pl.ds(start, count), :] = mixed[:, b * LANES : (b + 1) * LANES]

    mix(8, tokens - 8)

    @pl.when(first)
    def _():
        halo_ref[...] = jnp.zeros_like(halo_ref)

    @pl.when(jnp.logical_not(first))
    def _():
        halo_copy(seq.me + 1).wait_recv()

    keys_ref[pl.ds(0, 8), :] = halo_ref[...]
    mix(0, 8)
    for b in range(blocks):
        decay, out_coef = decay_ref[:, cut(b)], out_coef_ref[:, cut(b)]

        def scan(k, state, b=b, decay=decay, out_coef=out_coef):
            starts_ref[k, :, cut(b)] = state
            base = pl.multiple_of(k * CHUNK, CHUNK)
            for j in range(CHUNK):
                state = decay * state + rows_ref[b, pl.ds(base + j, 1), :]
                part_ref[j] = fold_states(out_coef * state)
            out_ref[pl.ds(base, CHUNK), cut(b)] = jnp.sum(part_ref[...], axis=1)
            return state

        seq.send_end(b, lax.fori_loop(0, tokens // CHUNK, scan, jnp.zeros_like(decay)), ends_ref, sems)
    befores = [seq.group_total(b, device_decay_ref[:, cut(b)], ends_ref, totals_ref, sems) for b in range(blocks)]
    for b in range(blocks):
        decay, out_coef = decay_ref[:, cut(b)], out_coef_ref[:, cut(b)]
        skip = skip_ref[:, cut(b)]

        def carry(k, state, b=b, decay=decay, out_coef=out_coef, skip=skip):
            starts_ref[k, :, cut(b)] = starts_ref[k, :, cut(b)] + state
            base = pl.multiple_of(k * CHUNK, CHUNK)
            for j in range(CHUNK):
                state = decay * state
                part_ref[j] = fold_states(out_coef * state)
            rows = pl.ds(base, CHUNK)
            out = out_ref[rows, cut(b)] + jnp.sum(part_ref[...], axis=1) + skip * mixed_ref[rows, cut(b)]
            out_ref[rows, cut(b)] = out
            gated_ref[rows, cut(b)] = query_ref[rows, cut(b)] * out
            return state

        incoming = seq.carried(b, device_decay_ref[:, cut(b)], befores[b], totals_ref, sems)
        lax.fori_loop(0, tokens // CHUNK, carry, incoming)
    seq.drain(blocks, ends_ref, totals_ref, sems)
    pl.when(jnp.logical_not(last))(lambda: halo_copy(seq.me + 1).wait_send())


def mixer_grad_kernel(
    span, gated_grad_ref, query_ref, key_ref, value_ref, halo_ref, out_ref, mixed_ref, shifted_ref, starts_ref, taps_ref,
    skip_ref, decay_ref, out_coef_ref, device_decay_ref,
    query_grad_ref, key_grad_ref, value_grad_ref, coef_ref, slope_ref, sums_ref,
    grad_ref, rows_ref, grad_rows_ref, keys_ref, shifted_grad_ref, head_ref, part_ref, state_ref, ends_ref, totals_ref,
    end_send, end_recv, total_send, total_recv, halo_send, halo_recv
):
    tokens, width = key_ref.shape
    blocks = width // LANES
    chunks = tokens // CHUNK
    seq = Sequence(span, True)
    sems = (end_send, end_recv, total_send, total_recv)
    grad_ref[...] = gated_grad_ref[...] * query_ref[...]
    for b in range(blocks):
        grad_rows_ref[b] = grad_ref[:, cut(b)]
        rows_ref[b] = mixed_ref[:, cut(b)]
    seq.greet()
    for b in range(blocks):
        decay = decay_ref[:, cut(b)]

        def end(i, adjoint, b=b, decay=decay):
            base = pl.multiple_of((chunks - 1 - i) * CHUNK, CHUNK)
            for j in range(CHUNK - 1, -1, -1):
                adjoint = decay * adjoint + grad_rows_ref[b, pl.ds(base + j, 1), :]
            return adjoint

        seq.send_end(b, lax.fori_loop(0, chunks, end, jnp.zeros_like(decay)), ends_ref, sems)
    query_grad = gated_grad_ref[...] * out_ref[...]
    query_grad_ref[...] = query_grad
    keys_ref[pl.ds(0, 8), :] = halo_ref[...]
    keys_ref[pl.ds(8, tokens), :] = key_ref[...]

    def over_tokens(values):
        return jnp.sum(values, axis=0, keepdims=True)

    sums_ref[0:1, :] = over_tokens(grad_ref[...] * mixed_ref[...])
    sums_ref[5:6, :] = over_tokens(query_grad)
    befores = [seq.group_total(b, device_decay_ref[:, cut(b)], ends_ref, totals_ref, sems) for b in range(blocks)]
    for b in range(blocks):
        decay, out_coef = decay_ref[:, cut(b)], out_coef_ref[:, cut(b)]
        skip = skip_ref[:, cut(b)]
        coef_ref[:, cut(b)] = jnp.zeros_like(decay)
        slope_ref[:, cut(b)] = jnp.zeros_like(decay)

        def chunk(i, adjoint, b=b, decay=decay, out_coef=out_coef, skip=skip):
            k = chunks - 1 - i
            base = pl.multiple_of(k * CHUNK, CHUNK)
            state = starts_ref[k, :, cut(b)]
            for j in range(CHUNK):
                state_ref[j] = state
                state = decay * state + rows_ref[b, pl.ds(base + j, 1), :]
            coef, slope = coef_ref[:, cut(b)], slope_ref[:, cut(b)]
            for j in range(CHUNK - 1, -1, -1):
                adjoint = decay * adjoint + grad_rows_ref[b, pl.ds(base + j, 1), :]
                part_ref[j] = fold_states(out_coef * adjoint)
                coef = coef + adjoint * rows_ref[b, pl.ds(base + j, 1), :]
                slope = slope + adjoint * state_ref[j]
            coef_ref[:, cut(b)] = coef
            slope_ref[:, cut(b)] = slope
            rows = pl.ds(base, CHUNK)
            grad_mixed = jnp.sum(part_ref[...], axis=1) + skip * grad_ref[rows, cut(b)]
            shifted_grad_ref[rows, cut(b)] = grad_mixed * value_ref[rows, cut(b)]
            value_grad_ref[rows, cut(b)] = grad_mixed * shifted_ref[rows, cut(b)]
            return adjoint

        incoming = seq.carried(b, device_decay_ref[:, cut(b)], befores[b], totals_ref, sems)
        lax.fori_loop(0, chunks, chunk, incoming)

    def halo_copy():
        return seq.remote(
            shifted_grad_ref.at[pl.ds(0, 8)], head_ref, halo_send.at[0], halo_recv.at[0], seq.me - 1
        )

    first, last = seq.place == 0, seq.place == span - 1
    pl.when(jnp.logical_not(first))(lambda: halo_copy().start())
    for j in range(SHIFT):
        sums_ref[1 + j : 2 + j, :] = over_tokens(shifted_grad_ref[pl.ds(0, tokens), :] * keys_ref[pl.ds(8 - j, tokens), :])
    sums_ref[7:8, :] = over_tokens(value_grad_ref[...])

    @pl.when(last)
    def _():
        head_ref[...] = jnp.zeros_like(head_ref)

    @pl.when(jnp.logical_not(last))
    def _():
        halo_copy().wait_recv()

    shifted_grad_ref[pl.ds(tokens, 8), :] = head_ref[...]
    key_grad = taps_ref[0:1, :] * shifted_grad_ref[pl.ds(0, tokens), :]
    for j in range(1, SHIFT):
        key_grad = key_grad + taps_ref[j : j + 1, :] * shifted_grad_ref[pl.ds(j, tokens), :]
    key_grad_ref[...] = key_grad
    sums_ref[6:7, :] = over_tokens(key_grad)
    seq.drain(blocks, ends_ref, totals_ref, sems)
    pl.when(jnp.logical_not(first))(lambda: halo_copy().wait_send())


def mixer_call(kernel, span, args, outs, scratch, width, collective_id, name):
    blocks, groups = width // LANES, span // 4
    scratch = [pltpu.VMEM(dims, F32) for dims in scratch]
    scratch += [pltpu.VMEM((4, STATE, width), F32), pltpu.VMEM((groups, STATE, width), F32)]
    sems = [(blocks, 3), (blocks, 3), (blocks, max(1, groups - 1)), (blocks, max(1, groups - 1)), (1,), (1,)]
    return pl.pallas_call(
        functools.partial(kernel, span),
        in_specs=[pl.BlockSpec(memory_space=pltpu.VMEM)] * len(args),
        out_specs=[pl.BlockSpec(memory_space=pltpu.VMEM)] * len(outs),
        out_shape=outs,
        scratch_shapes=scratch + [pltpu.SemaphoreType.DMA(dims) for dims in sems],
        compiler_params=pltpu.CompilerParams(
            collective_id=collective_id, has_side_effects=True, vmem_limit_bytes=32 * 2**20
        ),
        name=name,
    )(*args)


def over_cores(value):
    count = lax.axis_size("tp")
    total = value
    for shift in range(1, count):
        total = total + lax.ppermute(value, "tp", [(i, (i + shift) % count) for i in range(count)])
    return total


MESH = pl.DeviceIdType.MESH


def is_far(i):
    return lax.rem(i, 4) == 2


def sum_kernel(
    length, pieces, rows, lag, own_ref, out_ref, sum_ref, got_ref, load_sem, store_sem, chain_send, chain_recv,
    z_send, z_recv, side_send, side_recv
):
    me = lax.axis_index("seq")
    place, quarter = me // 4, lax.rem(me, 4)
    x, y = lax.rem(quarter, 2), quarter // 2
    x_peer, y_peer = me + 1 - 2 * x, me + 2 - 4 * y
    quarter_x, quarter_y, quarter_d = quarter + 1 - 2 * x, quarter + 2 - 4 * y, 3 - quarter
    first = lag * (length - 1)
    started = (place, length - 1 - place)
    ahead = (me + 4, me - 4)
    behind = (me - 4, me + 4)

    loads = [pltpu.make_async_copy(own_ref.at[d], sum_ref.at[d], load_sem.at[d]) for d in range(2)]
    for load in loads:
        load.start()
    barrier = pltpu.get_barrier_semaphore()

    def greet(peer):
        pl.semaphore_signal(barrier, inc=1, device_id={"seq": peer}, device_id_type=MESH)

    greet(x_peer)
    greet(y_peer)
    pl.when(place > 0)(lambda: greet(me - 4))
    pl.when(place < length - 1)(lambda: greet(me + 4))
    pl.semaphore_wait(barrier, 2 + (place > 0).astype(jnp.int32) + (place < length - 1).astype(jnp.int32))
    for load in loads:
        load.wait()

    def remote(source, target, send, recv, peer):
        return pltpu.make_async_remote_copy(
            src_ref=source,
            dst_ref=target,
            send_sem=send,
            recv_sem=recv,
            device_id={"seq": peer},
            device_id_type=MESH,
        )

    def at(i):
        return pl.ds(pl.multiple_of(i * rows, 8), rows)

    def chain_copy(d, i):
        return remote(
            sum_ref.at[d, at(i)], got_ref.at[d, at(i)], chain_send.at[d, i], chain_recv.at[d, i], ahead[d]
        )

    def z_copy(d, i, k):
        ref = out_ref.at[(quarter, quarter_x, quarter_y, quarter_d)[k], d, at(i)]
        return remote(ref, ref, z_send.at[d, i, k], z_recv.at[d, i, k], behind[d])

    def side_copy(d, i, k):
        even = lax.rem(i, 2) == 0
        source = (quarter, quarter, jnp.where(even, quarter_x, quarter_y))[k]
        peer = (x_peer, y_peer, jnp.where(even, y_peer, x_peer))[k]
        ref = out_ref.at[source, d, at(i)]
        return remote(ref, ref, side_send.at[d, i, k], side_recv.at[d, i, k], peer)

    def chain_step(d, i):
        @pl.when(started[d] > 0)
        def _():
            chain_copy(d, i).wait_recv()
            sum_ref[d, at(i)] = sum_ref[d, at(i)] + got_ref[d, at(i)]

        @pl.when(started[d] < length - 1)
        def _():
            chain_copy(d, i).start()

        @pl.when(started[d] == length - 1)
        def _():
            store = pltpu.make_async_copy(sum_ref.at[d, at(i)], out_ref.at[quarter, d, at(i)], store_sem.at[d, i])
            store.start()
            store.wait()

    def kind(d, i):
        remaining = length - 1 - started[d]
        far = is_far(i)
        sideways = jnp.logical_or(jnp.logical_not(far), remaining == 0)
        onward = jnp.logical_and(far, remaining < length - 1)
        return remaining, sideways, onward

    def own_step(d, i):
        remaining, sideways, _ = kind(d, i)

        @pl.when(remaining > 0)
        def _():
            z_copy(d, i, 0).wait_recv()

        @pl.when(remaining < length - 1)
        def _():
            z_copy(d, i, 0).start()

        @pl.when(sideways)
        def _():
            side_copy(d, i, 0).start()
            side_copy(d, i, 1).start()

    def side_step(d, i):
        _, sideways, onward = kind(d, i)

        @pl.when(sideways)
        def _():
            side_copy(d, i, 0).wait_recv()
            side_copy(d, i, 1).wait_recv()
            side_copy(d, i, 2).start()

        @pl.when(jnp.logical_not(sideways))
        def _():
            z_copy(d, i, 1).wait_recv()
            z_copy(d, i, 2).wait_recv()

        @pl.when(onward)
        def _():
            z_copy(d, i, 1).start()
            z_copy(d, i, 2).start()

    def last_step(d, i):
        _, sideways, onward = kind(d, i)

        @pl.when(sideways)
        def _():
            side_copy(d, i, 2).wait_recv()

        @pl.when(jnp.logical_not(sideways))
        def _():
            z_copy(d, i, 3).wait_recv()

        @pl.when(onward)
        def _():
            z_copy(d, i, 3).start()

    def tick(t, _):
        for step, late in ((last_step, first + 2 * lag), (side_step, first + lag), (chain_step, 0), (own_step, first)):
            for d in range(2):
                passed = started[d] if step is chain_step else length - 1 - started[d]
                i = t - late - lag * passed
                pl.when(jnp.logical_and(i >= 0, i < pieces))(functools.partial(step, d, i))
        return 0

    lax.fori_loop(0, 2 * first + 2 * lag + pieces, tick, 0)

    def drain(i, _):
        for d in range(2):
            remaining, sideways, onward = kind(d, i)
            pl.when(remaining > 0)(lambda: chain_copy(d, i).wait_send())
            pl.when(remaining < length - 1)(lambda: z_copy(d, i, 0).wait_send())

            @pl.when(onward)
            def _():
                for k in range(1, 4):
                    z_copy(d, i, k).wait_send()

            @pl.when(sideways)
            def _():
                for k in range(3):
                    side_copy(d, i, k).wait_send()

        return 0

    lax.fori_loop(0, pieces, drain, 0)


def summed_quarters(own, pieces, lag):
    _, total, columns = own.shape
    length = lax.axis_size("seq") // 4
    sems = [(2,), (2, pieces), (2, pieces), (2, pieces), (2, pieces, 4), (2, pieces, 4), (2, pieces, 3), (2, pieces, 3)]
    return pl.pallas_call(
        functools.partial(sum_kernel, length, pieces, total // pieces, lag),
        out_shape=shape(4, 2, total, columns),
        in_specs=[pl.BlockSpec(memory_space=pl.ANY)],
        out_specs=pl.BlockSpec(memory_space=pltpu.HBM),
        scratch_shapes=[pltpu.VMEM((2, total, columns), F32)] * 2 + [pltpu.SemaphoreType.DMA(dims) for dims in sems],
        compiler_params=pltpu.CompilerParams(collective_id=0, has_side_effects=True, vmem_limit_bytes=32 * 2**20),
        cost_estimate=pl.CostEstimate(flops=total * columns * 2, bytes_accessed=total * columns * 64, transcendentals=0),
        name="gradient_sums",
    )(own)


def swapped(value, bit):
    return lax.ppermute(value, "seq", [(i, i ^ bit) for i in range(lax.axis_size("seq"))])


def half(value, axis, which):
    size = value.shape[axis] // 2
    return lax.dynamic_slice_in_dim(value, which * size, size, axis)


def halved_sum(value, bit, mine):
    return half(value, 0, mine) + swapped(half(value, 0, 1 - mine), bit)


def matmul(left, right):
    return jnp.dot(left, right, precision=PRECISION, preferred_element_type=F32)


def matmul_tn(left, right):
    return lax.dot_general(left, right, (((0,), (0,)), ((), ())), precision=PRECISION, preferred_element_type=F32)


def matmul_nt(left, right):
    return lax.dot_general(left, right, (((1,), (1,)), ((), ())), precision=PRECISION, preferred_element_type=F32)


def layer_norm(values, gain, bias):
    centered = values - jnp.mean(values, axis=-1, keepdims=True)
    spread = jnp.mean(centered * centered, axis=-1, keepdims=True)
    return centered * lax.rsqrt(spread + EPSILON) * gain + bias


def decay_terms(log_step, state_rate):
    decay_rate = jnp.exp(log_step)[None, :] * state_rate
    return (jnp.exp(-decay_rate), jnp.sqrt(-jnp.expm1(-2.0 * decay_rate)))


def on_device(
    tokens,
    cotangent,
    norm1_gain,
    norm1_bias,
    query_weight,
    query_bias,
    key_weight,
    key_bias,
    value_weight,
    value_bias,
    shift_kernel,
    log_step,
    state_rate,
    state_out,
    skip_gain,
    out_weight,
    out_bias,
    norm2_gain,
    norm2_bias,
    up_weight,
    up_bias,
    down_weight,
    down_bias,
):
    tok_rows = tokens.shape[0]
    width_local = query_weight.shape[1]
    span = lax.axis_size("seq") // SEQS
    chunks = tok_rows // CHUNK
    x, y = lax.axis_index("seq") % 2, lax.axis_index("seq") // 2 % 2
    normed, norm1_pull = jax.vjp(layer_norm, tokens, norm1_gain, norm1_bias)
    queries = matmul(normed, query_weight) + query_bias
    key_rows = matmul(normed, key_weight) + key_bias
    value_rows = matmul(normed, value_weight) + value_bias
    decay_rate = jnp.exp(log_step)[None, :] * state_rate
    (decay_factor, in_coef), decay_pull = jax.vjp(decay_terms, log_step, state_rate)
    device_decay = jnp.exp(-decay_rate * tok_rows)
    out_coef = in_coef * state_out
    skip_row = skip_gain[None, :]
    tok_shape, state_shape = shape(tok_rows, width_local), shape(STATE, width_local)
    gated, ssm_out, mixed, shifted, starts, halo = mixer_call(
        mixer_kernel,
        span,
        (queries, key_rows, value_rows, shift_kernel, skip_row, decay_factor, out_coef, device_decay),
        [tok_shape] * 4 + [shape(chunks, STATE, width_local), shape(8, width_local)],
        [(tok_rows + 8, width_local), (width_local // LANES, tok_rows, LANES), (CHUNK, 8, LANES)],
        width_local,
        1,
        "mixer",
    )
    middle = tokens + over_cores(matmul(gated, out_weight)) + out_bias
    normed2, norm2_pull = jax.vjp(layer_norm, middle, norm2_gain, norm2_bias)
    activated, gelu_pull = jax.vjp(jax.nn.gelu, matmul(normed2, up_weight) + up_bias)
    (grad_pre,) = gelu_pull(matmul_nt(cotangent, down_weight))
    grad_normed2 = over_cores(matmul_nt(grad_pre, up_weight))
    block_out = middle + over_cores(matmul(activated, down_weight)) + down_bias
    grad_down_bias = jnp.sum(cotangent, axis=0)
    grad_up_bias = jnp.sum(grad_pre, axis=0)
    down_half = matmul_tn(half(activated, 1, x), cotangent) + matmul_tn(
        swapped(half(activated, 1, 1 - x), 1), swapped(cotangent, 1)
    )
    up_half = matmul_tn(normed2, half(grad_pre, 1, y)) + matmul_tn(
        swapped(normed2, 2), swapped(half(grad_pre, 1, 1 - y), 2)
    )
    down_quarter = halved_sum(down_half, 2, y)
    up_quarter = halved_sum(up_half, 1, x)
    grad_mid_norm, grad_norm2_gain, grad_norm2_bias = norm2_pull(grad_normed2)
    grad_middle = cotangent + grad_mid_norm
    grad_out_bias = jnp.sum(grad_middle, axis=0)
    grad_gated = matmul_nt(grad_middle, out_weight)
    grad_queries, grad_keys, grad_values, coef_sum, slope_sum, mixer_sums = mixer_call(
        mixer_grad_kernel,
        span,
        (grad_gated, queries, key_rows, value_rows, halo, ssm_out, mixed, shifted, starts, shift_kernel)
        + (skip_row, decay_factor, out_coef, device_decay),
        [tok_shape] * 3 + [state_shape] * 2 + [shape(8, width_local)],
        [(tok_rows, width_local)]
        + [(width_local // LANES, tok_rows, LANES)] * 2
        + [(tok_rows + 8, width_local), (tok_rows + 8, width_local), (8, width_local)]
        + [(CHUNK, 8, LANES), (CHUNK, STATE, LANES)],
        width_local,
        2,
        "mixer_grad",
    )
    grad_state_out = in_coef * coef_sum
    grad_log_step, grad_state_rate = decay_pull((out_coef * slope_sum, state_out * coef_sum))
    local_normed = (
        matmul_nt(grad_queries, query_weight)
        + matmul_nt(grad_keys, key_weight)
        + matmul_nt(grad_values, value_weight)
    )
    grad_normed = over_cores(local_normed)
    grad_in_norm, grad_norm1_gain, grad_norm1_bias = norm1_pull(grad_normed)
    input_grad = grad_middle + grad_in_norm
    query_key = matmul_tn(normed, jnp.where(x == 0, grad_queries, grad_keys)) + matmul_tn(
        swapped(normed, 1), swapped(jnp.where(x == 0, grad_keys, grad_queries), 1)
    )
    value_out = matmul_tn(jnp.where(y == 0, normed, grad_middle), jnp.where(y == 0, grad_values, gated)) + matmul_tn(
        swapped(jnp.where(y == 0, grad_middle, normed), 2), swapped(jnp.where(y == 0, gated, grad_values), 2)
    )
    small = (
        grad_norm1_gain,
        grad_norm1_bias,
        grad_norm2_gain,
        grad_norm2_bias,
        grad_out_bias,
        grad_down_bias,
        grad_up_bias,
        grad_log_step,
        grad_state_rate,
        grad_state_out,
        mixer_sums,
    )
    small_rows = jnp.concatenate([part.reshape(-1, width_local) for part in small], axis=0)
    small_count = small_rows.shape[0]
    small_size = -(-small_count // 32) * 8
    small_rows = jnp.pad(small_rows, ((0, 4 * small_size - small_count), (0, 0)))
    small_quarter = halved_sum(halved_sum(small_rows, 1, x), 2, y)
    mixer_quarter = jnp.concatenate(
        [halved_sum(query_key, 2, y), halved_sum(value_out, 1, x), small_quarter], axis=0
    )
    mixer_rows = mixer_quarter.shape[0] // 2
    feed_rows = up_quarter.shape[0]
    piece_rows = PIECE_ROWS
    pieces = -(-(feed_rows + -(-mixer_rows // 2)) // piece_rows)
    spare = 2 * (pieces * piece_rows - feed_rows) - mixer_rows
    mixer_wide = jnp.concatenate([mixer_quarter[:mixer_rows], mixer_quarter[mixer_rows:]], axis=1)
    mixer_wide = jnp.pad(mixer_wide, ((0, spare), (0, 0)))
    own = jnp.concatenate(
        [jnp.stack([up_quarter, down_quarter]), mixer_wide.reshape(2, -1, mixer_wide.shape[1])], axis=1
    )
    sums = summed_quarters(own, pieces, LAG)
    width = sums.shape[-1]
    feed = sums[:, :, :feed_rows].reshape(2, 2, 2, feed_rows, width)
    grad_up_weight = feed[:, :, 0].transpose(1, 2, 0, 3).reshape(2 * feed_rows, 2 * width)
    grad_down_weight = feed[:, :, 1].transpose(1, 0, 2, 3).reshape(4 * feed_rows, width)
    rest = sums[:, :, feed_rows:].reshape(4, -1, width)[:, :mixer_rows]
    rest = jnp.concatenate([rest[..., :width_local], rest[..., width_local:]], axis=1)
    rest = rest.reshape(2, 2, 2 * mixer_rows, width_local)
    projection = 2 * (width // 4)
    grad_query_weight = rest[:, 0, :projection].reshape(-1, width_local)
    grad_key_weight = rest[:, 1, :projection].reshape(-1, width_local)
    grad_value_weight = rest[0, :, projection : 2 * projection].reshape(-1, width_local)
    grad_out_weight = rest[1, :, projection : 2 * projection].reshape(-1, width_local).T
    flat = rest[:, :, 2 * projection :].transpose(1, 0, 2, 3).reshape(-1, width_local)
    unpacked = []
    start = 0
    for part in small:
        count = part.size // width_local
        unpacked.append(flat[start : start + count].reshape(part.shape))
        start += count
    (
        grad_norm1_gain,
        grad_norm1_bias,
        grad_norm2_gain,
        grad_norm2_bias,
        grad_out_bias,
        grad_down_bias,
        grad_up_bias,
        grad_log_step,
        grad_state_rate,
        grad_state_out,
        mixer_sums,
    ) = unpacked
    grad_skip_gain, grad_shift_kernel = mixer_sums[0], mixer_sums[1:5]
    grad_query_bias, grad_key_bias, grad_value_bias = mixer_sums[5], mixer_sums[6], mixer_sums[7]
    return (
        block_out,
        input_grad,
        grad_norm1_gain,
        grad_norm1_bias,
        grad_query_weight,
        grad_query_bias,
        grad_key_weight,
        grad_key_bias,
        grad_value_weight,
        grad_value_bias,
        grad_shift_kernel,
        grad_log_step,
        grad_state_rate,
        grad_state_out,
        grad_skip_gain,
        grad_out_weight,
        grad_out_bias,
        grad_norm2_gain,
        grad_norm2_bias,
        grad_up_weight,
        grad_up_bias,
        grad_down_weight,
        grad_down_bias,
    )


def solution(mesh):
    return jax.shard_map(
        on_device,
        mesh=mesh,
        in_specs=(
            P("seq", None),
            P("seq", None),
            P(),
            P(),
            P(None, "tp"),
            P("tp"),
            P(None, "tp"),
            P("tp"),
            P(None, "tp"),
            P("tp"),
            P(None, "tp"),
            P("tp"),
            P(None, "tp"),
            P(None, "tp"),
            P("tp"),
            P("tp", None),
            P(),
            P(),
            P(),
            P(None, "tp"),
            P("tp"),
            P("tp", None),
            P(),
        ),
        out_specs=(
            P("seq", None),
            P("seq", None),
            P(),
            P(),
            P(None, "tp"),
            P("tp"),
            P(None, "tp"),
            P("tp"),
            P(None, "tp"),
            P("tp"),
            P(None, "tp"),
            P("tp"),
            P(None, "tp"),
            P(None, "tp"),
            P("tp"),
            P("tp", None),
            P(),
            P(),
            P(),
            P(None, "tp"),
            P("tp"),
            P("tp", None),
            P(),
        ),
        check_vma=False,
    )
```

```python
import functools

import jax
import jax.numpy as jnp
from jax import lax
from jax.experimental import pallas as pl
from jax.experimental.pallas import tpu as pltpu
from jax.sharding import PartitionSpec as P

SHIFT = 4
SEQS = 2
STATE = 64
LANES = 128
CHUNK = 32
PIECE_ROWS = 24
LAG = 2
GELU_SCALE = (2.0 / 3.141592653589793) ** 0.5

EPSILON = 1e-05
F32 = jnp.float32
PRECISION = lax.Precision.HIGH


def shape(*dims):
    return jax.ShapeDtypeStruct(dims, F32)


def fold_states(values):
    return jnp.sum(values.reshape(STATE // 8, 8, LANES), axis=0)


def cut(block):
    return pl.ds(block * LANES, LANES)


class Sequence:
    def __init__(self, span, backward):
        self.me = lax.axis_index("seq")
        self.span = span
        self.place = lax.rem(self.me, span)
        self.start = self.me - self.place
        self.groups = span // 4
        self.quarter, self.group = lax.rem(self.place, 4), self.place // 4
        if backward:
            self.rank, self.turn = 3 - self.quarter, self.groups - 1 - self.group
        else:
            self.rank, self.turn = self.quarter, self.group
        self.backward = backward

    def greet(self, other_core=None):
        barrier = pltpu.get_barrier_semaphore()
        for k in range(1, self.span):
            peer = self.start + lax.rem(self.place + k, self.span)
            pl.semaphore_signal(barrier, inc=1, device_id={"seq": peer}, device_id_type=pl.DeviceIdType.MESH)
        if other_core is not None:
            pl.semaphore_signal(barrier, inc=1, device_id={"tp": other_core}, device_id_type=pl.DeviceIdType.MESH)
        pl.semaphore_wait(barrier, self.span - 1 + (other_core is not None))

    def remote(self, source, target, send, recv, peer, core=None):
        return pltpu.make_async_remote_copy(
            src_ref=source,
            dst_ref=target,
            send_sem=send,
            recv_sem=recv,
            device_id={"seq": peer} if core is None else {"tp": core},
            device_id_type=pl.DeviceIdType.MESH,
        )

    def end_copy(self, b, k, ends_ref, sems):
        other = lax.rem(self.quarter + k, 4)
        peer = self.me - self.quarter + other
        ref = ends_ref.at[self.rank, :, cut(b)]
        return self.remote(ref, ref, sems[0].at[b, k - 1], sems[1].at[b, k - 1], peer)

    def total_copy(self, b, k, totals_ref, sems):
        peer = self.me - 4 * k if self.backward else self.me + 4 * k
        ref = totals_ref.at[self.turn, :, cut(b)]
        return self.remote(ref, ref, sems[2].at[b, k - 1], sems[3].at[b, k - 1], peer)

    def send_end(self, b, end, ends_ref, sems):
        ends_ref[self.rank, :, cut(b)] = end
        for k in range(1, 4):
            self.end_copy(b, k, ends_ref, sems).start()

    def group_total(self, b, decay, ends_ref, totals_ref, sems):
        for k in range(1, 4):
            self.end_copy(b, k, ends_ref, sems).wait_recv()
        before = jnp.zeros_like(decay)
        total = ends_ref[0, :, cut(b)]
        for r in range(3):
            before = jnp.where(self.rank > r, before * decay + ends_ref[r, :, cut(b)], before)
            total = total * decay + ends_ref[r + 1, :, cut(b)]
        if self.groups > 1:
            totals_ref[self.turn, :, cut(b)] = total
            for k in range(1, self.groups):
                pl.when(self.turn + k < self.groups)(lambda: self.total_copy(b, k, totals_ref, sems).start())
        return before

    def carried(self, b, decay, before, totals_ref, sems):
        if self.groups == 1:
            return before
        square = decay * decay
        fourth = square * square
        carry = jnp.zeros_like(decay)
        for h in range(self.groups - 1):
            for k in range(1, self.groups - h):
                pl.when(self.turn == h + k)(lambda: self.total_copy(b, k, totals_ref, sems).wait_recv())
        for h in range(self.groups - 1):
            carry = jnp.where(self.turn > h, carry * fourth + totals_ref[h, :, cut(b)], carry)
        for r in range(3):
            carry = jnp.where(self.rank > r, carry * decay, carry)
        return before + carry

    def drain(self, blocks, ends_ref, totals_ref, sems):
        for b in range(blocks):
            for k in range(1, 4):
                self.end_copy(b, k, ends_ref, sems).wait_send()
            for k in range(1, self.groups):
                pl.when(self.turn + k < self.groups)(lambda: self.total_copy(b, k, totals_ref, sems).wait_send())


def mixer_kernel(
    span, query_ref, key_ref, value_ref, taps_ref, skip_ref, decay_ref, out_coef_ref, device_decay_ref,
    gated_ref, out_ref, mixed_ref, shifted_ref, starts_ref, halo_ref,
    keys_ref, rows_ref, part_ref, ends_ref, totals_ref, end_send, end_recv, total_send, total_recv, halo_send, halo_recv
):
    tokens, width = key_ref.shape
    blocks = width // LANES
    seq = Sequence(span, False)
    sems = (end_send, end_recv, total_send, total_recv)
    keys_ref[pl.ds(8, tokens), :] = key_ref[...]
    seq.greet()

    def halo_copy(peer):
        return seq.remote(key_ref.at[pl.ds(tokens - 8, 8)], halo_ref, halo_send.at[0], halo_recv.at[0], peer)

    first, last = seq.place == 0, seq.place == span - 1
    pl.when(jnp.logical_not(last))(lambda: halo_copy(seq.me + 1).start())

    def mix(start, count):
        total = taps_ref[0:1, :] * keys_ref[pl.ds(8 + start, count), :]
        for j in range(1, SHIFT):
            total = total + taps_ref[j : j + 1, :] * keys_ref[pl.ds(8 + start - j, count), :]
        shifted_ref[pl.ds(start, count), :] = total
        mixed = total * value_ref[pl.ds(start, count), :]
        mixed_ref[pl.ds(start, count), :] = mixed
        for b in range(blocks):
            rows_ref[b, pl.ds(start, count), :] = mixed[:, b * LANES : (b + 1) * LANES]

    mix(8, tokens - 8)

    @pl.when(first)
    def _():
        halo_ref[...] = jnp.zeros_like(halo_ref)

    @pl.when(jnp.logical_not(first))
    def _():
        halo_copy(seq.me + 1).wait_recv()

    keys_ref[pl.ds(0, 8), :] = halo_ref[...]
    mix(0, 8)
    for b in range(blocks):
        decay, out_coef = decay_ref[:, cut(b)], out_coef_ref[:, cut(b)]

        def scan(k, state, b=b, decay=decay, out_coef=out_coef):
            starts_ref[k, :, cut(b)] = state
            base = pl.multiple_of(k * CHUNK, CHUNK)
            for j in range(CHUNK):
                state = decay * state + rows_ref[b, pl.ds(base + j, 1), :]
                part_ref[j] = fold_states(out_coef * state)
            out_ref[pl.ds(base, CHUNK), cut(b)] = jnp.sum(part_ref[...], axis=1)
            return state

        seq.send_end(b, lax.fori_loop(0, tokens // CHUNK, scan, jnp.zeros_like(decay)), ends_ref, sems)
    befores = [seq.group_total(b, device_decay_ref[:, cut(b)], ends_ref, totals_ref, sems) for b in range(blocks)]
    for b in range(blocks):
        decay, out_coef = decay_ref[:, cut(b)], out_coef_ref[:, cut(b)]
        skip = skip_ref[:, cut(b)]

        def carry(k, state, b=b, decay=decay, out_coef=out_coef, skip=skip):
            starts_ref[k, :, cut(b)] = starts_ref[k, :, cut(b)] + state
            base = pl.multiple_of(k * CHUNK, CHUNK)
            for j in range(CHUNK):
                state = decay * state
                part_ref[j] = fold_states(out_coef * state)
            rows = pl.ds(base, CHUNK)
            out = out_ref[rows, cut(b)] + jnp.sum(part_ref[...], axis=1) + skip * mixed_ref[rows, cut(b)]
            out_ref[rows, cut(b)] = out
            gated_ref[rows, cut(b)] = query_ref[rows, cut(b)] * out
            return state

        incoming = seq.carried(b, device_decay_ref[:, cut(b)], befores[b], totals_ref, sems)
        lax.fori_loop(0, tokens // CHUNK, carry, incoming)
    seq.drain(blocks, ends_ref, totals_ref, sems)
    pl.when(jnp.logical_not(last))(lambda: halo_copy(seq.me + 1).wait_send())


def dot(left, right, left_axis, right_axis):
    return lax.dot_general(
        left, right, (((left_axis,), (right_axis,)), ((), ())), precision=PRECISION, preferred_element_type=F32
    )


def over_tokens(values):
    return jnp.sum(values, axis=0, keepdims=True)


def over_features(values):
    return jnp.mean(values, axis=1, keepdims=True)


class Share:
    def __init__(self, seq, source_ref, target_ref, send, recv, peer, core, other_core):
        self.source_ref, self.target_ref, self.send, self.recv = source_ref, target_ref, send, recv
        self.seq, self.peer, self.core, self.other_core = seq, peer, core, other_core
        size = source_ref.shape[0] // 2
        self.mine = pl.ds(pl.multiple_of(core * size, 8), size)

    def across(self):
        return self.seq.remote(
            self.source_ref.at[self.mine], self.target_ref.at[self.mine], self.send.at[0], self.recv.at[0], self.peer
        )

    def between(self):
        ref = self.target_ref.at[self.mine]
        return self.seq.remote(ref, ref, self.send.at[1], self.recv.at[1], self.seq.me, self.other_core)

    def relay(self):
        self.across().wait_recv()
        self.between().start()

    def finish(self):
        self.between().wait_recv()
        self.across().wait_send()
        self.between().wait_send()


def layer_kernel(
    span,
    gated_ref, tokens_ref, cotangent_ref, out_weight_ref, out_bias_ref, gain_ref, bias_ref, up_hbm, up_bias_ref, down_hbm,
    down_bias_ref, query_ref, key_ref, value_ref, halo_ref, out_ref, mixed_ref, shifted_ref, starts_ref, taps_ref,
    skip_ref, decay_ref, out_coef_ref, device_decay_ref, normed1_ref, in_coef_ref, coef_rate_ref, rate_ref, step_ref,
    block_out_ref, middle_grad_ref, query_grad_ref, key_grad_ref, value_grad_ref, small_ref, down_half_ref, up_half_ref,
    normed1_x_ref, narrow_x_ref, wide_y_ref, narrow_y_ref,
    up_ref, down_ref, active_ref, pre_grad_ref, normed_ref, scaled_ref, middle_ref, merged_ref, merged_other_ref,
    feed_ref, feed_other_ref, normed_grad_ref, normed_grad_other_ref,
    active_peer_ref, pre_grad_peer_ref, cotangent_peer_ref, normed_peer_ref,
    gated_grad_ref, grad_ref, rows_ref, grad_rows_ref, keys_ref, shifted_grad_ref, head_ref, part_ref, state_ref,
    coef_ref, slope_ref, ends_ref, totals_ref,
    end_send, end_recv, total_send, total_recv, halo_send, halo_recv,
    load_sem, core_send, core_recv, half_send, half_recv, share_send, share_recv
):
    tokens, width = key_ref.shape
    hidden = up_ref.shape[1]
    hidden_half = hidden // 2
    blocks = width // LANES
    chunks = tokens // CHUNK
    seq = Sequence(span, True)
    sems = (end_send, end_recv, total_send, total_recv)
    x, y = lax.rem(seq.me, 2), lax.rem(seq.me // 2, 2)
    x_peer, y_peer = seq.me + 1 - 2 * x, seq.me + 2 - 4 * y
    core = lax.axis_index("tp")
    other_core = 1 - core
    loads = [
        pltpu.make_async_copy(source, target, load_sem.at[n])
        for n, (source, target) in enumerate(((up_hbm, up_ref), (down_hbm, down_ref)))
    ]
    for load in loads:
        load.start()
    seq.greet(other_core)

    def core_copy(n, source, target):
        return seq.remote(source, target, core_send.at[n], core_recv.at[n], seq.me, other_core)

    cotangent_share = Share(
        seq, cotangent_ref, cotangent_peer_ref, share_send.at[0], share_recv.at[0], x_peer, core, other_core
    )
    normed_share = Share(
        seq, normed_ref, normed_peer_ref, share_send.at[1], share_recv.at[1], y_peer, core, other_core
    )
    normed1_share = Share(
        seq, normed1_ref, normed1_x_ref, share_send.at[2], share_recv.at[2], x_peer, core, other_core
    )
    wide_shares = [
        Share(seq, source, wide_y_ref, share_send.at[3], share_recv.at[3], y_peer, core, other_core)
        for source in (middle_grad_ref, normed1_ref)
    ]

    def narrow_copies():
        return (
            seq.remote(key_grad_ref, narrow_x_ref, half_send.at[2], half_recv.at[2], x_peer),
            seq.remote(query_grad_ref, narrow_x_ref, half_send.at[2], half_recv.at[2], x_peer),
            seq.remote(gated_ref, narrow_y_ref, half_send.at[3], half_recv.at[3], y_peer),
            seq.remote(value_grad_ref, narrow_y_ref, half_send.at[3], half_recv.at[3], y_peer),
        )

    cotangent_share.across().start()
    normed1_share.across().start()
    pl.when(y == 0)(lambda: narrow_copies()[2].start())
    pl.when(y == 1)(lambda: wide_shares[1].across().start())

    small_ref[...] = jnp.zeros_like(small_ref)

    def put(k, row):
        small_ref[1, pl.ds(STATE // 4 + k // 2, 1), pl.ds(k % 2 * width, width)] = row

    top = tokens // 2
    merged_copies = []
    for n in range(2):
        rows = pl.ds(n * top, top)
        merged_ref[rows, :] = dot(gated_ref[rows, :], out_weight_ref[...], 1, 0)
        copy = core_copy(n, merged_ref.at[rows], merged_other_ref.at[rows])
        copy.start()
        merged_copies.append(copy)
    spreads = []
    for n, copy in enumerate(merged_copies):
        rows = pl.ds(n * top, top)
        copy.wait_recv()
        middle = tokens_ref[rows, :] + (merged_ref[rows, :] + merged_other_ref[rows, :]) + out_bias_ref[...]
        centered = middle - over_features(middle)
        inverse = lax.rsqrt(over_features(centered * centered) + EPSILON)
        scaled = centered * inverse
        middle_ref[rows, :] = middle
        scaled_ref[rows, :] = scaled
        normed_ref[rows, :] = scaled * gain_ref[...] + bias_ref[...]
        spreads.append(inverse)
    normed_share.across().start()

    for load in loads:
        load.wait()
    for n in range(2):
        part = pl.ds(n * hidden_half, hidden_half)
        pre = dot(normed_ref[...], up_ref[:, part], 1, 0) + up_bias_ref[:, part]
        square = pre * pre
        curve = jnp.tanh(GELU_SCALE * (pre + 0.044715 * (square * pre)))
        active = 0.5 * pre * (1.0 + curve)
        active_ref[n] = active
        slope = 0.5 * (1.0 + curve) + 0.5 * pre * (1.0 - curve * curve) * (
            GELU_SCALE * (1.0 + 3 * 0.044715 * square)
        )
        pre_grad = dot(cotangent_ref[...], down_ref[part, :], 1, 1) * slope
        pre_grad_ref[n] = pre_grad
        small_ref[0, pl.ds(STATE // 4 + 6 + n, 1), :] = over_tokens(pre_grad)
        normed_grad = dot(pre_grad, up_ref[:, part], 1, 1)
        if n == 0:
            normed_grad_ref[...] = normed_grad
        else:
            normed_grad_ref[...] = normed_grad_ref[...] + normed_grad
    normed_grad_copy = core_copy(2, normed_grad_ref, normed_grad_other_ref)
    normed_grad_copy.start()
    for n in range(2):
        part = pl.ds(n * hidden_half, hidden_half)
        feed = dot(active_ref[n], down_ref[part, :], 1, 0)
        if n == 0:
            feed_ref[...] = feed
        else:
            feed_ref[...] = feed_ref[...] + feed
    feed_copy = core_copy(3, feed_ref, feed_other_ref)
    feed_copy.start()
    cotangent_share.relay()
    normed1_share.relay()
    normed_share.relay()
    normed_grad_copy.wait_recv()
    for n in range(2):
        rows = pl.ds(n * top, top)
        normed_grad = normed_grad_ref[rows, :] + normed_grad_other_ref[rows, :]
        scaled = scaled_ref[rows, :]
        scaled_grad = normed_grad * gain_ref[...]
        centered = scaled_grad - over_features(scaled_grad) - scaled * over_features(scaled_grad * scaled)
        middle_grad = cotangent_ref[rows, :] + spreads[n] * centered
        middle_grad_ref[rows, :] = middle_grad
        sums = (normed_grad * scaled, normed_grad, middle_grad, cotangent_ref[rows, :])
        for k, values in enumerate(sums):
            row = pl.ds(STATE // 4 + 2 + k, 1)
            if n == 0:
                small_ref[0, row, :] = over_tokens(values)
            else:
                small_ref[0, row, :] = small_ref[0, row, :] + over_tokens(values)
        gated_grad_ref[rows, :] = dot(middle_grad, out_weight_ref[...], 1, 1)

    grad = gated_grad_ref[...] * query_ref[...]
    grad_ref[...] = grad
    for b in range(blocks):
        grad_rows_ref[b] = grad[:, b * LANES : (b + 1) * LANES]
        rows_ref[b] = mixed_ref[:, cut(b)]
    for b in range(blocks):
        decay = decay_ref[:, cut(b)]

        def end(i, adjoint, b=b, decay=decay):
            base = pl.multiple_of((chunks - 1 - i) * CHUNK, CHUNK)
            for j in range(CHUNK - 1, -1, -1):
                adjoint = decay * adjoint + grad_rows_ref[b, pl.ds(base + j, 1), :]
            return adjoint

        seq.send_end(b, lax.fori_loop(0, chunks, end, jnp.zeros_like(decay)), ends_ref, sems)
    query_grad = gated_grad_ref[...] * out_ref[...]
    query_grad_ref[...] = query_grad
    keys_ref[pl.ds(0, 8), :] = halo_ref[...]
    keys_ref[pl.ds(8, tokens), :] = key_ref[...]
    put(0, over_tokens(grad_ref[...] * mixed_ref[...]))
    put(5, over_tokens(query_grad))
    feed_copy.wait_recv()
    block_out_ref[...] = middle_ref[...] + (feed_ref[...] + feed_other_ref[...]) + down_bias_ref[...]

    def half_product(result_ref, left_ref, right_ref, first):
        size = width

        def tile(i, _):
            part = pl.ds(pl.multiple_of(i * size, size), size)
            product = dot(left_ref[:, part], right_ref[...], 0, 0)
            result_ref[part, :] = product if first else result_ref[part, :] + product
            return 0

        lax.fori_loop(0, result_ref.shape[0] // size, tile, 0)

    befores = [seq.group_total(b, device_decay_ref[:, cut(b)], ends_ref, totals_ref, sems) for b in range(blocks)]
    half_product(down_half_ref, active_ref.at[x], cotangent_ref, True)
    incoming = [seq.carried(b, device_decay_ref[:, cut(b)], befores[b], totals_ref, sems) for b in range(blocks)]

    def half_copies():
        return (
            seq.remote(active_ref.at[1 - x], active_peer_ref, half_send.at[0], half_recv.at[0], x_peer),
            seq.remote(pre_grad_ref.at[1 - y], pre_grad_peer_ref, half_send.at[1], half_recv.at[1], y_peer),
        )

    for copy in half_copies():
        copy.start()
    pl.when(y == 0)(lambda: wide_shares[0].across().start())
    pl.when(x == 1)(lambda: narrow_copies()[1].start())

    def state_sums():
        quarter = STATE // 4
        for p in range(4):
            rows = pl.ds(p * quarter, quarter)
            coef = coef_ref[rows, :]
            rate_grad = coef_rate_ref[rows, :] * coef - decay_ref[rows, :] * out_coef_ref[rows, :] * slope_ref[rows, :]
            step_grad = over_tokens(rate_ref[rows, :] * rate_grad)
            put(8, step_grad if p == 0 else small_ref[1, pl.ds(quarter + 4, 1), pl.ds(0, width)] + step_grad)
            small_ref[p, pl.ds(0, quarter), pl.ds(0, width)] = step_ref[...] * rate_grad
            small_ref[p, pl.ds(0, quarter), pl.ds(width, width)] = in_coef_ref[rows, :] * coef

    for b in range(blocks):
        decay, out_coef = decay_ref[:, cut(b)], out_coef_ref[:, cut(b)]
        skip = skip_ref[:, cut(b)]
        coef_ref[:, cut(b)] = jnp.zeros_like(decay)
        slope_ref[:, cut(b)] = jnp.zeros_like(decay)

        def chunk(i, adjoint, b=b, decay=decay, out_coef=out_coef, skip=skip):
            k = chunks - 1 - i
            base = pl.multiple_of(k * CHUNK, CHUNK)
            state = starts_ref[k, :, cut(b)]
            for j in range(CHUNK):
                state_ref[j] = state
                state = decay * state + rows_ref[b, pl.ds(base + j, 1), :]
            coef, slope = coef_ref[:, cut(b)], slope_ref[:, cut(b)]
            for j in range(CHUNK - 1, -1, -1):
                adjoint = decay * adjoint + grad_rows_ref[b, pl.ds(base + j, 1), :]
                part_ref[j] = fold_states(out_coef * adjoint)
                coef = coef + adjoint * rows_ref[b, pl.ds(base + j, 1), :]
                slope = slope + adjoint * state_ref[j]
            coef_ref[:, cut(b)] = coef
            slope_ref[:, cut(b)] = slope
            rows = pl.ds(base, CHUNK)
            grad_mixed = jnp.sum(part_ref[...], axis=1) + skip * grad_ref[rows, cut(b)]
            shifted_grad_ref[rows, cut(b)] = grad_mixed * value_ref[rows, cut(b)]
            value_grad_ref[rows, cut(b)] = grad_mixed * shifted_ref[rows, cut(b)]
            return adjoint

        lax.fori_loop(0, chunks, chunk, incoming[b])

    def halo_copy():
        return seq.remote(
            shifted_grad_ref.at[pl.ds(0, 8)], head_ref, halo_send.at[0], halo_recv.at[0], seq.me - 1
        )

    first, last = seq.place == 0, seq.place == span - 1
    pl.when(jnp.logical_not(first))(lambda: halo_copy().start())
    for j in range(SHIFT):
        put(1 + j, over_tokens(shifted_grad_ref[pl.ds(0, tokens), :] * keys_ref[pl.ds(8 - j, tokens), :]))
    pl.when(y == 1)(lambda: narrow_copies()[3].start())
    put(7, over_tokens(value_grad_ref[...]))
    half_product(up_half_ref, normed_ref, pre_grad_ref.at[y], True)

    @pl.when(last)
    def _():
        head_ref[...] = jnp.zeros_like(head_ref)

    @pl.when(jnp.logical_not(last))
    def _():
        halo_copy().wait_recv()

    shifted_grad_ref[pl.ds(tokens, 8), :] = head_ref[...]
    key_grad = taps_ref[0:1, :] * shifted_grad_ref[pl.ds(0, tokens), :]
    for j in range(1, SHIFT):
        key_grad = key_grad + taps_ref[j : j + 1, :] * shifted_grad_ref[pl.ds(j, tokens), :]
    key_grad_ref[...] = key_grad
    put(6, over_tokens(key_grad))
    pl.when(x == 0)(lambda: narrow_copies()[0].start())
    state_sums()

    cotangent_share.finish()
    normed_share.finish()
    for copy in half_copies():
        copy.wait()
    half_product(down_half_ref, active_peer_ref, cotangent_peer_ref, False)
    half_product(up_half_ref, normed_peer_ref, pre_grad_peer_ref, False)
    wide_shares[0].relay()
    normed1_share.finish()
    wide_shares[0].finish()
    for copy in narrow_copies()[::2]:
        copy.wait()
    for copy in merged_copies + [normed_grad_copy, feed_copy]:
        copy.wait_send()
    seq.drain(blocks, ends_ref, totals_ref, sems)
    pl.when(jnp.logical_not(first))(lambda: halo_copy().wait_send())


def mixer_call(kernel, span, args, outs, scratch, width, collective_id, name, more_sems=(), in_hbm=(), megabytes=16):
    blocks, groups = width // LANES, span // 4
    scratch = [pltpu.VMEM(dims, F32) for dims in scratch]
    scratch += [pltpu.VMEM((4, STATE, width), F32), pltpu.VMEM((groups, STATE, width), F32)]
    sems = [(blocks, 3), (blocks, 3), (blocks, max(1, groups - 1)), (blocks, max(1, groups - 1)), (1,), (1,), *more_sems]
    return pl.pallas_call(
        functools.partial(kernel, span),
        in_specs=[pl.BlockSpec(memory_space=pltpu.HBM if n in in_hbm else pltpu.VMEM) for n in range(len(args))],
        out_specs=[pl.BlockSpec(memory_space=pltpu.VMEM)] * len(outs),
        out_shape=outs,
        scratch_shapes=scratch + [pltpu.SemaphoreType.DMA(dims) for dims in sems],
        compiler_params=pltpu.CompilerParams(
            collective_id=collective_id, has_side_effects=True, vmem_limit_bytes=megabytes * 2**20
        ),
        name=name,
    )(*args)


MESH = pl.DeviceIdType.MESH


def is_far(i):
    return lax.rem(i, 4) == 2


class Plan:
    def __init__(self, feed_rows, mixer_rows, rows):
        self.rows = rows
        self.feed, self.mixer = feed_rows // rows, mixer_rows // 2 // rows
        self.pieces = self.feed + self.mixer + 1
        self.total = self.pieces * rows
        self.feed_rows, self.mixer_rows = feed_rows, mixer_rows


def sum_kernel(
    length, plan, lag,
    up_half_ref, down_half_ref, normed_ref, middle_grad_ref, gated_ref, query_grad_ref, key_grad_ref, value_grad_ref,
    normed_x_ref, narrow_x_ref, wide_y_ref, narrow_y_ref, small_ref, tokens_ref, gain_ref,
    query_hbm, key_hbm, value_hbm,
    out_ref, input_grad_ref,
    sum_ref, got_ref, feed_got_ref, keep_ref, send_ref, mixer_got_ref, small_got_ref, small_sum_ref, weights_ref, local_ref,
    other_ref,
    load_sem, store_sem, chain_send, chain_recv, z_send, z_recv, side_send, side_recv, feed_send, feed_recv,
    mixer_send, mixer_recv, small_send, small_recv, core_send, core_recv
):
    me = lax.axis_index("seq")
    core = lax.axis_index("tp")
    place, quarter = me // 4, lax.rem(me, 4)
    x, y = lax.rem(quarter, 2), quarter // 2
    x_peer, y_peer = me + 1 - 2 * x, me + 2 - 4 * y
    quarter_x, quarter_y, quarter_d = quarter + 1 - 2 * x, quarter + 2 - 4 * y, 3 - quarter
    rows, pieces = plan.rows, plan.pieces
    width = gated_ref.shape[1]
    first = lag * (length - 1)
    started = (place, length - 1 - place)
    ahead = (me + 4, me - 4)
    behind = (me - 4, me + 4)
    side_peers = (x_peer, y_peer)
    side_bits = (x, y)
    halves = (up_half_ref, down_half_ref)
    loads = [
        pltpu.make_async_copy(source, weights_ref.at[n], load_sem.at[n])
        for n, source in enumerate((query_hbm, key_hbm, value_hbm))
    ]
    for load in loads:
        load.start()
    barrier = pltpu.get_barrier_semaphore()

    def greet(peer):
        pl.semaphore_signal(barrier, inc=1, device_id={"seq": peer}, device_id_type=MESH)

    greet(x_peer)
    greet(y_peer)
    pl.semaphore_signal(barrier, inc=1, device_id={"tp": 1 - core}, device_id_type=MESH)
    pl.when(place > 0)(lambda: greet(me - 4))
    pl.when(place < length - 1)(lambda: greet(me + 4))
    pl.semaphore_wait(barrier, 3 + (place > 0).astype(jnp.int32) + (place < length - 1).astype(jnp.int32))

    def remote(source, target, send, recv, peer):
        return pltpu.make_async_remote_copy(
            src_ref=source,
            dst_ref=target,
            send_sem=send,
            recv_sem=recv,
            device_id={"seq": peer},
            device_id_type=MESH,
        )

    def at(i):
        return pl.ds(pl.multiple_of(i * rows, 8), rows)

    def feed_copy(d, i):
        source = pl.ds(pl.multiple_of((1 - side_bits[d]) * plan.feed_rows + i * rows, 8), rows)
        return remote(
            halves[d].at[source], feed_got_ref.at[d, at(i)], feed_send.at[d, i], feed_recv.at[d, i], side_peers[d]
        )

    def send_feed(i, _):
        for d in range(2):
            feed_copy(d, i).start()
        return 0

    lax.fori_loop(0, plan.feed, send_feed, 0)

    def features(ref, h):
        return ref[:, pl.ds(pl.multiple_of(h * width, LANES), width)]

    def query_or_key(h):
        narrow = jnp.where(x == 0, query_grad_ref[...], key_grad_ref[...])
        return dot(features(normed_ref, h), narrow, 0, 0) + dot(features(normed_x_ref, h), narrow_x_ref[...], 0, 0)

    def value_or_out(h):
        left = jnp.where(y == 0, features(normed_ref, h), gated_ref[...])
        right = jnp.where(y == 0, value_grad_ref[...], features(middle_grad_ref, h))
        wide, narrow = features(wide_y_ref, h), narrow_y_ref[...]
        return dot(left, right, 0, 0) + dot(jnp.where(y == 0, wide, narrow), jnp.where(y == 0, narrow, wide), 0, 0)

    mixer_copies = [
        remote(send_ref.at[n], mixer_got_ref.at[n], mixer_send.at[n], mixer_recv.at[n], peer)
        for n, peer in enumerate((y_peer, x_peer))
    ]
    send_ref[0] = query_or_key(1 - y)
    mixer_copies[0].start()
    send_ref[1] = value_or_out(1 - x)
    mixer_copies[1].start()

    def chain_copy(d, i):
        return remote(
            sum_ref.at[d, at(i)], got_ref.at[d, at(i)], chain_send.at[d, i], chain_recv.at[d, i], ahead[d]
        )

    def z_copy(d, i, k):
        ref = out_ref.at[(quarter, quarter_x, quarter_y, quarter_d)[k], d, at(i)]
        return remote(ref, ref, z_send.at[d, i, k], z_recv.at[d, i, k], behind[d])

    def side_copy(d, i, k):
        even = lax.rem(i, 2) == 0
        source = (quarter, quarter, jnp.where(even, quarter_x, quarter_y))[k]
        peer = (x_peer, y_peer, jnp.where(even, y_peer, x_peer))[k]
        ref = out_ref.at[source, d, at(i)]
        return remote(ref, ref, side_send.at[d, i, k], side_recv.at[d, i, k], peer)

    def chain_step(d, i):
        @pl.when(i < plan.feed)
        def _():
            feed_copy(d, i).wait_recv()
            mine = pl.ds(pl.multiple_of(side_bits[d] * plan.feed_rows + i * rows, 8), rows)
            sum_ref[d, at(i)] = halves[d][mine, :] + feed_got_ref[d, at(i)]

        @pl.when(started[d] > 0)
        def _():
            chain_copy(d, i).wait_recv()
            sum_ref[d, at(i)] = sum_ref[d, at(i)] + got_ref[d, at(i)]

        @pl.when(started[d] < length - 1)
        def _():
            chain_copy(d, i).start()

        @pl.when(started[d] == length - 1)
        def _():
            store = pltpu.make_async_copy(sum_ref.at[d, at(i)], out_ref.at[quarter, d, at(i)], store_sem.at[d, i])
            store.start()
            store.wait()

    def kind(d, i):
        remaining = length - 1 - started[d]
        far = is_far(i)
        sideways = jnp.logical_or(jnp.logical_not(far), remaining == 0)
        onward = jnp.logical_and(far, remaining < length - 1)
        return remaining, sideways, onward

    def own_step(d, i):
        remaining, sideways, _ = kind(d, i)

        @pl.when(remaining > 0)
        def _():
            z_copy(d, i, 0).wait_recv()

        @pl.when(remaining < length - 1)
        def _():
            z_copy(d, i, 0).start()

        @pl.when(sideways)
        def _():
            side_copy(d, i, 0).start()
            side_copy(d, i, 1).start()

    def side_step(d, i):
        _, sideways, onward = kind(d, i)

        @pl.when(sideways)
        def _():
            side_copy(d, i, 0).wait_recv()
            side_copy(d, i, 1).wait_recv()
            side_copy(d, i, 2).start()

        @pl.when(jnp.logical_not(sideways))
        def _():
            z_copy(d, i, 1).wait_recv()
            z_copy(d, i, 2).wait_recv()

        @pl.when(onward)
        def _():
            z_copy(d, i, 1).start()
            z_copy(d, i, 2).start()

    def last_step(d, i):
        _, sideways, onward = kind(d, i)

        @pl.when(sideways)
        def _():
            side_copy(d, i, 2).wait_recv()

        @pl.when(jnp.logical_not(sideways))
        def _():
            z_copy(d, i, 3).wait_recv()

        @pl.when(onward)
        def _():
            z_copy(d, i, 3).start()

    def tick(t, _):
        for step, late in ((last_step, first + 2 * lag), (side_step, first + lag), (chain_step, 0), (own_step, first)):
            for d in range(2):
                passed = started[d] if step is chain_step else length - 1 - started[d]
                i = t - late - lag * passed
                pl.when(jnp.logical_and(i >= 0, i < pieces))(functools.partial(step, d, i))
        return 0

    core_copy = pltpu.make_async_remote_copy(
        src_ref=local_ref,
        dst_ref=other_ref,
        send_sem=core_send.at[0],
        recv_sem=core_recv.at[0],
        device_id={"tp": 1 - core},
        device_id_type=MESH,
    )
    small_x = remote(
        small_sum_ref.at[1 - x], small_got_ref.at[pl.ds(0, 2)], small_send.at[0], small_recv.at[0], x_peer
    )
    small_y = remote(
        small_sum_ref.at[x, 1 - y], small_got_ref.at[2], small_send.at[1], small_recv.at[1], y_peer
    )

    def normed_grad():
        for load in loads:
            load.wait()
        local_ref[...] = (
            dot(query_grad_ref[...], weights_ref[0], 1, 1)
            + dot(key_grad_ref[...], weights_ref[1], 1, 1)
            + dot(value_grad_ref[...], weights_ref[2], 1, 1)
        )
        core_copy.start()

    def first_norm():
        core_copy.wait_recv()
        grad = local_ref[...] + other_ref[...]
        values = tokens_ref[...]
        centered = values - over_features(values)
        inverse = lax.rsqrt(over_features(centered * centered) + EPSILON)
        scaled = centered * inverse
        scaled_grad = grad * gain_ref[...]
        scaled_grad = scaled_grad - over_features(scaled_grad) - scaled * over_features(scaled_grad * scaled)
        input_grad_ref[...] = middle_grad_ref[...] + inverse * scaled_grad
        for p in range(4):
            small_sum_ref[p // 2, p % 2] = small_ref[p]
        small_sum_ref[0, 0, pl.ds(STATE // 4, 1), :] = over_tokens(grad * scaled)
        small_sum_ref[0, 0, pl.ds(STATE // 4 + 1, 1), :] = over_tokens(grad)
        small_x.start()

    def keep_mixer():
        keep_ref[0] = query_or_key(y)
        keep_ref[1] = value_or_out(x)

    def add_small():
        small_x.wait()
        small_sum_ref[x] = small_sum_ref[x] + small_got_ref[pl.ds(0, 2)]
        small_y.start()

    def mixer_sums():
        for copy in mixer_copies:
            copy.wait_recv()
        count = plan.mixer_rows // 2
        for d in range(2):
            source, target = pl.ds(d * count, count), pl.ds(plan.feed_rows, count)
            for n in range(2):
                sum_ref[d, target, pl.ds(n * width, width)] = keep_ref[n, source, :] + mixer_got_ref[n, source, :]

    def small_sums():
        small_y.wait()
        last = pl.ds(plan.total - rows, rows)
        sum_ref[0, last, :] = small_sum_ref[x, y] + small_got_ref[2]
        sum_ref[1, last, :] = jnp.zeros_like(sum_ref[1, last, :])

    stages = (
        (2, (normed_grad,)),
        (5, (first_norm,)),
        (8, (keep_mixer, add_small)),
        (plan.feed, (mixer_sums, small_sums)),
    )
    at_tick = 0
    for until, work in stages:
        lax.fori_loop(at_tick, until, tick, 0)
        at_tick = until
        for piece in work:
            piece()
    lax.fori_loop(at_tick, 2 * first + 2 * lag + pieces, tick, 0)

    def drain(i, _):
        for d in range(2):
            remaining, sideways, onward = kind(d, i)
            pl.when(i < plan.feed)(lambda: feed_copy(d, i).wait_send())
            pl.when(remaining > 0)(lambda: chain_copy(d, i).wait_send())
            pl.when(remaining < length - 1)(lambda: z_copy(d, i, 0).wait_send())

            @pl.when(onward)
            def _():
                for k in range(1, 4):
                    z_copy(d, i, k).wait_send()

            @pl.when(sideways)
            def _():
                for k in range(3):
                    side_copy(d, i, k).wait_send()

        return 0

    lax.fori_loop(0, pieces, drain, 0)
    for copy in mixer_copies + [core_copy]:
        copy.wait_send()


def summed_quarters(plan, lag, args, in_hbm, collective_id):
    length = lax.axis_size("seq") // 4
    pieces, feed = plan.pieces, plan.feed
    tokens, columns = args[2].shape
    width = args[4].shape[1]
    sems = [(3,), (2, pieces), (2, pieces), (2, pieces), (2, pieces, 4), (2, pieces, 4), (2, pieces, 3), (2, pieces, 3)]
    sems += [(2, feed), (2, feed), (2,), (2,), (2,), (2,), (1,), (1,)]
    scratch = [(2, plan.total, columns)] * 2 + [(2, plan.feed_rows, columns)] + [(2, plan.mixer_rows, width)] * 3
    scratch += [(3, plan.rows, columns), (2, 2, plan.rows, columns), (3, columns, width)] + [(tokens, columns)] * 2
    return pl.pallas_call(
        functools.partial(sum_kernel, length, plan, lag),
        out_shape=[shape(4, 2, plan.total, columns), shape(tokens, columns)],
        in_specs=[pl.BlockSpec(memory_space=pltpu.HBM if n in in_hbm else pltpu.VMEM) for n in range(len(args))],
        out_specs=[pl.BlockSpec(memory_space=pltpu.HBM), pl.BlockSpec(memory_space=pltpu.VMEM)],
        scratch_shapes=[pltpu.VMEM(dims, F32) for dims in scratch] + [pltpu.SemaphoreType.DMA(dims) for dims in sems],
        compiler_params=pltpu.CompilerParams(
            collective_id=collective_id, has_side_effects=True, vmem_limit_bytes=60 * 2**20
        ),
        name="gradient_sums",
    )(*args)


def unpack_kernel(plan, sums_ref, *refs):
    (
        up_ref, down_ref, query_ref, key_ref, value_ref, out_ref, rate_ref, state_out_ref, wide_ref, narrow_ref, small_ref, sem
    ) = refs
    columns, width = up_ref.shape[0], query_ref.shape[1]
    feed, count, state = plan.feed_rows, plan.mixer_rows // 2, STATE // 4
    copies = []

    def copy(source, target):
        copies.append(pltpu.make_async_copy(source, target, sem.at[len(copies)]))
        copies[-1].start()

    def span(start, size):
        return pl.ds(start, size)

    for x in range(2):
        for y in range(2):
            part = sums_ref.at[2 * y + x]
            copy(part.at[0, span(plan.total - plan.rows, plan.rows)], small_ref.at[2 * x + y])
    for x in range(2):
        for y in range(2):
            part = sums_ref.at[2 * y + x]
            copy(part.at[0, span(0, feed)], up_ref.at[span(x * feed, feed), span(y * columns, columns)])
            copy(part.at[1, span(0, feed)], down_ref.at[span((2 * x + y) * feed, feed)])
            for d in range(2):
                mixer = part.at[d, span(feed, count)]
                target = (query_ref, key_ref)[x]
                copy(mixer.at[:, span(0, width)], target.at[span((2 * y + d) * count, count)])
                if y == 0:
                    target = value_ref.at[span((2 * x + d) * count, count)]
                else:
                    target = out_ref.at[span(d * count, count), span(x * width, width)]
                copy(mixer.at[:, span(width, width)], target)
            rows = span((2 * x + y) * state, state)
            last = part.at[0, span(plan.total - plan.rows, state)]
            copy(last.at[:, span(0, width)], rate_ref.at[rows])
            copy(last.at[:, span(width, width)], state_out_ref.at[rows])
    for n in range(4):
        copies[n].wait()
    wide_ref[...] = small_ref[0, pl.ds(state, 8), :]
    narrow_ref[...] = small_ref[1, pl.ds(state, 8), :]
    for item in copies[4:]:
        item.wait()


def unpacked(plan, sums, outs):
    columns = sums.shape[-1]
    outs = outs + [shape(8, columns)] * 2
    return pl.pallas_call(
        functools.partial(unpack_kernel, plan),
        out_shape=outs,
        in_specs=[pl.BlockSpec(memory_space=pl.ANY)],
        out_specs=[pl.BlockSpec(memory_space=pltpu.HBM)] * (len(outs) - 2) + [pl.BlockSpec(memory_space=pltpu.VMEM)] * 2,
        scratch_shapes=[pltpu.VMEM((4, plan.rows, columns), F32), pltpu.SemaphoreType.DMA((64,))],
        compiler_params=pltpu.CompilerParams(vmem_limit_bytes=16 * 2**20),
        name="unpack",
    )(sums)


def matmul(left, right):
    return jnp.dot(left, right, precision=PRECISION, preferred_element_type=F32)


def layer_norm(values, gain, bias):
    centered = values - jnp.mean(values, axis=-1, keepdims=True)
    spread = jnp.mean(centered * centered, axis=-1, keepdims=True)
    return centered * lax.rsqrt(spread + EPSILON) * gain + bias


def decay_terms(log_step, state_rate):
    decay_rate = jnp.exp(log_step)[None, :] * state_rate
    return (jnp.exp(-decay_rate), jnp.sqrt(-jnp.expm1(-2.0 * decay_rate)))


def on_device(
    tokens,
    cotangent,
    norm1_gain,
    norm1_bias,
    query_weight,
    query_bias,
    key_weight,
    key_bias,
    value_weight,
    value_bias,
    shift_kernel,
    log_step,
    state_rate,
    state_out,
    skip_gain,
    out_weight,
    out_bias,
    norm2_gain,
    norm2_bias,
    up_weight,
    up_bias,
    down_weight,
    down_bias,
):
    tok_rows = tokens.shape[0]
    width_local = query_weight.shape[1]
    span = lax.axis_size("seq") // SEQS
    chunks = tok_rows // CHUNK
    normed = layer_norm(tokens, norm1_gain, norm1_bias)
    queries = matmul(normed, query_weight) + query_bias
    key_rows = matmul(normed, key_weight) + key_bias
    value_rows = matmul(normed, value_weight) + value_bias
    decay_rate = jnp.exp(log_step)[None, :] * state_rate
    decay_factor, in_coef = decay_terms(log_step, state_rate)
    device_decay = jnp.exp(-decay_rate * tok_rows)
    out_coef = in_coef * state_out
    skip_row = skip_gain[None, :]
    tok_shape, state_shape = shape(tok_rows, width_local), shape(STATE, width_local)
    gated, ssm_out, mixed, shifted, starts, halo = mixer_call(
        mixer_kernel,
        span,
        (queries, key_rows, value_rows, shift_kernel, skip_row, decay_factor, out_coef, device_decay),
        [tok_shape] * 4 + [shape(chunks, STATE, width_local), shape(8, width_local)],
        [(tok_rows + 8, width_local), (width_local // LANES, tok_rows, LANES), (CHUNK, 8, LANES)],
        width_local,
        1,
        "mixer",
    )
    hidden, columns = up_weight.shape[1], tokens.shape[1]
    plan = Plan(columns // 2, width_local, PIECE_ROWS)
    wide_shape = shape(*tokens.shape)
    (
        block_out,
        grad_middle,
        grad_queries,
        grad_keys,
        grad_values,
        small,
        down_half,
        up_half,
        normed_x,
        narrow_x,
        wide_y,
        narrow_y,
    ) = mixer_call(
        layer_kernel,
        span,
        (gated, tokens, cotangent, out_weight, out_bias[None], norm2_gain[None], norm2_bias[None], up_weight)
        + (up_bias[None], down_weight, down_bias[None], queries, key_rows, value_rows, halo, ssm_out, mixed, shifted)
        + (starts, shift_kernel, skip_row, decay_factor, out_coef, device_decay)
        + (normed, in_coef, decay_factor * decay_factor / in_coef * state_out, decay_rate, jnp.exp(log_step)[None]),
        [wide_shape] * 2
        + [tok_shape] * 3
        + [shape(4, PIECE_ROWS, columns)]
        + [shape(hidden // 2, columns), shape(columns, hidden // 2)]
        + [wide_shape, tok_shape, wide_shape, tok_shape],
        [up_weight.shape, down_weight.shape, (2, tok_rows, hidden // 2), (2, tok_rows, hidden // 2)]
        + [tokens.shape] * 9
        + [(tok_rows, hidden // 2)] * 2
        + [tokens.shape] * 2
        + [(tok_rows, width_local)] * 2
        + [(width_local // LANES, tok_rows, LANES)] * 2
        + [(tok_rows + 8, width_local), (tok_rows + 8, width_local), (8, width_local)]
        + [(CHUNK, 8, LANES), (CHUNK, STATE, LANES)]
        + [(STATE, width_local)] * 2,
        width_local,
        2,
        "layer",
        [(2,), (4,), (4,), (4,), (4,), (4, 2), (4, 2)],
        (7, 9),
        60,
    )
    sums, input_grad = summed_quarters(
        plan,
        LAG,
        (up_half, down_half, normed, grad_middle, gated, grad_queries, grad_keys, grad_values, normed_x, narrow_x)
        + (wide_y, narrow_y, small, tokens, norm1_gain[None], query_weight, key_weight, value_weight),
        (15, 16, 17),
        3,
    )
    weights = (up_weight, down_weight, query_weight, key_weight, value_weight, out_weight, state_rate, state_out)
    (
        grad_up_weight,
        grad_down_weight,
        grad_query_weight,
        grad_key_weight,
        grad_value_weight,
        grad_out_weight,
        grad_state_rate,
        grad_state_out,
        wide,
        narrow,
    ) = unpacked(plan, sums, [shape(*weight.shape) for weight in weights])
    grad_norm1_gain, grad_norm1_bias, grad_norm2_gain, grad_norm2_bias, grad_out_bias, grad_down_bias = (
        wide[k] for k in range(6)
    )
    grad_up_bias = wide[6:8].reshape(-1)
    narrow = narrow.reshape(-1, width_local)
    grad_skip_gain, grad_shift_kernel, grad_log_step = narrow[0], narrow[1:5], narrow[8]
    grad_query_bias, grad_key_bias, grad_value_bias = narrow[5], narrow[6], narrow[7]
    return (
        block_out,
        input_grad,
        grad_norm1_gain,
        grad_norm1_bias,
        grad_query_weight,
        grad_query_bias,
        grad_key_weight,
        grad_key_bias,
        grad_value_weight,
        grad_value_bias,
        grad_shift_kernel,
        grad_log_step,
        grad_state_rate,
        grad_state_out,
        grad_skip_gain,
        grad_out_weight,
        grad_out_bias,
        grad_norm2_gain,
        grad_norm2_bias,
        grad_up_weight,
        grad_up_bias,
        grad_down_weight,
        grad_down_bias,
    )


def solution(mesh):
    return jax.shard_map(
        on_device,
        mesh=mesh,
        in_specs=(
            P("seq", None),
            P("seq", None),
            P(),
            P(),
            P(None, "tp"),
            P("tp"),
            P(None, "tp"),
            P("tp"),
            P(None, "tp"),
            P("tp"),
            P(None, "tp"),
            P("tp"),
            P(None, "tp"),
            P(None, "tp"),
            P("tp"),
            P("tp", None),
            P(),
            P(),
            P(),
            P(None, "tp"),
            P("tp"),
            P("tp", None),
            P(),
        ),
        out_specs=(
            P("seq", None),
            P("seq", None),
            P(),
            P(),
            P(None, "tp"),
            P("tp"),
            P(None, "tp"),
            P("tp"),
            P(None, "tp"),
            P("tp"),
            P(None, "tp"),
            P("tp"),
            P(None, "tp"),
            P(None, "tp"),
            P("tp"),
            P("tp", None),
            P(),
            P(),
            P(),
            P(None, "tp"),
            P("tp"),
            P("tp", None),
            P(),
        ),
        check_vma=False,
    )
```

```python
import functools
import types

import jax
import jax.numpy as jnp
from jax import lax
from jax.experimental import pallas as pl
from jax.experimental.pallas import tpu as pltpu
from jax.sharding import PartitionSpec as P

SHIFT = 4
SEQS = 2
STATE = 64
LANES = 128
CHUNK = 32
PIECE_ROWS = 24
LAG = 2
SPREAD = 3
WINDOW = 3
GELU_SCALE = (2.0 / 3.141592653589793) ** 0.5

EPSILON = 1e-05
F32 = jnp.float32
PRECISION = lax.Precision.HIGH


def shape(*dims):
    return jax.ShapeDtypeStruct(dims, F32)


def fold_states(values):
    return jnp.sum(values.reshape(STATE // 8, 8, LANES), axis=0)


def cut(block):
    return pl.ds(block * LANES, LANES)


class Sequence:
    def __init__(self, span, backward):
        self.me = lax.axis_index("seq")
        self.span = span
        self.place = lax.rem(self.me, span)
        self.start = self.me - self.place
        self.groups = span // 4
        self.quarter, self.group = lax.rem(self.place, 4), self.place // 4
        if backward:
            self.rank, self.turn = 3 - self.quarter, self.groups - 1 - self.group
        else:
            self.rank, self.turn = self.quarter, self.group
        self.backward = backward

    def greet(self, other_core):
        barrier = pltpu.get_barrier_semaphore()
        for k in range(1, self.span):
            peer = self.start + lax.rem(self.place + k, self.span)
            pl.semaphore_signal(barrier, inc=1, device_id={"seq": peer}, device_id_type=pl.DeviceIdType.MESH)
        pl.semaphore_signal(barrier, inc=1, device_id={"tp": other_core}, device_id_type=pl.DeviceIdType.MESH)

    def greeted(self):
        pl.semaphore_wait(pltpu.get_barrier_semaphore(), self.span)

    def remote(self, source, target, send, recv, peer, core=None):
        return pltpu.make_async_remote_copy(
            src_ref=source,
            dst_ref=target,
            send_sem=send,
            recv_sem=recv,
            device_id={"seq": peer} if core is None else {"tp": core},
            device_id_type=pl.DeviceIdType.MESH,
        )

    def end_copy(self, b, k, ends_ref, sems):
        other = lax.rem(self.quarter + k, 4)
        peer = self.me - self.quarter + other
        ref = ends_ref.at[self.rank, :, cut(b)]
        return self.remote(ref, ref, sems[0].at[b, k - 1], sems[1].at[b, k - 1], peer)

    def total_copy(self, b, k, totals_ref, sems):
        peer = self.me - 4 * k if self.backward else self.me + 4 * k
        ref = totals_ref.at[self.turn, :, cut(b)]
        return self.remote(ref, ref, sems[2].at[b, k - 1], sems[3].at[b, k - 1], peer)

    def send_end(self, b, end, ends_ref, sems):
        ends_ref[self.rank, :, cut(b)] = end
        for k in range(1, 4):
            self.end_copy(b, k, ends_ref, sems).start()

    def group_total(self, b, decay, ends_ref, totals_ref, sems):
        for k in range(1, 4):
            self.end_copy(b, k, ends_ref, sems).wait_recv()
        before = jnp.zeros_like(decay)
        total = ends_ref[0, :, cut(b)]
        for r in range(3):
            before = jnp.where(self.rank > r, before * decay + ends_ref[r, :, cut(b)], before)
            total = total * decay + ends_ref[r + 1, :, cut(b)]
        if self.groups > 1:
            totals_ref[self.turn, :, cut(b)] = total
            for k in range(1, self.groups):
                pl.when(self.turn + k < self.groups)(lambda: self.total_copy(b, k, totals_ref, sems).start())
        return before

    def carried(self, b, decay, before, totals_ref, sems):
        if self.groups == 1:
            return before
        square = decay * decay
        fourth = square * square
        carry = jnp.zeros_like(decay)
        for h in range(self.groups - 1):
            for k in range(1, self.groups - h):
                pl.when(self.turn == h + k)(lambda: self.total_copy(b, k, totals_ref, sems).wait_recv())
        for h in range(self.groups - 1):
            carry = jnp.where(self.turn > h, carry * fourth + totals_ref[h, :, cut(b)], carry)
        for r in range(3):
            carry = jnp.where(self.rank > r, carry * decay, carry)
        return before + carry

    def drain(self, blocks, ends_ref, totals_ref, sems):
        for b in range(blocks):
            for k in range(1, 4):
                self.end_copy(b, k, ends_ref, sems).wait_send()
            for k in range(1, self.groups):
                pl.when(self.turn + k < self.groups)(lambda: self.total_copy(b, k, totals_ref, sems).wait_send())


def dot(left, right, left_axis, right_axis):
    return lax.dot_general(
        left, right, (((left_axis,), (right_axis,)), ((), ())), precision=PRECISION, preferred_element_type=F32
    )


def over_tokens(values):
    return jnp.sum(values, axis=0, keepdims=True)


def over_features(values):
    return jnp.mean(values, axis=1, keepdims=True)


class Share:
    def __init__(self, seq, source_ref, target_ref, send, recv, peer, core, other_core):
        self.source_ref, self.target_ref, self.send, self.recv = source_ref, target_ref, send, recv
        self.seq, self.peer, self.core, self.other_core = seq, peer, core, other_core
        size = source_ref.shape[0] // 2
        self.mine = pl.ds(pl.multiple_of(core * size, 8), size)

    def across(self):
        return self.seq.remote(
            self.source_ref.at[self.mine], self.target_ref.at[self.mine], self.send.at[0], self.recv.at[0], self.peer
        )

    def between(self):
        ref = self.target_ref.at[self.mine]
        return self.seq.remote(ref, ref, self.send.at[1], self.recv.at[1], self.seq.me, self.other_core)

    def relay(self):
        self.across().wait_recv()
        self.between().start()

    def finish(self):
        self.between().wait_recv()
        self.across().wait_send()
        self.between().wait_send()


def one_less_exp(values):
    series = jnp.ones_like(values)
    for k in range(8, 1, -1):
        series = 1.0 - values * series * (1.0 / k)
    return jnp.where(values < 0.25, values * series, 1.0 - jnp.exp(-values))


def front_kernel(names, span, *refs):
    r = types.SimpleNamespace(**dict(zip(names, refs)))
    tokens, width = r.gated.shape
    hidden_half = r.up.shape[1] // 2
    blocks, chunks, top = width // LANES, tokens // CHUNK, tokens // 2
    ahead, back = Sequence(span, False), Sequence(span, True)
    ahead_sems = (r.end_send, r.end_recv, r.total_send, r.total_recv)
    back_sems = (r.back_end_send, r.back_end_recv, r.back_total_send, r.back_total_recv)
    me, remote = ahead.me, ahead.remote
    x, y = lax.rem(me, 2), lax.rem(me // 2, 2)
    x_peer, y_peer = me + 1 - 2 * x, me + 2 - 4 * y
    core = lax.axis_index("tp")
    other_core = 1 - core
    first, last = ahead.place == 0, ahead.place == span - 1

    pairs = (
        (r.tokens_hbm, r.tokens),
        (r.key_hbm, r.key_weight),
        (r.value_hbm, r.value_weight),
        (r.query_hbm, r.query_weight),
        (r.cotangent_hbm, r.cotangent),
        (r.down_hbm, r.down),
        (r.out_hbm, r.out_weight),
        (r.up_hbm, r.up),
    )
    loads = [pltpu.make_async_copy(source, target, r.load_sem.at[n]) for n, (source, target) in enumerate(pairs)]
    for load in loads:
        load.start()
    ahead.greet(other_core)
    vectors = (r.norm1_gain, r.norm1_bias, r.out_bias, r.norm2_gain, r.norm2_bias, r.down_bias)
    for k, vector in enumerate(vectors):
        r.wide[k : k + 1, :] = vector[...].reshape(1, -1)
    for k in range(2):
        r.wide[6 + k : 7 + k, :] = r.up_bias[pl.ds(k * hidden_half, hidden_half)].reshape(1, -1)
    for k, vector in enumerate((r.query_bias, r.key_bias, r.value_bias, r.skip_gain)):
        r.narrow[k : k + 1, :] = vector[...].reshape(1, -1)
    step = jnp.exp(r.log_step[...].reshape(1, -1))
    r.narrow[4:5, :] = step
    r.narrow[5 : 5 + SHIFT, :] = r.taps[...]
    rate = step * r.state_rate[...]
    decay = jnp.exp(-rate)
    in_coef = jnp.sqrt(one_less_exp(2.0 * rate))
    out_coef = in_coef * r.state_out[...]
    r.rate[...] = rate
    r.decay[...] = decay
    r.in_coef[...] = in_coef
    r.out_coef[...] = out_coef
    r.device_decay[...] = jnp.exp(-rate * tokens)
    r.coef_rate[...] = decay * decay / in_coef * r.state_out[...]
    stores = []

    def store(source, target):
        stores.append(pltpu.make_async_copy(source, target, r.store_sem.at[len(stores)]))
        stores[-1].start()

    def wide(k):
        return r.wide[k : k + 1, :]

    def narrow(k):
        return r.narrow[k : k + 1, :]

    def tap(j):
        return narrow(5 + j)

    def features(b):
        return slice(b * LANES, (b + 1) * LANES)

    loads[0].wait()
    values = r.tokens[...]
    centered = values - over_features(values)
    normed = centered * lax.rsqrt(over_features(centered * centered) + EPSILON) * wide(0) + wide(1)
    r.normed1[...] = normed
    store(r.normed1, r.normed1_hbm)
    loads[1].wait()
    r.keys[pl.ds(8, tokens), :] = dot(r.normed1[...], r.key_weight[...], 1, 0) + narrow(1)
    ahead.greeted()

    def halo_copy():
        return remote(
            r.keys.at[pl.ds(tokens, 8)], r.keys.at[pl.ds(0, 8)], r.halo_send.at[0], r.halo_recv.at[0], me + 1
        )

    @pl.when(jnp.logical_not(last))
    def _():
        halo_copy().start()

    loads[2].wait()
    r.value[...] = dot(r.normed1[...], r.value_weight[...], 1, 0) + narrow(2)

    def mix(start, count):
        total = tap(0) * r.keys[pl.ds(8 + start, count), :]
        for j in range(1, SHIFT):
            total = total + tap(j) * r.keys[pl.ds(8 + start - j, count), :]
        r.shifted[pl.ds(start, count), :] = total
        mixed = total * r.value[pl.ds(start, count), :]
        r.mixed[pl.ds(start, count), :] = mixed
        for b in range(blocks):
            r.rows[b, pl.ds(start, count), :] = mixed[:, features(b)]

    mix(8, tokens - 8)

    @pl.when(first)
    def _():
        r.keys[pl.ds(0, 8), :] = jnp.zeros((8, width), F32)

    @pl.when(jnp.logical_not(first))
    def _():
        halo_copy().wait_recv()

    mix(0, 8)

    for b in range(blocks):
        decay, out_coef = r.decay[:, cut(b)], r.out_coef[:, cut(b)]

        def scan(k, state, b=b, decay=decay, out_coef=out_coef):
            r.starts[k, :, cut(b)] = state
            base = pl.multiple_of(k * CHUNK, CHUNK)
            for j in range(CHUNK):
                state = decay * state + r.rows[b, pl.ds(base + j, 1), :]
                r.part[j] = fold_states(out_coef * state)
            r.out[pl.ds(base, CHUNK), cut(b)] = jnp.sum(r.part[...], axis=1)
            return state

        ahead.send_end(b, lax.fori_loop(0, chunks, scan, jnp.zeros_like(decay)), r.ends, ahead_sems)
    loads[3].wait()
    r.query[...] = dot(r.normed1[...], r.query_weight[...], 1, 0) + narrow(0)
    befores = [ahead.group_total(b, r.device_decay[:, cut(b)], r.ends, r.totals, ahead_sems) for b in range(blocks)]
    loads[4].wait()
    loads[5].wait()
    for n in range(2):
        r.pre_grad[n] = dot(r.cotangent[...], r.down[pl.ds(n * hidden_half, hidden_half), :], 1, 1)
    incoming = [
        ahead.carried(b, r.device_decay[:, cut(b)], befores[b], r.totals, ahead_sems) for b in range(blocks)
    ]

    cotangent_share = Share(
        ahead, r.cotangent, r.cotangent_peer, r.share_send.at[0], r.share_recv.at[0], x_peer, core, other_core
    )
    normed2_share = Share(
        ahead, r.normed2, r.normed2_peer, r.share_send.at[1], r.share_recv.at[1], y_peer, core, other_core
    )
    normed1_share = Share(
        ahead, r.normed1, r.normed1_x, r.share_send.at[2], r.share_recv.at[2], x_peer, core, other_core
    )
    wide_shares = [
        Share(ahead, source, r.wide_y, r.share_send.at[3], r.share_recv.at[3], y_peer, core, other_core)
        for source in (r.middle_grad, r.normed1)
    ]

    def narrow_copy(source, n, target, peer):
        return remote(source, target, r.half_send.at[n], r.half_recv.at[n], peer)

    def key_copy():
        return narrow_copy(r.key_grad, 2, r.narrow_x, x_peer)

    def query_copy():
        return narrow_copy(r.query_grad, 2, r.narrow_x, x_peer)

    def gated_copy():
        return narrow_copy(r.gated, 3, r.narrow_y, y_peer)

    def value_copy():
        return narrow_copy(r.value_grad, 3, r.narrow_y, y_peer)

    cotangent_share.across().start()

    @pl.when(y == 1)
    def _():
        wide_shares[1].across().start()

    for b in range(blocks):
        decay, out_coef = r.decay[:, cut(b)], r.out_coef[:, cut(b)]
        skip = narrow(3)[:, features(b)]

        def carry(k, state, b=b, decay=decay, out_coef=out_coef, skip=skip):
            r.starts[k, :, cut(b)] = r.starts[k, :, cut(b)] + state
            base = pl.multiple_of(k * CHUNK, CHUNK)
            for j in range(CHUNK):
                state = decay * state
                r.part[j] = fold_states(out_coef * state)
            rows = pl.ds(base, CHUNK)
            out = r.out[rows, cut(b)] + jnp.sum(r.part[...], axis=1) + skip * r.mixed[rows, cut(b)]
            r.out[rows, cut(b)] = out
            r.gated[rows, cut(b)] = r.query[rows, cut(b)] * out
            return state

        lax.fori_loop(0, chunks, carry, incoming[b])
    store(r.gated, r.gated_hbm)

    def core_copy(n, source, target):
        return remote(source, target, r.core_send.at[n], r.core_recv.at[n], me, other_core)

    loads[6].wait()
    merged_copies = []
    for n in range(2):
        rows = pl.ds(n * top, top)
        r.merged[rows, :] = dot(r.gated[rows, :], r.out_weight[...], 1, 0)
        copy = core_copy(n, r.merged.at[rows], r.merged_other.at[rows])
        copy.start()
        merged_copies.append(copy)

    @pl.when(y == 0)
    def _():
        gated_copy().start()

    normed1_share.across().start()
    small_start = STATE // 4
    r.small[...] = jnp.zeros_like(r.small)

    def put(k, row):
        r.small[1, pl.ds(small_start + k // 2, 1), pl.ds(k % 2 * width, width)] = row

    spreads = []
    for n, copy in enumerate(merged_copies):
        rows = pl.ds(n * top, top)
        copy.wait_recv()
        middle = r.tokens[rows, :] + (r.merged[rows, :] + r.merged_other[rows, :]) + wide(2)
        centered = middle - over_features(middle)
        inverse = lax.rsqrt(over_features(centered * centered) + EPSILON)
        scaled = centered * inverse
        r.middle[rows, :] = middle
        r.scaled[rows, :] = scaled
        r.normed2[rows, :] = scaled * wide(3) + wide(4)
        spreads.append(inverse)
    normed2_share.across().start()

    loads[7].wait()
    for n in range(2):
        part = pl.ds(n * hidden_half, hidden_half)
        pre = dot(r.normed2[...], r.up[:, part], 1, 0) + wide(6 + n)
        square = pre * pre
        curve = jnp.tanh(GELU_SCALE * (pre + 0.044715 * (square * pre)))
        r.active[n] = 0.5 * pre * (1.0 + curve)
        slope = 0.5 * (1.0 + curve) + 0.5 * pre * (1.0 - curve * curve) * (
            GELU_SCALE * (1.0 + 3 * 0.044715 * square)
        )
        pre_grad = r.pre_grad[n] * slope
        r.pre_grad[n] = pre_grad
        r.small[0, pl.ds(small_start + 6 + n, 1), :] = over_tokens(pre_grad)
        normed_grad = dot(pre_grad, r.up[:, part], 1, 1)
        if n == 0:
            r.normed_grad[...] = normed_grad
        else:
            r.normed_grad[...] = r.normed_grad[...] + normed_grad
    normed_grad_copy = core_copy(2, r.normed_grad, r.normed_grad_other)
    normed_grad_copy.start()
    for n in range(2):
        feed = dot(r.active[n], r.down[pl.ds(n * hidden_half, hidden_half), :], 1, 0)
        if n == 0:
            r.feed[...] = feed
        else:
            r.feed[...] = r.feed[...] + feed
    feed_copy = core_copy(3, r.feed, r.feed_other)
    feed_copy.start()
    normed_grad_copy.wait_recv()
    for n in range(2):
        rows = pl.ds(n * top, top)
        normed_grad = r.normed_grad[rows, :] + r.normed_grad_other[rows, :]
        scaled = r.scaled[rows, :]
        scaled_grad = normed_grad * wide(3)
        centered = scaled_grad - over_features(scaled_grad) - scaled * over_features(scaled_grad * scaled)
        middle_grad = r.cotangent[rows, :] + spreads[n] * centered
        r.middle_grad[rows, :] = middle_grad
        sums = (normed_grad * scaled, normed_grad, middle_grad, r.cotangent[rows, :])
        for k, values in enumerate(sums):
            row = pl.ds(small_start + 2 + k, 1)
            if n == 0:
                r.small[0, row, :] = over_tokens(values)
            else:
                r.small[0, row, :] = r.small[0, row, :] + over_tokens(values)
        r.gated_grad[rows, :] = dot(middle_grad, r.out_weight[...], 1, 1)
    store(r.middle_grad, r.middle_grad_hbm)

    grad = r.gated_grad[...] * r.query[...]
    r.grad[...] = grad
    for b in range(blocks):
        r.grad_rows[b] = grad[:, features(b)]
    for b in range(blocks):
        decay = r.decay[:, cut(b)]

        def end(i, adjoint, b=b, decay=decay):
            base = pl.multiple_of((chunks - 1 - i) * CHUNK, CHUNK)
            for j in range(CHUNK - 1, -1, -1):
                adjoint = decay * adjoint + r.grad_rows[b, pl.ds(base + j, 1), :]
            return adjoint

        back.send_end(b, lax.fori_loop(0, chunks, end, jnp.zeros_like(decay)), r.back_ends, back_sems)
    query_grad = r.gated_grad[...] * r.out[...]
    r.query_grad[...] = query_grad
    store(r.query_grad, r.query_grad_hbm)
    put(0, over_tokens(r.grad[...] * r.mixed[...]))
    put(5, over_tokens(query_grad))
    cotangent_share.relay()
    normed1_share.relay()
    normed2_share.relay()
    feed_copy.wait_recv()
    r.block_out[...] = r.middle[...] + (r.feed[...] + r.feed_other[...]) + wide(5)
    store(r.block_out, r.block_out_hbm)
    befores = [
        back.group_total(b, r.device_decay[:, cut(b)], r.back_ends, r.back_totals, back_sems) for b in range(blocks)
    ]

    def product(left_ref, right_ref):
        return dot(left_ref[...], right_ref[...], 0, 0)

    r.down_half[...] = product(r.active.at[x], r.cotangent)
    incoming = [
        back.carried(b, r.device_decay[:, cut(b)], befores[b], r.back_totals, back_sems) for b in range(blocks)
    ]

    def half_copies():
        return (
            remote(r.active.at[1 - x], r.active_peer, r.half_send.at[0], r.half_recv.at[0], x_peer),
            remote(r.pre_grad.at[1 - y], r.pre_grad_peer, r.half_send.at[1], r.half_recv.at[1], y_peer),
        )

    for copy in half_copies():
        copy.start()

    @pl.when(y == 0)
    def _():
        wide_shares[0].across().start()

    @pl.when(x == 1)
    def _():
        query_copy().start()

    for b in range(blocks):
        decay, out_coef = r.decay[:, cut(b)], r.out_coef[:, cut(b)]
        skip = narrow(3)[:, features(b)]
        r.coef[:, cut(b)] = jnp.zeros_like(decay)
        r.slope[:, cut(b)] = jnp.zeros_like(decay)

        def chunk(i, adjoint, b=b, decay=decay, out_coef=out_coef, skip=skip):
            k = chunks - 1 - i
            base = pl.multiple_of(k * CHUNK, CHUNK)
            state = r.starts[k, :, cut(b)]
            for j in range(CHUNK):
                r.state[j] = state
                state = decay * state + r.rows[b, pl.ds(base + j, 1), :]
            coef, slope = r.coef[:, cut(b)], r.slope[:, cut(b)]
            for j in range(CHUNK - 1, -1, -1):
                adjoint = decay * adjoint + r.grad_rows[b, pl.ds(base + j, 1), :]
                r.part[j] = fold_states(out_coef * adjoint)
                coef = coef + adjoint * r.rows[b, pl.ds(base + j, 1), :]
                slope = slope + adjoint * r.state[j]
            r.coef[:, cut(b)] = coef
            r.slope[:, cut(b)] = slope
            rows = pl.ds(base, CHUNK)
            grad_mixed = jnp.sum(r.part[...], axis=1) + skip * r.grad[rows, cut(b)]
            r.shifted_grad[rows, cut(b)] = grad_mixed * r.value[rows, cut(b)]
            r.value_grad[rows, cut(b)] = grad_mixed * r.shifted[rows, cut(b)]
            return adjoint

        lax.fori_loop(0, chunks, chunk, incoming[b])
    store(r.value_grad, r.value_grad_hbm)

    def head_copy():
        return remote(
            r.shifted_grad.at[pl.ds(0, 8)], r.shifted_grad.at[pl.ds(tokens, 8)], r.halo_send.at[1], r.halo_recv.at[1], me - 1
        )

    @pl.when(jnp.logical_not(first))
    def _():
        head_copy().start()

    @pl.when(y == 1)
    def _():
        value_copy().start()

    for j in range(SHIFT):
        put(1 + j, over_tokens(r.shifted_grad[pl.ds(0, tokens), :] * r.keys[pl.ds(8 - j, tokens), :]))
    put(7, over_tokens(r.value_grad[...]))
    r.up_half[...] = product(r.normed2, r.pre_grad.at[y])

    @pl.when(last)
    def _():
        r.shifted_grad[pl.ds(tokens, 8), :] = jnp.zeros((8, width), F32)

    @pl.when(jnp.logical_not(last))
    def _():
        head_copy().wait_recv()

    key_grad = tap(0) * r.shifted_grad[pl.ds(0, tokens), :]
    for j in range(1, SHIFT):
        key_grad = key_grad + tap(j) * r.shifted_grad[pl.ds(j, tokens), :]
    r.key_grad[...] = key_grad
    store(r.key_grad, r.key_grad_hbm)

    @pl.when(x == 0)
    def _():
        key_copy().start()

    put(6, over_tokens(key_grad))

    for p in range(4):
        rows = pl.ds(p * small_start, small_start)
        coef = r.coef[rows, :]
        rate_grad = r.coef_rate[rows, :] * coef - r.decay[rows, :] * r.out_coef[rows, :] * r.slope[rows, :]
        step_grad = over_tokens(r.rate[rows, :] * rate_grad)
        put(8, step_grad if p == 0 else r.small[1, pl.ds(small_start + 4, 1), pl.ds(0, width)] + step_grad)
        r.small[p, pl.ds(0, small_start), pl.ds(0, width)] = narrow(4) * rate_grad
        r.small[p, pl.ds(0, small_start), pl.ds(width, width)] = r.in_coef[rows, :] * coef
    store(r.small, r.small_hbm)
    wide_shares[0].relay()

    cotangent_share.finish()
    normed2_share.finish()
    halves = half_copies()
    halves[0].wait()
    r.down_half[...] = r.down_half[...] + product(r.active_peer, r.cotangent_peer)
    store(r.down_half, r.down_half_hbm)
    halves[1].wait()
    r.up_half[...] = r.up_half[...] + product(r.normed2_peer, r.pre_grad_peer)
    store(r.up_half, r.up_half_hbm)
    normed1_share.finish()
    wide_shares[0].finish()
    key_copy().wait()
    gated_copy().wait()
    for copy in merged_copies + [normed_grad_copy, feed_copy]:
        copy.wait_send()
    ahead.drain(blocks, r.ends, r.totals, ahead_sems)
    back.drain(blocks, r.back_ends, r.back_totals, back_sems)

    @pl.when(jnp.logical_not(last))
    def _():
        halo_copy().wait_send()

    @pl.when(jnp.logical_not(first))
    def _():
        head_copy().wait_send()

    for copy in stores:
        copy.wait()


def front_call(span, inputs, in_hbm, outs, scratch, sems):
    names = [*inputs, *in_hbm, *outs, *scratch, *sems]
    results = pl.pallas_call(
        functools.partial(front_kernel, names, span),
        in_specs=[pl.BlockSpec(memory_space=pltpu.VMEM)] * len(inputs)
        + [pl.BlockSpec(memory_space=pltpu.HBM)] * len(in_hbm),
        out_specs=[pl.BlockSpec(memory_space=pltpu.HBM)] * len(outs),
        out_shape=[shape(*dims) for dims in outs.values()],
        scratch_shapes=[pltpu.VMEM(dims, F32) for dims in scratch.values()]
        + [pltpu.SemaphoreType.DMA(dims) for dims in sems.values()],
        compiler_params=pltpu.CompilerParams(collective_id=1, has_side_effects=True, vmem_limit_bytes=60 * 2**20),
        name="front",
    )(*inputs.values(), *in_hbm.values())
    return types.SimpleNamespace(**dict(zip(outs, results)))


MESH = pl.DeviceIdType.MESH


def is_far(i):
    return lax.rem(i, 5) == 2


class Plan:
    def __init__(self, feed_rows, mixer_rows, rows):
        self.rows = rows
        self.feed, self.mixer = feed_rows // rows, mixer_rows // 2 // rows
        self.small_rows = STATE // 4 + 8
        self.pieces = self.feed + self.mixer + -(-self.small_rows // rows)
        self.total = self.pieces * rows
        self.feed_rows, self.mixer_rows = feed_rows, mixer_rows


def sum_kernel(
    length, plan, lag,
    small_ref, gain_ref, up_half_ref, down_half_ref, normed_hbm, middle_grad_hbm, gated_hbm, query_grad_hbm, key_grad_hbm,
    value_grad_hbm, normed_x_hbm, narrow_x_hbm, wide_y_hbm, narrow_y_hbm, tokens_hbm, query_hbm, key_hbm, value_hbm,
    out_ref, input_grad_ref,
    normed_ref, middle_grad_ref, gated_ref, query_grad_ref, key_grad_ref, value_grad_ref,
    normed_x_ref, narrow_x_ref, wide_y_ref, narrow_y_ref, tokens_ref,
    sum_ref, got_ref, feed_got_ref, keep_ref, send_ref, mixer_got_ref, small_got_ref, small_sum_ref, weights_ref, local_ref,
    other_ref,
    load_sem, store_sem, chain_send, chain_recv, z_send, z_recv, side_send, side_recv, feed_send, feed_recv,
    mixer_send, mixer_recv, small_send, small_recv, core_send, core_recv
):
    me = lax.axis_index("seq")
    core = lax.axis_index("tp")
    place, quarter = me // 4, lax.rem(me, 4)
    x, y = lax.rem(quarter, 2), quarter // 2
    x_peer, y_peer = me + 1 - 2 * x, me + 2 - 4 * y
    quarter_x, quarter_y, quarter_d = quarter + 1 - 2 * x, quarter + 2 - 4 * y, 3 - quarter
    rows, pieces = plan.rows, plan.pieces
    width = gated_ref.shape[1]
    first = lag * (length - 1)
    spread = SPREAD
    started = (place, length - 1 - place)
    ahead = (me + 4, me - 4)
    behind = (me - 4, me + 4)
    side_peers = (x_peer, y_peer)
    side_bits = (x, y)
    halves = (up_half_ref, down_half_ref)
    barrier = pltpu.get_barrier_semaphore()

    def greet(peer):
        pl.semaphore_signal(barrier, inc=1, device_id={"seq": peer}, device_id_type=MESH)

    greet(x_peer)
    greet(y_peer)
    pl.semaphore_signal(barrier, inc=1, device_id={"tp": 1 - core}, device_id_type=MESH)
    pl.when(place > 0)(lambda: greet(me - 4))
    pl.when(place < length - 1)(lambda: greet(me + 4))
    pairs = [
        (half_ref.at[pl.ds(pl.multiple_of(bit * plan.feed_rows, 8), plan.feed_rows)], sum_ref.at[d, pl.ds(0, plan.feed_rows)])
        for d, (half_ref, bit) in enumerate(zip(halves, side_bits))
    ]
    pairs += [
        (normed_hbm, normed_ref),
        (query_grad_hbm, query_grad_ref),
        (key_grad_hbm, key_grad_ref),
        (normed_x_hbm, normed_x_ref),
        (narrow_x_hbm, narrow_x_ref),
        (gated_hbm, gated_ref),
        (value_grad_hbm, value_grad_ref),
        (middle_grad_hbm, middle_grad_ref),
        (wide_y_hbm, wide_y_ref),
        (narrow_y_hbm, narrow_y_ref),
        (tokens_hbm, tokens_ref),
        (query_hbm, weights_ref.at[0]),
        (key_hbm, weights_ref.at[1]),
        (value_hbm, weights_ref.at[2]),
    ]
    loads = [pltpu.make_async_copy(source, target, load_sem.at[n]) for n, (source, target) in enumerate(pairs)]
    for load in loads:
        load.start()
    pl.semaphore_wait(barrier, 3 + (place > 0).astype(jnp.int32) + (place < length - 1).astype(jnp.int32))

    def remote(source, target, send, recv, peer):
        return pltpu.make_async_remote_copy(
            src_ref=source,
            dst_ref=target,
            send_sem=send,
            recv_sem=recv,
            device_id={"seq": peer},
            device_id_type=MESH,
        )

    def at(i):
        return pl.ds(pl.multiple_of(i * rows, 8), rows)

    def feed_copy(d, i):
        source = pl.ds(pl.multiple_of((1 - side_bits[d]) * plan.feed_rows + i * rows, 8), rows)
        return remote(
            halves[d].at[source], feed_got_ref.at[d, at(i)], feed_send.at[d, i], feed_recv.at[d, i], side_peers[d]
        )

    def send_feed(i, _):
        for d in range(2):
            feed_copy(d, i).start()
        return 0

    lax.fori_loop(0, min(WINDOW, plan.feed), send_feed, 0)

    def features(ref, h):
        return ref[:, pl.ds(pl.multiple_of(h * width, LANES), width)]

    def query_or_key(h):
        narrow = jnp.where(x == 0, query_grad_ref[...], key_grad_ref[...])
        return dot(features(normed_ref, h), narrow, 0, 0) + dot(features(normed_x_ref, h), narrow_x_ref[...], 0, 0)

    def value_or_out(h):
        left = jnp.where(y == 0, features(normed_ref, h), gated_ref[...])
        right = jnp.where(y == 0, value_grad_ref[...], features(middle_grad_ref, h))
        wide, narrow = features(wide_y_ref, h), narrow_y_ref[...]
        return dot(left, right, 0, 0) + dot(jnp.where(y == 0, wide, narrow), jnp.where(y == 0, narrow, wide), 0, 0)

    mixer_copies = [
        remote(send_ref.at[n], mixer_got_ref.at[n], mixer_send.at[n], mixer_recv.at[n], peer)
        for n, peer in enumerate((y_peer, x_peer))
    ]
    for load in loads:
        load.wait()

    def send_mixer():
        send_ref[0] = query_or_key(1 - y)
        mixer_copies[0].start()
        send_ref[1] = value_or_out(1 - x)
        mixer_copies[1].start()


    def chain_copy(d, i):
        return remote(
            sum_ref.at[d, at(i)], got_ref.at[d, at(i)], chain_send.at[d, i], chain_recv.at[d, i], ahead[d]
        )

    def z_copy(d, i, k):
        ref = out_ref.at[(quarter, quarter_x, quarter_y, quarter_d)[k], d, at(i)]
        return remote(ref, ref, z_send.at[d, i, k], z_recv.at[d, i, k], behind[d])

    def side_copy(d, i, k):
        even = lax.rem(i, 2) == 0
        source = (quarter, quarter, jnp.where(even, quarter_x, quarter_y))[k]
        peer = (x_peer, y_peer, jnp.where(even, y_peer, x_peer))[k]
        ref = out_ref.at[source, d, at(i)]
        return remote(ref, ref, side_send.at[d, i, k], side_recv.at[d, i, k], peer)

    def chain_step(d, i):
        @pl.when(i < plan.feed)
        def _():
            feed_copy(d, i).wait_recv()
            sum_ref[d, at(i)] = sum_ref[d, at(i)] + feed_got_ref[d, at(i)]

        @pl.when(started[d] > 0)
        def _():
            chain_copy(d, i).wait_recv()
            sum_ref[d, at(i)] = sum_ref[d, at(i)] + got_ref[d, at(i)]

        @pl.when(started[d] < length - 1)
        def _():
            chain_copy(d, i).start()

        @pl.when(started[d] == length - 1)
        def _():
            store = pltpu.make_async_copy(sum_ref.at[d, at(i)], out_ref.at[quarter, d, at(i)], store_sem.at[d, i])
            store.start()
            store.wait()

    def kind(d, i):
        remaining = length - 1 - started[d]
        far = is_far(i)
        sideways = jnp.logical_or(jnp.logical_not(far), remaining == 0)
        onward = jnp.logical_and(far, remaining < length - 1)
        return remaining, sideways, onward

    def own_step(d, i):
        remaining, sideways, _ = kind(d, i)

        @pl.when(remaining > 0)
        def _():
            z_copy(d, i, 0).wait_recv()

        @pl.when(remaining < length - 1)
        def _():
            z_copy(d, i, 0).start()

        @pl.when(sideways)
        def _():
            side_copy(d, i, 0).start()
            side_copy(d, i, 1).start()

    def side_step(d, i):
        _, sideways, onward = kind(d, i)

        @pl.when(sideways)
        def _():
            side_copy(d, i, 0).wait_recv()
            side_copy(d, i, 1).wait_recv()
            side_copy(d, i, 2).start()

        @pl.when(jnp.logical_not(sideways))
        def _():
            z_copy(d, i, 1).wait_recv()
            z_copy(d, i, 2).wait_recv()

        @pl.when(onward)
        def _():
            z_copy(d, i, 1).start()
            z_copy(d, i, 2).start()

    def last_step(d, i):
        _, sideways, onward = kind(d, i)

        @pl.when(sideways)
        def _():
            side_copy(d, i, 2).wait_recv()

        @pl.when(jnp.logical_not(sideways))
        def _():
            z_copy(d, i, 3).wait_recv()

        @pl.when(onward)
        def _():
            z_copy(d, i, 3).start()

    def tick(t, _):
        @pl.when(t + WINDOW < plan.feed)
        def _():
            send_feed(t + WINDOW, 0)

        steps = ((chain_step, 0), (own_step, first), (last_step, first + 2 * spread), (side_step, first + spread))
        for step, late in steps:
            for d in range(2):
                passed = lag * started[d] if step is chain_step else spread * (length - 1 - started[d])
                i = t - late - passed
                pl.when(jnp.logical_and(i >= 0, i < pieces))(functools.partial(step, d, i))
        return 0

    core_copy = pltpu.make_async_remote_copy(
        src_ref=local_ref,
        dst_ref=other_ref,
        send_sem=core_send.at[0],
        recv_sem=core_recv.at[0],
        device_id={"tp": 1 - core},
        device_id_type=MESH,
    )
    small_x = remote(
        small_sum_ref.at[1 - x], small_got_ref.at[pl.ds(0, 2)], small_send.at[0], small_recv.at[0], x_peer
    )
    small_y = remote(
        small_sum_ref.at[x, 1 - y], small_got_ref.at[2], small_send.at[1], small_recv.at[1], y_peer
    )

    def normed_grad():
        local_ref[...] = (
            dot(query_grad_ref[...], weights_ref[0], 1, 1)
            + dot(key_grad_ref[...], weights_ref[1], 1, 1)
            + dot(value_grad_ref[...], weights_ref[2], 1, 1)
        )
        core_copy.start()

    def first_norm():
        core_copy.wait_recv()
        grad = local_ref[...] + other_ref[...]
        values = tokens_ref[...]
        centered = values - over_features(values)
        inverse = lax.rsqrt(over_features(centered * centered) + EPSILON)
        scaled = centered * inverse
        scaled_grad = grad * gain_ref[...].reshape(1, -1)
        scaled_grad = scaled_grad - over_features(scaled_grad) - scaled * over_features(scaled_grad * scaled)
        input_grad_ref[...] = middle_grad_ref[...] + inverse * scaled_grad
        for p in range(4):
            small_sum_ref[p // 2, p % 2] = small_ref[p]
        small_sum_ref[0, 0, pl.ds(STATE // 4, 1), :] = over_tokens(grad * scaled)
        small_sum_ref[0, 0, pl.ds(STATE // 4 + 1, 1), :] = over_tokens(grad)
        small_x.start()

    def keep_mixer():
        keep_ref[0] = query_or_key(y)
        keep_ref[1] = value_or_out(x)

    def add_small():
        small_x.wait()
        small_sum_ref[x] = small_sum_ref[x] + small_got_ref[pl.ds(0, 2)]
        small_y.start()

    def mixer_sums():
        for copy in mixer_copies:
            copy.wait_recv()
        count = plan.mixer_rows // 2
        for d in range(2):
            source, target = pl.ds(d * count, count), pl.ds(plan.feed_rows, count)
            for n in range(2):
                sum_ref[d, target, pl.ds(n * width, width)] = keep_ref[n, source, :] + mixer_got_ref[n, source, :]

    def small_sums():
        small_y.wait()
        start = plan.feed_rows + plan.mixer_rows // 2
        sum_ref[:, pl.ds(start, plan.total - start), :] = jnp.zeros((2, plan.total - start, sum_ref.shape[2]), F32)
        sum_ref[0, pl.ds(start, plan.small_rows), :] = small_sum_ref[x, y] + small_got_ref[2]

    stages = (
        (1, (send_mixer,)),
        (2, (normed_grad,)),
        (5, (first_norm,)),
        (8, (keep_mixer, add_small)),
        (plan.feed, (mixer_sums, small_sums)),
    )
    at_tick = 0
    for until, work in stages:
        lax.fori_loop(at_tick, until, tick, 0)
        at_tick = until
        for piece in work:
            piece()
    lax.fori_loop(at_tick, first + spread * (length + 1) + pieces, tick, 0)

    def drain(i, _):
        for d in range(2):
            remaining, sideways, onward = kind(d, i)
            pl.when(i < plan.feed)(lambda: feed_copy(d, i).wait_send())
            pl.when(remaining > 0)(lambda: chain_copy(d, i).wait_send())
            pl.when(remaining < length - 1)(lambda: z_copy(d, i, 0).wait_send())

            @pl.when(onward)
            def _():
                for k in range(1, 4):
                    z_copy(d, i, k).wait_send()

            @pl.when(sideways)
            def _():
                for k in range(3):
                    side_copy(d, i, k).wait_send()

        return 0

    lax.fori_loop(0, pieces, drain, 0)
    for copy in mixer_copies + [core_copy]:
        copy.wait_send()


def summed_quarters(plan, lag, args, in_hbm, collective_id):
    length = lax.axis_size("seq") // 4
    pieces, feed = plan.pieces, plan.feed
    tokens, columns = args[4].shape
    width = args[6].shape[1]
    sems = [(16,), (2, pieces), (2, pieces), (2, pieces), (2, pieces, 4), (2, pieces, 4), (2, pieces, 3), (2, pieces, 3)]
    sems += [(2, feed), (2, feed), (2,), (2,), (2,), (2,), (1,), (1,)]
    wide, narrow = (tokens, columns), (tokens, width)
    scratch = [wide, wide, narrow, narrow, narrow, narrow, wide, narrow, wide, narrow, wide]
    scratch += [(2, plan.total, columns)] * 2 + [(2, plan.feed_rows, columns)] + [(2, plan.mixer_rows, width)] * 3
    scratch += [(3, plan.small_rows, columns), (2, 2, plan.small_rows, columns), (3, columns, width)] + [(tokens, columns)] * 2
    return pl.pallas_call(
        functools.partial(sum_kernel, length, plan, lag),
        out_shape=[shape(4, 2, plan.total, columns), shape(tokens, columns)],
        in_specs=[pl.BlockSpec(memory_space=pltpu.HBM if n in in_hbm else pltpu.VMEM) for n in range(len(args))],
        out_specs=[pl.BlockSpec(memory_space=pltpu.HBM), pl.BlockSpec(memory_space=pltpu.VMEM)],
        scratch_shapes=[pltpu.VMEM(dims, F32) for dims in scratch] + [pltpu.SemaphoreType.DMA(dims) for dims in sems],
        compiler_params=pltpu.CompilerParams(
            collective_id=collective_id, has_side_effects=True, vmem_limit_bytes=60 * 2**20
        ),
        name="gradient_sums",
    )(*args)


def unpack_kernel(plan, sums_hbm, block_hbm, grad_hbm, *refs):
    (
        up_ref, down_ref, query_ref, key_ref, value_ref, out_ref, rate_ref, state_out_ref, block_out_ref, input_grad_ref,
        *vector_refs, sums_ref, rows_ref, load_sem, store_sem
    ) = refs
    columns, width = up_ref.shape[0], query_ref.shape[1]
    feed, count, state = plan.feed_rows, plan.mixer_rows // 2, STATE // 4
    loads, stores = [], []

    def load(source, target):
        loads.append(pltpu.make_async_copy(source, target, load_sem.at[len(loads)]))
        loads[-1].start()

    def store(source, target):
        stores.append(pltpu.make_async_copy(source, target, store_sem.at[len(stores)]))
        stores[-1].start()

    def span(start, size):
        return pl.ds(start, size)

    quarters = [(x, y, 2 * y + x) for x in range(2) for y in range(2)]
    for part in (span(feed, plan.total - feed), span(0, feed)):
        for _, _, q in quarters:
            for d in range(2):
                load(sums_hbm.at[q, d, part], sums_ref.at[q, d, part])
    load(block_hbm, rows_ref.at[0])
    load(grad_hbm, rows_ref.at[1])
    waiting = iter(loads)
    for x, y, q in quarters:
        for d in range(2):
            next(waiting).wait()
            mixer = sums_ref.at[q, d, span(feed, count)]
            target = (query_ref, key_ref)[x]
            store(mixer.at[:, span(0, width)], target.at[span((2 * y + d) * count, count)])
            if y == 0:
                target = value_ref.at[span((2 * x + d) * count, count)]
            else:
                target = out_ref.at[span(d * count, count), span(x * width, width)]
            store(mixer.at[:, span(width, width)], target)
        rows = span((2 * x + y) * state, state)
        last = sums_ref.at[q, 0, span(feed + count, state)]
        store(last.at[:, span(0, width)], rate_ref.at[rows])
        store(last.at[:, span(width, width)], state_out_ref.at[rows])
    for x, y, q in quarters:
        next(waiting).wait()
        store(sums_ref.at[q, 0, span(0, feed)], up_ref.at[span(x * feed, feed), span(y * columns, columns)])
        next(waiting).wait()
        store(sums_ref.at[q, 1, span(0, feed)], down_ref.at[span((2 * x + y) * feed, feed)])
    for n, target in enumerate((block_out_ref, input_grad_ref)):
        next(waiting).wait()
        store(rows_ref.at[n], target)
    *wide_refs, up_bias_ref, skip_ref, taps_ref, query_bias_ref, key_bias_ref, value_bias_ref, step_ref = vector_refs
    row = feed + count + state

    def narrow(k):
        return sums_ref[2, 0, row + k // 2, pl.ds(k % 2 * width, width)]

    for k, ref in enumerate(wide_refs):
        ref[...] = sums_ref[0, 0, row + k, :]
    for k in range(2):
        up_bias_ref[pl.ds(k * columns, columns)] = sums_ref[0, 0, row + 6 + k, :]
    for k in range(SHIFT):
        taps_ref[k, :] = narrow(1 + k)
    for k, ref in ((0, skip_ref), (5, query_bias_ref), (6, key_bias_ref), (7, value_bias_ref), (8, step_ref)):
        ref[...] = narrow(k)
    for item in stores:
        item.wait()


def unpacked(plan, args, matrices, vectors):
    return pl.pallas_call(
        functools.partial(unpack_kernel, plan),
        out_shape=[shape(*out.shape) for out in (*matrices, *args[1:], *vectors)],
        in_specs=[pl.BlockSpec(memory_space=pltpu.HBM)] * 3,
        out_specs=[pl.BlockSpec(memory_space=pltpu.HBM)] * (len(matrices) + 2)
        + [pl.BlockSpec(memory_space=pltpu.VMEM)] * len(vectors),
        scratch_shapes=[
            pltpu.VMEM(args[0].shape, F32),
            pltpu.VMEM((2, *args[1].shape), F32),
            pltpu.SemaphoreType.DMA((18,)),
            pltpu.SemaphoreType.DMA((34,)),
        ],
        compiler_params=pltpu.CompilerParams(vmem_limit_bytes=60 * 2**20),
        name="unpack",
    )(*args)


def on_device(
    tokens,
    cotangent,
    norm1_gain,
    norm1_bias,
    query_weight,
    query_bias,
    key_weight,
    key_bias,
    value_weight,
    value_bias,
    shift_kernel,
    log_step,
    state_rate,
    state_out,
    skip_gain,
    out_weight,
    out_bias,
    norm2_gain,
    norm2_bias,
    up_weight,
    up_bias,
    down_weight,
    down_bias,
):
    rows, columns = tokens.shape
    width = query_weight.shape[1]
    hidden = up_weight.shape[1]
    span = lax.axis_size("seq") // SEQS
    blocks, groups = width // LANES, span // 4
    plan = Plan(columns // 2, width, PIECE_ROWS)
    tok, wide_tok, state, row_blocks = (rows, width), (rows, columns), (STATE, width), (blocks, rows, LANES)
    hidden_tok = (rows, hidden // 2)
    ends, totals = (4, STATE, width), (groups, STATE, width)
    end_sems, total_sems = (blocks, 3), (blocks, max(1, groups - 1))
    front = front_call(
        span,
        dict(
            norm1_gain=norm1_gain,
            norm1_bias=norm1_bias,
            query_bias=query_bias,
            key_bias=key_bias,
            value_bias=value_bias,
            taps=shift_kernel,
            log_step=log_step,
            state_rate=state_rate,
            state_out=state_out,
            skip_gain=skip_gain,
            out_bias=out_bias,
            norm2_gain=norm2_gain,
            norm2_bias=norm2_bias,
            up_bias=up_bias,
            down_bias=down_bias,
        ),
        dict(
            tokens_hbm=tokens,
            key_hbm=key_weight,
            value_hbm=value_weight,
            query_hbm=query_weight,
            cotangent_hbm=cotangent,
            down_hbm=down_weight,
            out_hbm=out_weight,
            up_hbm=up_weight,
        ),
        dict(
            block_out_hbm=wide_tok,
            middle_grad_hbm=wide_tok,
            normed1_hbm=wide_tok,
            gated_hbm=tok,
            query_grad_hbm=tok,
            key_grad_hbm=tok,
            value_grad_hbm=tok,
            small_hbm=(4, plan.small_rows, columns),
            down_half_hbm=(hidden // 2, columns),
            up_half_hbm=(columns, hidden // 2),
            normed1_x=wide_tok,
            narrow_x=tok,
            wide_y=wide_tok,
            narrow_y=tok,
        ),
        dict(
            tokens=wide_tok,
            cotangent=wide_tok,
            key_weight=key_weight.shape,
            value_weight=value_weight.shape,
            query_weight=query_weight.shape,
            out_weight=out_weight.shape,
            up=up_weight.shape,
            down=down_weight.shape,
            normed1=wide_tok,
            keys=(rows + 8, width),
            value=tok,
            query=tok,
            shifted=tok,
            mixed=tok,
            out=tok,
            gated=tok,
            rows=row_blocks,
            grad_rows=row_blocks,
            starts=(rows // CHUNK, STATE, width),
            part=(CHUNK, 8, LANES),
            state=(CHUNK, STATE, LANES),
            ends=ends,
            totals=totals,
            back_ends=ends,
            back_totals=totals,
            merged=wide_tok,
            merged_other=wide_tok,
            middle=wide_tok,
            scaled=wide_tok,
            normed2=wide_tok,
            active=(2, *hidden_tok),
            pre_grad=(2, *hidden_tok),
            normed_grad=wide_tok,
            normed_grad_other=wide_tok,
            feed=wide_tok,
            feed_other=wide_tok,
            active_peer=hidden_tok,
            pre_grad_peer=hidden_tok,
            cotangent_peer=wide_tok,
            normed2_peer=wide_tok,
            middle_grad=wide_tok,
            gated_grad=tok,
            grad=tok,
            query_grad=tok,
            key_grad=tok,
            value_grad=tok,
            shifted_grad=(rows + 8, width),
            coef=state,
            slope=state,
            wide=(8, columns),
            narrow=(16, width),
            rate=state,
            decay=state,
            in_coef=state,
            out_coef=state,
            device_decay=state,
            coef_rate=state,
            small=(4, plan.small_rows, columns),
            block_out=wide_tok,
            down_half=(hidden // 2, columns),
            up_half=(columns, hidden // 2),
        ),
        dict(
            end_send=end_sems,
            end_recv=end_sems,
            total_send=total_sems,
            total_recv=total_sems,
            back_end_send=end_sems,
            back_end_recv=end_sems,
            back_total_send=total_sems,
            back_total_recv=total_sems,
            halo_send=(2,),
            halo_recv=(2,),
            load_sem=(8,),
            store_sem=(10,),
            core_send=(4,),
            core_recv=(4,),
            half_send=(4,),
            half_recv=(4,),
            share_send=(4, 2),
            share_recv=(4, 2),
        ),
    )
    sums, input_grad = summed_quarters(
        plan,
        LAG,
        (front.small_hbm, norm1_gain, front.up_half_hbm, front.down_half_hbm, front.normed1_hbm)
        + (front.middle_grad_hbm, front.gated_hbm, front.query_grad_hbm, front.key_grad_hbm, front.value_grad_hbm)
        + (front.normed1_x, front.narrow_x, front.wide_y, front.narrow_y, tokens, query_weight, key_weight, value_weight),
        range(2, 18),
        3,
    )
    (
        grad_up_weight,
        grad_down_weight,
        grad_query_weight,
        grad_key_weight,
        grad_value_weight,
        grad_out_weight,
        grad_state_rate,
        grad_state_out,
        block_out,
        input_grad,
        grad_norm1_gain,
        grad_norm1_bias,
        grad_norm2_gain,
        grad_norm2_bias,
        grad_out_bias,
        grad_down_bias,
        grad_up_bias,
        grad_skip_gain,
        grad_shift_kernel,
        grad_query_bias,
        grad_key_bias,
        grad_value_bias,
        grad_log_step,
    ) = unpacked(
        plan,
        (sums, front.block_out_hbm, input_grad),
        (up_weight, down_weight, query_weight, key_weight, value_weight, out_weight, state_rate, state_out),
        (norm1_gain, norm1_bias, norm2_gain, norm2_bias, out_bias, down_bias, up_bias, skip_gain, shift_kernel)
        + (query_bias, key_bias, value_bias, log_step),
    )
    return (
        block_out,
        input_grad,
        grad_norm1_gain,
        grad_norm1_bias,
        grad_query_weight,
        grad_query_bias,
        grad_key_weight,
        grad_key_bias,
        grad_value_weight,
        grad_value_bias,
        grad_shift_kernel,
        grad_log_step,
        grad_state_rate,
        grad_state_out,
        grad_skip_gain,
        grad_out_weight,
        grad_out_bias,
        grad_norm2_gain,
        grad_norm2_bias,
        grad_up_weight,
        grad_up_bias,
        grad_down_weight,
        grad_down_bias,
    )


def solution(mesh):
    return jax.shard_map(
        on_device,
        mesh=mesh,
        in_specs=(
            P("seq", None),
            P("seq", None),
            P(),
            P(),
            P(None, "tp"),
            P("tp"),
            P(None, "tp"),
            P("tp"),
            P(None, "tp"),
            P("tp"),
            P(None, "tp"),
            P("tp"),
            P(None, "tp"),
            P(None, "tp"),
            P("tp"),
            P("tp", None),
            P(),
            P(),
            P(),
            P(None, "tp"),
            P("tp"),
            P("tp", None),
            P(),
        ),
        out_specs=(
            P("seq", None),
            P("seq", None),
            P(),
            P(),
            P(None, "tp"),
            P("tp"),
            P(None, "tp"),
            P("tp"),
            P(None, "tp"),
            P("tp"),
            P(None, "tp"),
            P("tp"),
            P(None, "tp"),
            P(None, "tp"),
            P("tp"),
            P("tp", None),
            P(),
            P(),
            P(),
            P(None, "tp"),
            P("tp"),
            P("tp", None),
            P(),
        ),
        check_vma=False,
    )
```

```python
import functools
import types

import jax
import jax.numpy as jnp
from jax import lax
from jax.experimental import pallas as pl
from jax.experimental.pallas import tpu as pltpu
from jax.sharding import PartitionSpec as P

SHIFT = 4
SEQS = 2
STATE = 64
LANES = 128
CHUNK = 32
PIECE_ROWS = 24
LAG = 2
SPREAD = 2
SIDE = 4
LAST = 6
WINDOW = 3
GELU_SCALE = (2.0 / 3.141592653589793) ** 0.5

EPSILON = 1e-05
F32 = jnp.float32
PRECISION = lax.Precision.HIGH


def shape(*dims):
    return jax.ShapeDtypeStruct(dims, F32)


def fold_states(values):
    return jnp.sum(values.reshape(STATE // 8, 8, LANES), axis=0)


def cut(block):
    return pl.ds(block * LANES, LANES)


class Sequence:
    def __init__(self, span, backward):
        self.me = lax.axis_index("seq")
        self.span = span
        self.place = lax.rem(self.me, span)
        self.start = self.me - self.place
        self.groups = span // 4
        self.quarter, self.group = lax.rem(self.place, 4), self.place // 4
        if backward:
            self.rank, self.turn = 3 - self.quarter, self.groups - 1 - self.group
        else:
            self.rank, self.turn = self.quarter, self.group
        self.backward = backward

    def greet(self, other_core):
        barrier = pltpu.get_barrier_semaphore()
        for k in range(1, self.span):
            peer = self.start + lax.rem(self.place + k, self.span)
            pl.semaphore_signal(barrier, inc=1, device_id={"seq": peer}, device_id_type=pl.DeviceIdType.MESH)
        pl.semaphore_signal(barrier, inc=1, device_id={"tp": other_core}, device_id_type=pl.DeviceIdType.MESH)

    def greeted(self):
        pl.semaphore_wait(pltpu.get_barrier_semaphore(), self.span)

    def remote(self, source, target, send, recv, peer, core=None):
        return pltpu.make_async_remote_copy(
            src_ref=source,
            dst_ref=target,
            send_sem=send,
            recv_sem=recv,
            device_id={"seq": peer} if core is None else {"tp": core},
            device_id_type=pl.DeviceIdType.MESH,
        )

    def end_copy(self, b, k, ends_ref, sems):
        other = lax.rem(self.quarter + k, 4)
        peer = self.me - self.quarter + other
        ref = ends_ref.at[self.rank, :, cut(b)]
        return self.remote(ref, ref, sems[0].at[b, k - 1], sems[1].at[b, k - 1], peer)

    def total_copy(self, b, k, totals_ref, sems):
        peer = self.me - 4 * k if self.backward else self.me + 4 * k
        ref = totals_ref.at[self.turn, :, cut(b)]
        return self.remote(ref, ref, sems[2].at[b, k - 1], sems[3].at[b, k - 1], peer)

    def send_end(self, b, end, ends_ref, sems):
        ends_ref[self.rank, :, cut(b)] = end
        for k in range(1, 4):
            self.end_copy(b, k, ends_ref, sems).start()

    def group_total(self, b, decay, ends_ref, totals_ref, sems):
        for k in range(1, 4):
            self.end_copy(b, k, ends_ref, sems).wait_recv()
        before = jnp.zeros_like(decay)
        total = ends_ref[0, :, cut(b)]
        for r in range(3):
            before = jnp.where(self.rank > r, before * decay + ends_ref[r, :, cut(b)], before)
            total = total * decay + ends_ref[r + 1, :, cut(b)]
        if self.groups > 1:
            totals_ref[self.turn, :, cut(b)] = total
            for k in range(1, self.groups):
                pl.when(self.turn + k < self.groups)(lambda: self.total_copy(b, k, totals_ref, sems).start())
        return before

    def carried(self, b, decay, before, totals_ref, sems):
        if self.groups == 1:
            return before
        square = decay * decay
        fourth = square * square
        carry = jnp.zeros_like(decay)
        for h in range(self.groups - 1):
            for k in range(1, self.groups - h):
                pl.when(self.turn == h + k)(lambda: self.total_copy(b, k, totals_ref, sems).wait_recv())
        for h in range(self.groups - 1):
            carry = jnp.where(self.turn > h, carry * fourth + totals_ref[h, :, cut(b)], carry)
        for r in range(3):
            carry = jnp.where(self.rank > r, carry * decay, carry)
        return before + carry

    def drain(self, blocks, ends_ref, totals_ref, sems):
        for b in range(blocks):
            for k in range(1, 4):
                self.end_copy(b, k, ends_ref, sems).wait_send()
            for k in range(1, self.groups):
                pl.when(self.turn + k < self.groups)(lambda: self.total_copy(b, k, totals_ref, sems).wait_send())


def dot(left, right, left_axis, right_axis):
    return lax.dot_general(
        left, right, (((left_axis,), (right_axis,)), ((), ())), precision=PRECISION, preferred_element_type=F32
    )


def over_tokens(values):
    return jnp.sum(values, axis=0, keepdims=True)


def over_features(values):
    return jnp.mean(values, axis=1, keepdims=True)


class Share:
    def __init__(self, seq, source_ref, target_ref, send, recv, peer, core, other_core):
        self.source_ref, self.target_ref, self.send, self.recv = source_ref, target_ref, send, recv
        self.seq, self.peer, self.core, self.other_core = seq, peer, core, other_core
        size = source_ref.shape[0] // 2
        self.mine = pl.ds(pl.multiple_of(core * size, 8), size)

    def across(self):
        return self.seq.remote(
            self.source_ref.at[self.mine], self.target_ref.at[self.mine], self.send.at[0], self.recv.at[0], self.peer
        )

    def between(self):
        ref = self.target_ref.at[self.mine]
        return self.seq.remote(ref, ref, self.send.at[1], self.recv.at[1], self.seq.me, self.other_core)

    def relay(self):
        self.across().wait_recv()
        self.between().start()

    def finish(self):
        self.between().wait_recv()
        self.across().wait_send()
        self.between().wait_send()


def one_less_exp(values):
    series = jnp.ones_like(values)
    for k in range(8, 1, -1):
        series = 1.0 - values * series * (1.0 / k)
    return jnp.where(values < 0.25, values * series, 1.0 - jnp.exp(-values))


def front_kernel(names, span, *refs):
    r = types.SimpleNamespace(**dict(zip(names, refs)))
    tokens, width = r.gated.shape
    hidden_half = r.up.shape[1] // 2
    blocks, chunks, top = width // LANES, tokens // CHUNK, tokens // 2
    ahead, back = Sequence(span, False), Sequence(span, True)
    ahead_sems = (r.end_send, r.end_recv, r.total_send, r.total_recv)
    back_sems = (r.back_end_send, r.back_end_recv, r.back_total_send, r.back_total_recv)
    me, remote = ahead.me, ahead.remote
    x, y = lax.rem(me, 2), lax.rem(me // 2, 2)
    x_peer, y_peer = me + 1 - 2 * x, me + 2 - 4 * y
    core = lax.axis_index("tp")
    other_core = 1 - core
    first, last = ahead.place == 0, ahead.place == span - 1

    pairs = (
        (r.tokens_hbm, r.tokens),
        (r.key_hbm, r.key_weight),
        (r.value_hbm, r.value_weight),
        (r.query_hbm, r.query_weight),
        (r.cotangent_hbm, r.cotangent),
        (r.down_hbm, r.down),
        (r.out_hbm, r.out_weight),
        (r.up_hbm, r.up),
    )
    loads = [pltpu.make_async_copy(source, target, r.load_sem.at[n]) for n, (source, target) in enumerate(pairs)]
    for load in loads:
        load.start()
    ahead.greet(other_core)
    vectors = (r.norm1_gain, r.norm1_bias, r.out_bias, r.norm2_gain, r.norm2_bias, r.down_bias)
    for k, vector in enumerate(vectors):
        r.wide[k : k + 1, :] = vector[...].reshape(1, -1)
    for k in range(2):
        r.wide[6 + k : 7 + k, :] = r.up_bias[pl.ds(k * hidden_half, hidden_half)].reshape(1, -1)
    for k, vector in enumerate((r.query_bias, r.key_bias, r.value_bias, r.skip_gain)):
        r.narrow[k : k + 1, :] = vector[...].reshape(1, -1)
    step = jnp.exp(r.log_step[...].reshape(1, -1))
    r.narrow[4:5, :] = step
    r.narrow[5 : 5 + SHIFT, :] = r.taps[...]
    rate = step * r.state_rate[...]
    decay = jnp.exp(-rate)
    in_coef = jnp.sqrt(one_less_exp(2.0 * rate))
    out_coef = in_coef * r.state_out[...]
    r.rate[...] = rate
    r.decay[...] = decay
    r.in_coef[...] = in_coef
    r.out_coef[...] = out_coef
    r.device_decay[...] = jnp.exp(-rate * tokens)
    r.coef_rate[...] = decay * decay / in_coef * r.state_out[...]
    stores = []

    def store(source, target):
        stores.append(pltpu.make_async_copy(source, target, r.store_sem.at[len(stores)]))
        stores[-1].start()

    def wide(k):
        return r.wide[k : k + 1, :]

    def narrow(k):
        return r.narrow[k : k + 1, :]

    def tap(j):
        return narrow(5 + j)

    def features(b):
        return slice(b * LANES, (b + 1) * LANES)

    loads[0].wait()
    values = r.tokens[...]
    centered = values - over_features(values)
    normed = centered * lax.rsqrt(over_features(centered * centered) + EPSILON) * wide(0) + wide(1)
    r.normed1[...] = normed
    store(r.normed1, r.normed1_hbm)
    loads[1].wait()
    r.keys[pl.ds(8, tokens), :] = dot(r.normed1[...], r.key_weight[...], 1, 0) + narrow(1)
    ahead.greeted()

    def halo_copy():
        return remote(
            r.keys.at[pl.ds(tokens, 8)], r.keys.at[pl.ds(0, 8)], r.halo_send.at[0], r.halo_recv.at[0], me + 1
        )

    @pl.when(jnp.logical_not(last))
    def _():
        halo_copy().start()

    loads[2].wait()
    r.value[...] = dot(r.normed1[...], r.value_weight[...], 1, 0) + narrow(2)

    def mix(start, count):
        total = tap(0) * r.keys[pl.ds(8 + start, count), :]
        for j in range(1, SHIFT):
            total = total + tap(j) * r.keys[pl.ds(8 + start - j, count), :]
        r.shifted[pl.ds(start, count), :] = total
        mixed = total * r.value[pl.ds(start, count), :]
        r.mixed[pl.ds(start, count), :] = mixed
        for b in range(blocks):
            r.rows[b, pl.ds(start, count), :] = mixed[:, features(b)]

    mix(8, tokens - 8)

    @pl.when(first)
    def _():
        r.keys[pl.ds(0, 8), :] = jnp.zeros((8, width), F32)

    @pl.when(jnp.logical_not(first))
    def _():
        halo_copy().wait_recv()

    mix(0, 8)

    for b in range(blocks):
        decay, out_coef = r.decay[:, cut(b)], r.out_coef[:, cut(b)]

        def scan(k, state, b=b, decay=decay, out_coef=out_coef):
            r.starts[k, :, cut(b)] = state
            base = pl.multiple_of(k * CHUNK, CHUNK)
            for j in range(CHUNK):
                state = decay * state + r.rows[b, pl.ds(base + j, 1), :]
                r.part[j] = fold_states(out_coef * state)
            r.out[pl.ds(base, CHUNK), cut(b)] = jnp.sum(r.part[...], axis=1)
            return state

        ahead.send_end(b, lax.fori_loop(0, chunks, scan, jnp.zeros_like(decay)), r.ends, ahead_sems)
    loads[3].wait()
    r.query[...] = dot(r.normed1[...], r.query_weight[...], 1, 0) + narrow(0)
    befores = [ahead.group_total(b, r.device_decay[:, cut(b)], r.ends, r.totals, ahead_sems) for b in range(blocks)]
    loads[4].wait()
    loads[5].wait()
    for n in range(2):
        r.pre_grad[n] = dot(r.cotangent[...], r.down[pl.ds(n * hidden_half, hidden_half), :], 1, 1)
    incoming = [
        ahead.carried(b, r.device_decay[:, cut(b)], befores[b], r.totals, ahead_sems) for b in range(blocks)
    ]

    cotangent_share = Share(
        ahead, r.cotangent, r.cotangent_peer, r.share_send.at[0], r.share_recv.at[0], x_peer, core, other_core
    )
    normed2_share = Share(
        ahead, r.normed2, r.normed2_peer, r.share_send.at[1], r.share_recv.at[1], y_peer, core, other_core
    )
    normed1_share = Share(
        ahead, r.normed1, r.normed1_x, r.share_send.at[2], r.share_recv.at[2], x_peer, core, other_core
    )
    wide_shares = [
        Share(ahead, source, r.wide_y, r.share_send.at[3], r.share_recv.at[3], y_peer, core, other_core)
        for source in (r.middle_grad, r.normed1)
    ]

    def narrow_copy(source, n, target, peer):
        return remote(source, target, r.half_send.at[n], r.half_recv.at[n], peer)

    def key_copy():
        return narrow_copy(r.key_grad, 4, r.narrow_x, x_peer)

    def query_copy():
        return narrow_copy(r.query_grad, 4, r.narrow_x, x_peer)

    def gated_copy():
        return narrow_copy(r.gated, 5, r.narrow_y, y_peer)

    def value_copy():
        return narrow_copy(r.value_grad, 5, r.narrow_y, y_peer)

    cotangent_share.across().start()

    @pl.when(y == 1)
    def _():
        wide_shares[1].across().start()

    for b in range(blocks):
        decay, out_coef = r.decay[:, cut(b)], r.out_coef[:, cut(b)]
        skip = narrow(3)[:, features(b)]

        def carry(k, state, b=b, decay=decay, out_coef=out_coef, skip=skip):
            r.starts[k, :, cut(b)] = r.starts[k, :, cut(b)] + state
            base = pl.multiple_of(k * CHUNK, CHUNK)
            for j in range(CHUNK):
                state = decay * state
                r.part[j] = fold_states(out_coef * state)
            rows = pl.ds(base, CHUNK)
            out = r.out[rows, cut(b)] + jnp.sum(r.part[...], axis=1) + skip * r.mixed[rows, cut(b)]
            r.out[rows, cut(b)] = out
            r.gated[rows, cut(b)] = r.query[rows, cut(b)] * out
            return state

        lax.fori_loop(0, chunks, carry, incoming[b])
    store(r.gated, r.gated_hbm)

    def core_copy(n, source, target):
        return remote(source, target, r.core_send.at[n], r.core_recv.at[n], me, other_core)

    loads[6].wait()
    merged_copies = []
    for n in range(2):
        rows = pl.ds(n * top, top)
        r.merged[rows, :] = dot(r.gated[rows, :], r.out_weight[...], 1, 0)
        copy = core_copy(n, r.merged.at[rows], r.merged_other.at[rows])
        copy.start()
        merged_copies.append(copy)

    @pl.when(y == 0)
    def _():
        gated_copy().start()

    normed1_share.across().start()
    small_start = STATE // 4
    r.small[...] = jnp.zeros_like(r.small)

    def put(k, row):
        r.small[1, pl.ds(small_start + k // 2, 1), pl.ds(k % 2 * width, width)] = row

    spreads = []
    for n, copy in enumerate(merged_copies):
        rows = pl.ds(n * top, top)
        copy.wait_recv()
        middle = r.tokens[rows, :] + (r.merged[rows, :] + r.merged_other[rows, :]) + wide(2)
        centered = middle - over_features(middle)
        inverse = lax.rsqrt(over_features(centered * centered) + EPSILON)
        scaled = centered * inverse
        r.middle[rows, :] = middle
        r.scaled[rows, :] = scaled
        r.normed2[rows, :] = scaled * wide(3) + wide(4)
        spreads.append(inverse)
    normed2_share.across().start()

    loads[7].wait()
    for n in range(2):
        part = pl.ds(n * hidden_half, hidden_half)
        pre = dot(r.normed2[...], r.up[:, part], 1, 0) + wide(6 + n)
        square = pre * pre
        curve = jnp.tanh(GELU_SCALE * (pre + 0.044715 * (square * pre)))
        r.active[n] = 0.5 * pre * (1.0 + curve)
        slope = 0.5 * (1.0 + curve) + 0.5 * pre * (1.0 - curve * curve) * (
            GELU_SCALE * (1.0 + 3 * 0.044715 * square)
        )
        pre_grad = r.pre_grad[n] * slope
        r.pre_grad[n] = pre_grad
        r.small[0, pl.ds(small_start + 6 + n, 1), :] = over_tokens(pre_grad)
        normed_grad = dot(pre_grad, r.up[:, part], 1, 1)
        if n == 0:
            r.normed_grad[...] = normed_grad
        else:
            r.normed_grad[...] = r.normed_grad[...] + normed_grad
    def half_copies(n):
        rows = pl.ds(n * top, top)
        return (
            remote(
                r.active.at[1 - x, rows], r.active_peer.at[rows], r.half_send.at[2 * n], r.half_recv.at[2 * n], x_peer
            ),
            remote(
                r.pre_grad.at[1 - y, rows],
                r.pre_grad_peer.at[rows],
                r.half_send.at[2 * n + 1],
                r.half_recv.at[2 * n + 1],
                y_peer,
            ),
        )

    normed_grad_copy = core_copy(2, r.normed_grad, r.normed_grad_other)
    normed_grad_copy.start()
    for copy in half_copies(0):
        copy.start()
    for n in range(2):
        feed = dot(r.active[n], r.down[pl.ds(n * hidden_half, hidden_half), :], 1, 0)
        if n == 0:
            r.feed[...] = feed
        else:
            r.feed[...] = r.feed[...] + feed
    feed_copy = core_copy(3, r.feed, r.feed_other)
    feed_copy.start()
    normed_grad_copy.wait_recv()
    for n in range(2):
        rows = pl.ds(n * top, top)
        normed_grad = r.normed_grad[rows, :] + r.normed_grad_other[rows, :]
        scaled = r.scaled[rows, :]
        scaled_grad = normed_grad * wide(3)
        centered = scaled_grad - over_features(scaled_grad) - scaled * over_features(scaled_grad * scaled)
        middle_grad = r.cotangent[rows, :] + spreads[n] * centered
        r.middle_grad[rows, :] = middle_grad
        sums = (normed_grad * scaled, normed_grad, middle_grad, r.cotangent[rows, :])
        for k, values in enumerate(sums):
            row = pl.ds(small_start + 2 + k, 1)
            if n == 0:
                r.small[0, row, :] = over_tokens(values)
            else:
                r.small[0, row, :] = r.small[0, row, :] + over_tokens(values)
        r.gated_grad[rows, :] = dot(middle_grad, r.out_weight[...], 1, 1)
    store(r.middle_grad, r.middle_grad_hbm)

    grad = r.gated_grad[...] * r.query[...]
    r.grad[...] = grad
    for b in range(blocks):
        r.grad_rows[b] = grad[:, features(b)]
    for b in range(blocks):
        decay = r.decay[:, cut(b)]

        def end(i, adjoint, b=b, decay=decay):
            base = pl.multiple_of((chunks - 1 - i) * CHUNK, CHUNK)
            for j in range(CHUNK - 1, -1, -1):
                adjoint = decay * adjoint + r.grad_rows[b, pl.ds(base + j, 1), :]
            return adjoint

        back.send_end(b, lax.fori_loop(0, chunks, end, jnp.zeros_like(decay)), r.back_ends, back_sems)
    for copy in half_copies(1):
        copy.start()
    query_grad = r.gated_grad[...] * r.out[...]
    r.query_grad[...] = query_grad
    store(r.query_grad, r.query_grad_hbm)
    put(0, over_tokens(r.grad[...] * r.mixed[...]))
    put(5, over_tokens(query_grad))
    cotangent_share.relay()
    normed1_share.relay()
    normed2_share.relay()
    feed_copy.wait_recv()
    r.block_out[...] = r.middle[...] + (r.feed[...] + r.feed_other[...]) + wide(5)
    store(r.block_out, r.block_out_hbm)
    befores = [
        back.group_total(b, r.device_decay[:, cut(b)], r.back_ends, r.back_totals, back_sems) for b in range(blocks)
    ]

    def product(left_ref, right_ref):
        return dot(left_ref[...], right_ref[...], 0, 0)

    r.down_half[...] = product(r.active.at[x], r.cotangent)
    incoming = [
        back.carried(b, r.device_decay[:, cut(b)], befores[b], r.back_totals, back_sems) for b in range(blocks)
    ]

    for b in range(blocks):
        if b == 1:

            @pl.when(y == 0)
            def _():
                wide_shares[0].across().start()

            @pl.when(x == 1)
            def _():
                query_copy().start()

        decay, out_coef = r.decay[:, cut(b)], r.out_coef[:, cut(b)]
        skip = narrow(3)[:, features(b)]
        r.coef[:, cut(b)] = jnp.zeros_like(decay)
        r.slope[:, cut(b)] = jnp.zeros_like(decay)

        def chunk(i, adjoint, b=b, decay=decay, out_coef=out_coef, skip=skip):
            k = chunks - 1 - i
            base = pl.multiple_of(k * CHUNK, CHUNK)
            state = r.starts[k, :, cut(b)]
            for j in range(CHUNK):
                r.state[j] = state
                state = decay * state + r.rows[b, pl.ds(base + j, 1), :]
            coef, slope = r.coef[:, cut(b)], r.slope[:, cut(b)]
            for j in range(CHUNK - 1, -1, -1):
                adjoint = decay * adjoint + r.grad_rows[b, pl.ds(base + j, 1), :]
                r.part[j] = fold_states(out_coef * adjoint)
                coef = coef + adjoint * r.rows[b, pl.ds(base + j, 1), :]
                slope = slope + adjoint * r.state[j]
            r.coef[:, cut(b)] = coef
            r.slope[:, cut(b)] = slope
            rows = pl.ds(base, CHUNK)
            grad_mixed = jnp.sum(r.part[...], axis=1) + skip * r.grad[rows, cut(b)]
            r.shifted_grad[rows, cut(b)] = grad_mixed * r.value[rows, cut(b)]
            r.value_grad[rows, cut(b)] = grad_mixed * r.shifted[rows, cut(b)]
            return adjoint

        lax.fori_loop(0, chunks, chunk, incoming[b])
    store(r.value_grad, r.value_grad_hbm)

    def head_copy():
        return remote(
            r.shifted_grad.at[pl.ds(0, 8)], r.shifted_grad.at[pl.ds(tokens, 8)], r.halo_send.at[1], r.halo_recv.at[1], me - 1
        )

    @pl.when(jnp.logical_not(first))
    def _():
        head_copy().start()

    @pl.when(y == 1)
    def _():
        value_copy().start()

    for j in range(SHIFT):
        put(1 + j, over_tokens(r.shifted_grad[pl.ds(0, tokens), :] * r.keys[pl.ds(8 - j, tokens), :]))
    put(7, over_tokens(r.value_grad[...]))
    r.up_half[...] = product(r.normed2, r.pre_grad.at[y])

    @pl.when(last)
    def _():
        r.shifted_grad[pl.ds(tokens, 8), :] = jnp.zeros((8, width), F32)

    @pl.when(jnp.logical_not(last))
    def _():
        head_copy().wait_recv()

    key_grad = tap(0) * r.shifted_grad[pl.ds(0, tokens), :]
    for j in range(1, SHIFT):
        key_grad = key_grad + tap(j) * r.shifted_grad[pl.ds(j, tokens), :]
    r.key_grad[...] = key_grad
    store(r.key_grad, r.key_grad_hbm)

    @pl.when(x == 0)
    def _():
        key_copy().start()

    put(6, over_tokens(key_grad))

    for p in range(4):
        rows = pl.ds(p * small_start, small_start)
        coef = r.coef[rows, :]
        rate_grad = r.coef_rate[rows, :] * coef - r.decay[rows, :] * r.out_coef[rows, :] * r.slope[rows, :]
        step_grad = over_tokens(r.rate[rows, :] * rate_grad)
        put(8, step_grad if p == 0 else r.small[1, pl.ds(small_start + 4, 1), pl.ds(0, width)] + step_grad)
        r.small[p, pl.ds(0, small_start), pl.ds(0, width)] = narrow(4) * rate_grad
        r.small[p, pl.ds(0, small_start), pl.ds(width, width)] = r.in_coef[rows, :] * coef
    store(r.small, r.small_hbm)
    wide_shares[0].relay()

    cotangent_share.finish()
    normed2_share.finish()
    halves = half_copies(0) + half_copies(1)
    for copy in halves[::2]:
        copy.wait()
    r.down_half[...] = r.down_half[...] + product(r.active_peer, r.cotangent_peer)
    store(r.down_half, r.down_half_hbm)
    for copy in halves[1::2]:
        copy.wait()
    r.up_half[...] = r.up_half[...] + product(r.normed2_peer, r.pre_grad_peer)
    store(r.up_half, r.up_half_hbm)
    normed1_share.finish()
    wide_shares[0].finish()
    key_copy().wait()
    gated_copy().wait()
    for copy in merged_copies + [normed_grad_copy, feed_copy]:
        copy.wait_send()
    ahead.drain(blocks, r.ends, r.totals, ahead_sems)
    back.drain(blocks, r.back_ends, r.back_totals, back_sems)

    @pl.when(jnp.logical_not(last))
    def _():
        halo_copy().wait_send()

    @pl.when(jnp.logical_not(first))
    def _():
        head_copy().wait_send()

    for copy in stores:
        copy.wait()


def front_call(span, inputs, in_hbm, outs, scratch, sems):
    names = [*inputs, *in_hbm, *outs, *scratch, *sems]
    results = pl.pallas_call(
        functools.partial(front_kernel, names, span),
        in_specs=[pl.BlockSpec(memory_space=pltpu.VMEM)] * len(inputs)
        + [pl.BlockSpec(memory_space=pltpu.HBM)] * len(in_hbm),
        out_specs=[pl.BlockSpec(memory_space=pltpu.HBM)] * len(outs),
        out_shape=[shape(*dims) for dims in outs.values()],
        scratch_shapes=[pltpu.VMEM(dims, F32) for dims in scratch.values()]
        + [pltpu.SemaphoreType.DMA(dims) for dims in sems.values()],
        compiler_params=pltpu.CompilerParams(collective_id=1, has_side_effects=True, vmem_limit_bytes=60 * 2**20),
        name="front",
    )(*inputs.values(), *in_hbm.values())
    return types.SimpleNamespace(**dict(zip(outs, results)))


MESH = pl.DeviceIdType.MESH


def is_far(i):
    return lax.rem(i, 5) == 1


class Plan:
    def __init__(self, feed_rows, mixer_rows, rows):
        self.rows = rows
        self.feed, self.mixer = feed_rows // rows, mixer_rows // 2 // rows
        self.small_rows = STATE // 4 + 8
        self.pieces = self.feed + self.mixer + -(-self.small_rows // rows)
        self.total = self.pieces * rows
        self.feed_rows, self.mixer_rows = feed_rows, mixer_rows


def sum_kernel(
    length, plan, lag,
    small_ref, gain_ref, up_half_ref, down_half_ref, normed_hbm, middle_grad_hbm, gated_hbm, query_grad_hbm, key_grad_hbm,
    value_grad_hbm, normed_x_hbm, narrow_x_hbm, wide_y_hbm, narrow_y_hbm, tokens_hbm, query_hbm, key_hbm, value_hbm,
    out_ref, input_grad_ref,
    normed_ref, middle_grad_ref, gated_ref, query_grad_ref, key_grad_ref, value_grad_ref,
    normed_x_ref, narrow_x_ref, wide_y_ref, narrow_y_ref, tokens_ref,
    sum_ref, got_ref, feed_got_ref, keep_ref, send_ref, mixer_got_ref, small_got_ref, small_sum_ref, weights_ref, local_ref,
    other_ref,
    load_sem, store_sem, chain_send, chain_recv, z_send, z_recv, side_send, side_recv, feed_send, feed_recv,
    mixer_send, mixer_recv, small_send, small_recv, core_send, core_recv
):
    me = lax.axis_index("seq")
    core = lax.axis_index("tp")
    place, quarter = me // 4, lax.rem(me, 4)
    x, y = lax.rem(quarter, 2), quarter // 2
    x_peer, y_peer = me + 1 - 2 * x, me + 2 - 4 * y
    quarter_x, quarter_y, quarter_d = quarter + 1 - 2 * x, quarter + 2 - 4 * y, 3 - quarter
    rows, pieces = plan.rows, plan.pieces
    width = gated_ref.shape[1]
    first = lag * (length - 1)
    spread = SPREAD
    started = (place, length - 1 - place)
    ahead = (me + 4, me - 4)
    behind = (me - 4, me + 4)
    side_peers = (x_peer, y_peer)
    side_bits = (x, y)
    halves = (up_half_ref, down_half_ref)
    barrier = pltpu.get_barrier_semaphore()

    def greet(peer):
        pl.semaphore_signal(barrier, inc=1, device_id={"seq": peer}, device_id_type=MESH)

    greet(x_peer)
    greet(y_peer)
    pl.semaphore_signal(barrier, inc=1, device_id={"tp": 1 - core}, device_id_type=MESH)
    pl.when(place > 0)(lambda: greet(me - 4))
    pl.when(place < length - 1)(lambda: greet(me + 4))
    pairs = [
        (half_ref.at[pl.ds(pl.multiple_of(bit * plan.feed_rows, 8), plan.feed_rows)], sum_ref.at[d, pl.ds(0, plan.feed_rows)])
        for d, (half_ref, bit) in enumerate(zip(halves, side_bits))
    ]
    pairs += [
        (normed_hbm, normed_ref),
        (query_grad_hbm, query_grad_ref),
        (key_grad_hbm, key_grad_ref),
        (normed_x_hbm, normed_x_ref),
        (narrow_x_hbm, narrow_x_ref),
        (gated_hbm, gated_ref),
        (value_grad_hbm, value_grad_ref),
        (middle_grad_hbm, middle_grad_ref),
        (wide_y_hbm, wide_y_ref),
        (narrow_y_hbm, narrow_y_ref),
        (tokens_hbm, tokens_ref),
        (query_hbm, weights_ref.at[0]),
        (key_hbm, weights_ref.at[1]),
        (value_hbm, weights_ref.at[2]),
    ]
    loads = [pltpu.make_async_copy(source, target, load_sem.at[n]) for n, (source, target) in enumerate(pairs)]
    for load in loads:
        load.start()
    pl.semaphore_wait(barrier, 3 + (place > 0).astype(jnp.int32) + (place < length - 1).astype(jnp.int32))

    def remote(source, target, send, recv, peer):
        return pltpu.make_async_remote_copy(
            src_ref=source,
            dst_ref=target,
            send_sem=send,
            recv_sem=recv,
            device_id={"seq": peer},
            device_id_type=MESH,
        )

    def at(i):
        return pl.ds(pl.multiple_of(i * rows, 8), rows)

    def feed_copy(d, i):
        source = pl.ds(pl.multiple_of((1 - side_bits[d]) * plan.feed_rows + i * rows, 8), rows)
        return remote(
            halves[d].at[source], feed_got_ref.at[d, at(i)], feed_send.at[d, i], feed_recv.at[d, i], side_peers[d]
        )

    def send_feed(i, _):
        for d in range(2):
            feed_copy(d, i).start()
        return 0

    lax.fori_loop(0, min(WINDOW, plan.feed), send_feed, 0)

    def features(ref, h):
        return ref[:, pl.ds(pl.multiple_of(h * width, LANES), width)]

    def query_or_key(h):
        narrow = jnp.where(x == 0, query_grad_ref[...], key_grad_ref[...])
        return dot(features(normed_ref, h), narrow, 0, 0) + dot(features(normed_x_ref, h), narrow_x_ref[...], 0, 0)

    def value_or_out(h):
        left = jnp.where(y == 0, features(normed_ref, h), gated_ref[...])
        right = jnp.where(y == 0, value_grad_ref[...], features(middle_grad_ref, h))
        wide, narrow = features(wide_y_ref, h), narrow_y_ref[...]
        return dot(left, right, 0, 0) + dot(jnp.where(y == 0, wide, narrow), jnp.where(y == 0, narrow, wide), 0, 0)

    mixer_copies = [
        remote(send_ref.at[n], mixer_got_ref.at[n], mixer_send.at[n], mixer_recv.at[n], peer)
        for n, peer in enumerate((y_peer, x_peer))
    ]
    for load in loads:
        load.wait()

    def send_mixer():
        send_ref[0] = query_or_key(1 - y)
        mixer_copies[0].start()
        send_ref[1] = value_or_out(1 - x)
        mixer_copies[1].start()


    def chain_copy(d, i):
        return remote(
            sum_ref.at[d, at(i)], got_ref.at[d, at(i)], chain_send.at[d, i], chain_recv.at[d, i], ahead[d]
        )

    def z_copy(d, i, k):
        ref = out_ref.at[(quarter, quarter_x, quarter_y, quarter_d)[k], d, at(i)]
        return remote(ref, ref, z_send.at[d, i, k], z_recv.at[d, i, k], behind[d])

    def side_copy(d, i, k):
        even = lax.rem(i, 2) == 0
        source = (quarter, quarter, jnp.where(even, quarter_x, quarter_y))[k]
        peer = (x_peer, y_peer, jnp.where(even, y_peer, x_peer))[k]
        ref = out_ref.at[source, d, at(i)]
        return remote(ref, ref, side_send.at[d, i, k], side_recv.at[d, i, k], peer)

    def chain_step(d, i):
        @pl.when(i < plan.feed)
        def _():
            feed_copy(d, i).wait_recv()
            sum_ref[d, at(i)] = sum_ref[d, at(i)] + feed_got_ref[d, at(i)]

        @pl.when(started[d] > 0)
        def _():
            chain_copy(d, i).wait_recv()
            sum_ref[d, at(i)] = sum_ref[d, at(i)] + got_ref[d, at(i)]

        @pl.when(started[d] < length - 1)
        def _():
            chain_copy(d, i).start()

        @pl.when(started[d] == length - 1)
        def _():
            store = pltpu.make_async_copy(sum_ref.at[d, at(i)], out_ref.at[quarter, d, at(i)], store_sem.at[d, i])
            store.start()
            store.wait()

    def kind(d, i):
        remaining = length - 1 - started[d]
        far = is_far(i)
        sideways = jnp.logical_or(jnp.logical_not(far), remaining == 0)
        onward = jnp.logical_and(far, remaining < length - 1)
        return remaining, sideways, onward

    def own_step(d, i):
        remaining, sideways, _ = kind(d, i)

        @pl.when(remaining > 0)
        def _():
            z_copy(d, i, 0).wait_recv()

        @pl.when(remaining < length - 1)
        def _():
            z_copy(d, i, 0).start()

        @pl.when(sideways)
        def _():
            side_copy(d, i, 0).start()
            side_copy(d, i, 1).start()

    def side_step(d, i):
        _, sideways, onward = kind(d, i)

        @pl.when(sideways)
        def _():
            side_copy(d, i, 0).wait_recv()
            side_copy(d, i, 1).wait_recv()
            side_copy(d, i, 2).start()

        @pl.when(jnp.logical_not(sideways))
        def _():
            z_copy(d, i, 1).wait_recv()
            z_copy(d, i, 2).wait_recv()

        @pl.when(onward)
        def _():
            z_copy(d, i, 1).start()
            z_copy(d, i, 2).start()

    def last_step(d, i):
        _, sideways, onward = kind(d, i)

        @pl.when(sideways)
        def _():
            side_copy(d, i, 2).wait_recv()

        @pl.when(jnp.logical_not(sideways))
        def _():
            z_copy(d, i, 3).wait_recv()

        @pl.when(onward)
        def _():
            z_copy(d, i, 3).start()

    def tick(t, _):
        @pl.when(t + WINDOW < plan.feed)
        def _():
            send_feed(t + WINDOW, 0)

        steps = ((chain_step, 0), (own_step, first), (last_step, first + SIDE + LAST), (side_step, first + SIDE))
        for step, late in steps:
            for d in range(2):
                passed = lag * started[d] if step is chain_step else spread * (length - 1 - started[d])
                i = t - late - passed
                pl.when(jnp.logical_and(i >= 0, i < pieces))(functools.partial(step, d, i))
        return 0

    core_copy = pltpu.make_async_remote_copy(
        src_ref=local_ref,
        dst_ref=other_ref,
        send_sem=core_send.at[0],
        recv_sem=core_recv.at[0],
        device_id={"tp": 1 - core},
        device_id_type=MESH,
    )
    small_x = remote(
        small_sum_ref.at[1 - x], small_got_ref.at[pl.ds(0, 2)], small_send.at[0], small_recv.at[0], x_peer
    )
    small_y = remote(
        small_sum_ref.at[x, 1 - y], small_got_ref.at[2], small_send.at[1], small_recv.at[1], y_peer
    )

    def normed_grad():
        local_ref[...] = (
            dot(query_grad_ref[...], weights_ref[0], 1, 1)
            + dot(key_grad_ref[...], weights_ref[1], 1, 1)
            + dot(value_grad_ref[...], weights_ref[2], 1, 1)
        )
        core_copy.start()

    def first_norm():
        core_copy.wait_recv()
        grad = local_ref[...] + other_ref[...]
        values = tokens_ref[...]
        centered = values - over_features(values)
        inverse = lax.rsqrt(over_features(centered * centered) + EPSILON)
        scaled = centered * inverse
        scaled_grad = grad * gain_ref[...].reshape(1, -1)
        scaled_grad = scaled_grad - over_features(scaled_grad) - scaled * over_features(scaled_grad * scaled)
        input_grad_ref[...] = middle_grad_ref[...] + inverse * scaled_grad
        for p in range(4):
            small_sum_ref[p // 2, p % 2] = small_ref[p]
        small_sum_ref[0, 0, pl.ds(STATE // 4, 1), :] = over_tokens(grad * scaled)
        small_sum_ref[0, 0, pl.ds(STATE // 4 + 1, 1), :] = over_tokens(grad)
        small_x.start()

    def keep_mixer():
        keep_ref[0] = query_or_key(y)
        keep_ref[1] = value_or_out(x)

    def add_small():
        small_x.wait()
        small_sum_ref[x] = small_sum_ref[x] + small_got_ref[pl.ds(0, 2)]
        small_y.start()

    def mixer_sums():
        for copy in mixer_copies:
            copy.wait_recv()
        count = plan.mixer_rows // 2
        for d in range(2):
            source, target = pl.ds(d * count, count), pl.ds(plan.feed_rows, count)
            for n in range(2):
                sum_ref[d, target, pl.ds(n * width, width)] = keep_ref[n, source, :] + mixer_got_ref[n, source, :]

    def small_sums():
        small_y.wait()
        start = plan.feed_rows + plan.mixer_rows // 2
        sum_ref[:, pl.ds(start, plan.total - start), :] = jnp.zeros((2, plan.total - start, sum_ref.shape[2]), F32)
        sum_ref[0, pl.ds(start, plan.small_rows), :] = small_sum_ref[x, y] + small_got_ref[2]

    stages = (
        (1, (send_mixer,)),
        (2, (normed_grad,)),
        (5, (first_norm,)),
        (8, (keep_mixer, add_small)),
        (plan.feed, (mixer_sums, small_sums)),
    )
    at_tick = 0
    for until, work in stages:
        lax.fori_loop(at_tick, until, tick, 0)
        at_tick = until
        for piece in work:
            piece()
    lax.fori_loop(at_tick, first + spread * (length - 1) + SIDE + LAST + pieces, tick, 0)

    def drain(i, _):
        for d in range(2):
            remaining, sideways, onward = kind(d, i)
            pl.when(i < plan.feed)(lambda: feed_copy(d, i).wait_send())
            pl.when(remaining > 0)(lambda: chain_copy(d, i).wait_send())
            pl.when(remaining < length - 1)(lambda: z_copy(d, i, 0).wait_send())

            @pl.when(onward)
            def _():
                for k in range(1, 4):
                    z_copy(d, i, k).wait_send()

            @pl.when(sideways)
            def _():
                for k in range(3):
                    side_copy(d, i, k).wait_send()

        return 0

    lax.fori_loop(0, pieces, drain, 0)
    for copy in mixer_copies + [core_copy]:
        copy.wait_send()


def summed_quarters(plan, lag, args, in_hbm, collective_id):
    length = lax.axis_size("seq") // 4
    pieces, feed = plan.pieces, plan.feed
    tokens, columns = args[4].shape
    width = args[6].shape[1]
    sems = [(16,), (2, pieces), (2, pieces), (2, pieces), (2, pieces, 4), (2, pieces, 4), (2, pieces, 3), (2, pieces, 3)]
    sems += [(2, feed), (2, feed), (2,), (2,), (2,), (2,), (1,), (1,)]
    wide, narrow = (tokens, columns), (tokens, width)
    scratch = [wide, wide, narrow, narrow, narrow, narrow, wide, narrow, wide, narrow, wide]
    scratch += [(2, plan.total, columns)] * 2 + [(2, plan.feed_rows, columns)] + [(2, plan.mixer_rows, width)] * 3
    scratch += [(3, plan.small_rows, columns), (2, 2, plan.small_rows, columns), (3, columns, width)] + [(tokens, columns)] * 2
    return pl.pallas_call(
        functools.partial(sum_kernel, length, plan, lag),
        out_shape=[shape(4, 2, plan.total, columns), shape(tokens, columns)],
        in_specs=[pl.BlockSpec(memory_space=pltpu.HBM if n in in_hbm else pltpu.VMEM) for n in range(len(args))],
        out_specs=[pl.BlockSpec(memory_space=pltpu.HBM), pl.BlockSpec(memory_space=pltpu.VMEM)],
        scratch_shapes=[pltpu.VMEM(dims, F32) for dims in scratch] + [pltpu.SemaphoreType.DMA(dims) for dims in sems],
        compiler_params=pltpu.CompilerParams(
            collective_id=collective_id, has_side_effects=True, vmem_limit_bytes=60 * 2**20
        ),
        name="gradient_sums",
    )(*args)


def unpack_kernel(plan, sums_hbm, block_hbm, grad_hbm, *refs):
    (
        up_ref, down_ref, query_ref, key_ref, value_ref, out_ref, rate_ref, state_out_ref, block_out_ref, input_grad_ref,
        *vector_refs, sums_ref, rows_ref, load_sem, store_sem
    ) = refs
    columns, width = up_ref.shape[0], query_ref.shape[1]
    feed, count, state = plan.feed_rows, plan.mixer_rows // 2, STATE // 4
    loads, stores = [], []

    def load(source, target):
        loads.append(pltpu.make_async_copy(source, target, load_sem.at[len(loads)]))
        loads[-1].start()

    def store(source, target):
        stores.append(pltpu.make_async_copy(source, target, store_sem.at[len(stores)]))
        stores[-1].start()

    def span(start, size):
        return pl.ds(start, size)

    quarters = [(x, y, 2 * y + x) for x in range(2) for y in range(2)]
    for part in (span(feed, plan.total - feed), span(0, feed)):
        for _, _, q in quarters:
            for d in range(2):
                load(sums_hbm.at[q, d, part], sums_ref.at[q, d, part])
    load(block_hbm, rows_ref.at[0])
    load(grad_hbm, rows_ref.at[1])
    waiting = iter(loads)
    for x, y, q in quarters:
        for d in range(2):
            next(waiting).wait()
            mixer = sums_ref.at[q, d, span(feed, count)]
            target = (query_ref, key_ref)[x]
            store(mixer.at[:, span(0, width)], target.at[span((2 * y + d) * count, count)])
            if y == 0:
                target = value_ref.at[span((2 * x + d) * count, count)]
            else:
                target = out_ref.at[span(d * count, count), span(x * width, width)]
            store(mixer.at[:, span(width, width)], target)
        rows = span((2 * x + y) * state, state)
        last = sums_ref.at[q, 0, span(feed + count, state)]
        store(last.at[:, span(0, width)], rate_ref.at[rows])
        store(last.at[:, span(width, width)], state_out_ref.at[rows])
    for x, y, q in quarters:
        next(waiting).wait()
        store(sums_ref.at[q, 0, span(0, feed)], up_ref.at[span(x * feed, feed), span(y * columns, columns)])
        next(waiting).wait()
        store(sums_ref.at[q, 1, span(0, feed)], down_ref.at[span((2 * x + y) * feed, feed)])
    for n, target in enumerate((block_out_ref, input_grad_ref)):
        next(waiting).wait()
        store(rows_ref.at[n], target)
    *wide_refs, up_bias_ref, skip_ref, taps_ref, query_bias_ref, key_bias_ref, value_bias_ref, step_ref = vector_refs
    row = feed + count + state

    def narrow(k):
        return sums_ref[2, 0, row + k // 2, pl.ds(k % 2 * width, width)]

    for k, ref in enumerate(wide_refs):
        ref[...] = sums_ref[0, 0, row + k, :]
    for k in range(2):
        up_bias_ref[pl.ds(k * columns, columns)] = sums_ref[0, 0, row + 6 + k, :]
    for k in range(SHIFT):
        taps_ref[k, :] = narrow(1 + k)
    for k, ref in ((0, skip_ref), (5, query_bias_ref), (6, key_bias_ref), (7, value_bias_ref), (8, step_ref)):
        ref[...] = narrow(k)
    for item in stores:
        item.wait()


def unpacked(plan, args, matrices, vectors):
    return pl.pallas_call(
        functools.partial(unpack_kernel, plan),
        out_shape=[shape(*out.shape) for out in (*matrices, *args[1:], *vectors)],
        in_specs=[pl.BlockSpec(memory_space=pltpu.HBM)] * 3,
        out_specs=[pl.BlockSpec(memory_space=pltpu.HBM)] * (len(matrices) + 2)
        + [pl.BlockSpec(memory_space=pltpu.VMEM)] * len(vectors),
        scratch_shapes=[
            pltpu.VMEM(args[0].shape, F32),
            pltpu.VMEM((2, *args[1].shape), F32),
            pltpu.SemaphoreType.DMA((18,)),
            pltpu.SemaphoreType.DMA((34,)),
        ],
        compiler_params=pltpu.CompilerParams(vmem_limit_bytes=60 * 2**20),
        name="unpack",
    )(*args)


def on_device(
    tokens,
    cotangent,
    norm1_gain,
    norm1_bias,
    query_weight,
    query_bias,
    key_weight,
    key_bias,
    value_weight,
    value_bias,
    shift_kernel,
    log_step,
    state_rate,
    state_out,
    skip_gain,
    out_weight,
    out_bias,
    norm2_gain,
    norm2_bias,
    up_weight,
    up_bias,
    down_weight,
    down_bias,
):
    rows, columns = tokens.shape
    width = query_weight.shape[1]
    hidden = up_weight.shape[1]
    span = lax.axis_size("seq") // SEQS
    blocks, groups = width // LANES, span // 4
    plan = Plan(columns // 2, width, PIECE_ROWS)
    tok, wide_tok, state, row_blocks = (rows, width), (rows, columns), (STATE, width), (blocks, rows, LANES)
    hidden_tok = (rows, hidden // 2)
    ends, totals = (4, STATE, width), (groups, STATE, width)
    end_sems, total_sems = (blocks, 3), (blocks, max(1, groups - 1))
    front = front_call(
        span,
        dict(
            norm1_gain=norm1_gain,
            norm1_bias=norm1_bias,
            query_bias=query_bias,
            key_bias=key_bias,
            value_bias=value_bias,
            taps=shift_kernel,
            log_step=log_step,
            state_rate=state_rate,
            state_out=state_out,
            skip_gain=skip_gain,
            out_bias=out_bias,
            norm2_gain=norm2_gain,
            norm2_bias=norm2_bias,
            up_bias=up_bias,
            down_bias=down_bias,
        ),
        dict(
            tokens_hbm=tokens,
            key_hbm=key_weight,
            value_hbm=value_weight,
            query_hbm=query_weight,
            cotangent_hbm=cotangent,
            down_hbm=down_weight,
            out_hbm=out_weight,
            up_hbm=up_weight,
        ),
        dict(
            block_out_hbm=wide_tok,
            middle_grad_hbm=wide_tok,
            normed1_hbm=wide_tok,
            gated_hbm=tok,
            query_grad_hbm=tok,
            key_grad_hbm=tok,
            value_grad_hbm=tok,
            small_hbm=(4, plan.small_rows, columns),
            down_half_hbm=(hidden // 2, columns),
            up_half_hbm=(columns, hidden // 2),
            normed1_x=wide_tok,
            narrow_x=tok,
            wide_y=wide_tok,
            narrow_y=tok,
        ),
        dict(
            tokens=wide_tok,
            cotangent=wide_tok,
            key_weight=key_weight.shape,
            value_weight=value_weight.shape,
            query_weight=query_weight.shape,
            out_weight=out_weight.shape,
            up=up_weight.shape,
            down=down_weight.shape,
            normed1=wide_tok,
            keys=(rows + 8, width),
            value=tok,
            query=tok,
            shifted=tok,
            mixed=tok,
            out=tok,
            gated=tok,
            rows=row_blocks,
            grad_rows=row_blocks,
            starts=(rows // CHUNK, STATE, width),
            part=(CHUNK, 8, LANES),
            state=(CHUNK, STATE, LANES),
            ends=ends,
            totals=totals,
            back_ends=ends,
            back_totals=totals,
            merged=wide_tok,
            merged_other=wide_tok,
            middle=wide_tok,
            scaled=wide_tok,
            normed2=wide_tok,
            active=(2, *hidden_tok),
            pre_grad=(2, *hidden_tok),
            normed_grad=wide_tok,
            normed_grad_other=wide_tok,
            feed=wide_tok,
            feed_other=wide_tok,
            active_peer=hidden_tok,
            pre_grad_peer=hidden_tok,
            cotangent_peer=wide_tok,
            normed2_peer=wide_tok,
            middle_grad=wide_tok,
            gated_grad=tok,
            grad=tok,
            query_grad=tok,
            key_grad=tok,
            value_grad=tok,
            shifted_grad=(rows + 8, width),
            coef=state,
            slope=state,
            wide=(8, columns),
            narrow=(16, width),
            rate=state,
            decay=state,
            in_coef=state,
            out_coef=state,
            device_decay=state,
            coef_rate=state,
            small=(4, plan.small_rows, columns),
            block_out=wide_tok,
            down_half=(hidden // 2, columns),
            up_half=(columns, hidden // 2),
        ),
        dict(
            end_send=end_sems,
            end_recv=end_sems,
            total_send=total_sems,
            total_recv=total_sems,
            back_end_send=end_sems,
            back_end_recv=end_sems,
            back_total_send=total_sems,
            back_total_recv=total_sems,
            halo_send=(2,),
            halo_recv=(2,),
            load_sem=(8,),
            store_sem=(10,),
            core_send=(4,),
            core_recv=(4,),
            half_send=(6,),
            half_recv=(6,),
            share_send=(4, 2),
            share_recv=(4, 2),
        ),
    )
    sums, input_grad = summed_quarters(
        plan,
        LAG,
        (front.small_hbm, norm1_gain, front.up_half_hbm, front.down_half_hbm, front.normed1_hbm)
        + (front.middle_grad_hbm, front.gated_hbm, front.query_grad_hbm, front.key_grad_hbm, front.value_grad_hbm)
        + (front.normed1_x, front.narrow_x, front.wide_y, front.narrow_y, tokens, query_weight, key_weight, value_weight),
        range(2, 18),
        3,
    )
    (
        grad_up_weight,
        grad_down_weight,
        grad_query_weight,
        grad_key_weight,
        grad_value_weight,
        grad_out_weight,
        grad_state_rate,
        grad_state_out,
        block_out,
        input_grad,
        grad_norm1_gain,
        grad_norm1_bias,
        grad_norm2_gain,
        grad_norm2_bias,
        grad_out_bias,
        grad_down_bias,
        grad_up_bias,
        grad_skip_gain,
        grad_shift_kernel,
        grad_query_bias,
        grad_key_bias,
        grad_value_bias,
        grad_log_step,
    ) = unpacked(
        plan,
        (sums, front.block_out_hbm, input_grad),
        (up_weight, down_weight, query_weight, key_weight, value_weight, out_weight, state_rate, state_out),
        (norm1_gain, norm1_bias, norm2_gain, norm2_bias, out_bias, down_bias, up_bias, skip_gain, shift_kernel)
        + (query_bias, key_bias, value_bias, log_step),
    )
    return (
        block_out,
        input_grad,
        grad_norm1_gain,
        grad_norm1_bias,
        grad_query_weight,
        grad_query_bias,
        grad_key_weight,
        grad_key_bias,
        grad_value_weight,
        grad_value_bias,
        grad_shift_kernel,
        grad_log_step,
        grad_state_rate,
        grad_state_out,
        grad_skip_gain,
        grad_out_weight,
        grad_out_bias,
        grad_norm2_gain,
        grad_norm2_bias,
        grad_up_weight,
        grad_up_bias,
        grad_down_weight,
        grad_down_bias,
    )


def solution(mesh):
    return jax.shard_map(
        on_device,
        mesh=mesh,
        in_specs=(
            P("seq", None),
            P("seq", None),
            P(),
            P(),
            P(None, "tp"),
            P("tp"),
            P(None, "tp"),
            P("tp"),
            P(None, "tp"),
            P("tp"),
            P(None, "tp"),
            P("tp"),
            P(None, "tp"),
            P(None, "tp"),
            P("tp"),
            P("tp", None),
            P(),
            P(),
            P(),
            P(None, "tp"),
            P("tp"),
            P("tp", None),
            P(),
        ),
        out_specs=(
            P("seq", None),
            P("seq", None),
            P(),
            P(),
            P(None, "tp"),
            P("tp"),
            P(None, "tp"),
            P("tp"),
            P(None, "tp"),
            P("tp"),
            P(None, "tp"),
            P("tp"),
            P(None, "tp"),
            P(None, "tp"),
            P("tp"),
            P("tp", None),
            P(),
            P(),
            P(),
            P(None, "tp"),
            P("tp"),
            P("tp", None),
            P(),
        ),
        check_vma=False,
    )
```

```python
import functools
import types

import jax
import jax.numpy as jnp
from jax import lax
from jax.experimental import pallas as pl
from jax.experimental.pallas import tpu as pltpu
from jax.sharding import PartitionSpec as P

SHIFT = 4
SEQS = 2
STATE = 64
LANES = 128
CHUNK = 32
PIECE_ROWS = 24
LAG = 2
SPREAD = 2
SIDE = 4
LAST = 6
WINDOW = 3
EARLY = 2
GELU_SCALE = (2.0 / 3.141592653589793) ** 0.5

EPSILON = 1e-05
F32 = jnp.float32
PRECISION = lax.Precision.HIGH


def shape(*dims):
    return jax.ShapeDtypeStruct(dims, F32)


def fold_states(values):
    return jnp.sum(values.reshape(STATE // 8, 8, LANES), axis=0)


def cut(block):
    return pl.ds(block * LANES, LANES)


class Sequence:
    def __init__(self, span, backward):
        self.me = lax.axis_index("seq")
        self.span = span
        self.place = lax.rem(self.me, span)
        self.start = self.me - self.place
        self.groups = span // 4
        self.quarter, self.group = lax.rem(self.place, 4), self.place // 4
        if backward:
            self.rank, self.turn = 3 - self.quarter, self.groups - 1 - self.group
        else:
            self.rank, self.turn = self.quarter, self.group
        self.backward = backward

    def greet(self, other_core):
        barrier = pltpu.get_barrier_semaphore()
        for k in range(1, self.span):
            peer = self.start + lax.rem(self.place + k, self.span)
            pl.semaphore_signal(barrier, inc=1, device_id={"seq": peer}, device_id_type=pl.DeviceIdType.MESH)
        pl.semaphore_signal(barrier, inc=1, device_id={"tp": other_core}, device_id_type=pl.DeviceIdType.MESH)

    def greeted(self):
        pl.semaphore_wait(pltpu.get_barrier_semaphore(), self.span)

    def remote(self, source, target, send, recv, peer, core=None):
        return pltpu.make_async_remote_copy(
            src_ref=source,
            dst_ref=target,
            send_sem=send,
            recv_sem=recv,
            device_id={"seq": peer} if core is None else {"tp": core},
            device_id_type=pl.DeviceIdType.MESH,
        )

    def end_copy(self, b, k, ends_ref, sems):
        other = lax.rem(self.quarter + k, 4)
        peer = self.me - self.quarter + other
        ref = ends_ref.at[self.rank, :, cut(b)]
        return self.remote(ref, ref, sems[0].at[b, k - 1], sems[1].at[b, k - 1], peer)

    def total_copy(self, b, k, totals_ref, sems):
        peer = self.me - 4 * k if self.backward else self.me + 4 * k
        ref = totals_ref.at[self.turn, :, cut(b)]
        return self.remote(ref, ref, sems[2].at[b, k - 1], sems[3].at[b, k - 1], peer)

    def send_end(self, b, end, ends_ref, sems):
        ends_ref[self.rank, :, cut(b)] = end
        for k in range(1, 4):
            self.end_copy(b, k, ends_ref, sems).start()

    def group_total(self, b, decay, ends_ref, totals_ref, sems):
        for k in range(1, 4):
            self.end_copy(b, k, ends_ref, sems).wait_recv()
        before = jnp.zeros_like(decay)
        total = ends_ref[0, :, cut(b)]
        for r in range(3):
            before = jnp.where(self.rank > r, before * decay + ends_ref[r, :, cut(b)], before)
            total = total * decay + ends_ref[r + 1, :, cut(b)]
        if self.groups > 1:
            totals_ref[self.turn, :, cut(b)] = total
            for k in range(1, self.groups):
                pl.when(self.turn + k < self.groups)(lambda: self.total_copy(b, k, totals_ref, sems).start())
        return before

    def carried(self, b, decay, before, totals_ref, sems):
        if self.groups == 1:
            return before
        square = decay * decay
        fourth = square * square
        carry = jnp.zeros_like(decay)
        for h in range(self.groups - 1):
            for k in range(1, self.groups - h):
                pl.when(self.turn == h + k)(lambda: self.total_copy(b, k, totals_ref, sems).wait_recv())
        for h in range(self.groups - 1):
            carry = jnp.where(self.turn > h, carry * fourth + totals_ref[h, :, cut(b)], carry)
        for r in range(3):
            carry = jnp.where(self.rank > r, carry * decay, carry)
        return before + carry

    def drain(self, blocks, ends_ref, totals_ref, sems):
        for b in range(blocks):
            for k in range(1, 4):
                self.end_copy(b, k, ends_ref, sems).wait_send()
            for k in range(1, self.groups):
                pl.when(self.turn + k < self.groups)(lambda: self.total_copy(b, k, totals_ref, sems).wait_send())


def dot(left, right, left_axis, right_axis):
    return lax.dot_general(
        left, right, (((left_axis,), (right_axis,)), ((), ())), precision=PRECISION, preferred_element_type=F32
    )


def over_tokens(values):
    return jnp.sum(values, axis=0, keepdims=True)


def over_features(values):
    return jnp.mean(values, axis=1, keepdims=True)


class Share:
    def __init__(self, seq, source_ref, target_ref, send, recv, peer, core, other_core):
        self.source_ref, self.target_ref, self.send, self.recv = source_ref, target_ref, send, recv
        self.seq, self.peer, self.core, self.other_core = seq, peer, core, other_core
        size = source_ref.shape[0] // 2
        self.mine = pl.ds(pl.multiple_of(core * size, 8), size)

    def across(self):
        return self.seq.remote(
            self.source_ref.at[self.mine], self.target_ref.at[self.mine], self.send.at[0], self.recv.at[0], self.peer
        )

    def between(self):
        ref = self.target_ref.at[self.mine]
        return self.seq.remote(ref, ref, self.send.at[1], self.recv.at[1], self.seq.me, self.other_core)

    def relay(self):
        self.across().wait_recv()
        self.between().start()

    def finish(self):
        self.between().wait_recv()
        self.across().wait_send()
        self.between().wait_send()


def one_less_exp(values):
    series = jnp.ones_like(values)
    for k in range(8, 1, -1):
        series = 1.0 - values * series * (1.0 / k)
    return jnp.where(values < 0.25, values * series, 1.0 - jnp.exp(-values))


def front_kernel(names, span, *refs):
    r = types.SimpleNamespace(**dict(zip(names, refs)))
    tokens, width = r.gated.shape
    hidden_half = r.up.shape[1] // 2
    blocks, chunks, top = width // LANES, tokens // CHUNK, tokens // 2
    ahead, back = Sequence(span, False), Sequence(span, True)
    ahead_sems = (r.end_send, r.end_recv, r.total_send, r.total_recv)
    back_sems = (r.back_end_send, r.back_end_recv, r.back_total_send, r.back_total_recv)
    me, remote = ahead.me, ahead.remote
    x, y = lax.rem(me, 2), lax.rem(me // 2, 2)
    x_peer, y_peer = me + 1 - 2 * x, me + 2 - 4 * y
    core = lax.axis_index("tp")
    other_core = 1 - core
    first, last = ahead.place == 0, ahead.place == span - 1

    pairs = (
        (r.tokens_hbm, r.tokens),
        (r.key_hbm, r.key_weight),
        (r.value_hbm, r.value_weight),
        (r.query_hbm, r.query_weight),
        (r.cotangent_hbm, r.cotangent),
        (r.down_hbm, r.down),
        (r.out_hbm, r.out_weight),
        (r.up_hbm, r.up),
    )
    loads = [pltpu.make_async_copy(source, target, r.load_sem.at[n]) for n, (source, target) in enumerate(pairs)]
    for load in loads:
        load.start()
    ahead.greet(other_core)
    vectors = (r.norm1_gain, r.norm1_bias, r.out_bias, r.norm2_gain, r.norm2_bias, r.down_bias)
    for k, vector in enumerate(vectors):
        r.wide[k : k + 1, :] = vector[...].reshape(1, -1)
    for k in range(2):
        r.wide[6 + k : 7 + k, :] = r.up_bias[pl.ds(k * hidden_half, hidden_half)].reshape(1, -1)
    for k, vector in enumerate((r.query_bias, r.key_bias, r.value_bias, r.skip_gain)):
        r.narrow[k : k + 1, :] = vector[...].reshape(1, -1)
    step = jnp.exp(r.log_step[...].reshape(1, -1))
    r.narrow[4:5, :] = step
    r.narrow[5 : 5 + SHIFT, :] = r.taps[...]
    rate = step * r.state_rate[...]
    decay = jnp.exp(-rate)
    in_coef = jnp.sqrt(one_less_exp(2.0 * rate))
    out_coef = in_coef * r.state_out[...]
    r.rate[...] = rate
    r.decay[...] = decay
    r.in_coef[...] = in_coef
    r.out_coef[...] = out_coef
    r.device_decay[...] = jnp.exp(-rate * tokens)
    r.coef_rate[...] = decay * decay / in_coef * r.state_out[...]
    stores = []

    def store(source, target):
        stores.append(pltpu.make_async_copy(source, target, r.store_sem.at[len(stores)]))
        stores[-1].start()

    def wide(k):
        return r.wide[k : k + 1, :]

    def narrow(k):
        return r.narrow[k : k + 1, :]

    def tap(j):
        return narrow(5 + j)

    def features(b):
        return slice(b * LANES, (b + 1) * LANES)

    loads[0].wait()
    values = r.tokens[...]
    centered = values - over_features(values)
    normed = centered * lax.rsqrt(over_features(centered * centered) + EPSILON) * wide(0) + wide(1)
    r.normed1[...] = normed
    store(r.normed1, r.normed1_hbm)
    loads[1].wait()
    r.keys[pl.ds(8, tokens), :] = dot(r.normed1[...], r.key_weight[...], 1, 0) + narrow(1)
    ahead.greeted()

    def halo_copy():
        return remote(
            r.keys.at[pl.ds(tokens, 8)], r.keys.at[pl.ds(0, 8)], r.halo_send.at[0], r.halo_recv.at[0], me + 1
        )

    @pl.when(jnp.logical_not(last))
    def _():
        halo_copy().start()

    loads[2].wait()
    r.value[...] = dot(r.normed1[...], r.value_weight[...], 1, 0) + narrow(2)

    def mix(start, count):
        total = tap(0) * r.keys[pl.ds(8 + start, count), :]
        for j in range(1, SHIFT):
            total = total + tap(j) * r.keys[pl.ds(8 + start - j, count), :]
        r.shifted[pl.ds(start, count), :] = total
        mixed = total * r.value[pl.ds(start, count), :]
        r.mixed[pl.ds(start, count), :] = mixed
        for b in range(blocks):
            r.rows[b, pl.ds(start, count), :] = mixed[:, features(b)]

    mix(8, tokens - 8)

    @pl.when(first)
    def _():
        r.keys[pl.ds(0, 8), :] = jnp.zeros((8, width), F32)

    @pl.when(jnp.logical_not(first))
    def _():
        halo_copy().wait_recv()

    mix(0, 8)

    for b in range(blocks):
        decay, out_coef = r.decay[:, cut(b)], r.out_coef[:, cut(b)]

        def scan(k, state, b=b, decay=decay, out_coef=out_coef):
            r.starts[k, :, cut(b)] = state
            base = pl.multiple_of(k * CHUNK, CHUNK)
            for j in range(CHUNK):
                state = decay * state + r.rows[b, pl.ds(base + j, 1), :]
                r.part[j] = fold_states(out_coef * state)
            r.out[pl.ds(base, CHUNK), cut(b)] = jnp.sum(r.part[...], axis=1)
            return state

        ahead.send_end(b, lax.fori_loop(0, chunks, scan, jnp.zeros_like(decay)), r.ends, ahead_sems)
    loads[3].wait()
    r.query[...] = dot(r.normed1[...], r.query_weight[...], 1, 0) + narrow(0)
    loads[4].wait()
    loads[5].wait()
    befores = []
    for b in range(blocks):
        befores.append(ahead.group_total(b, r.device_decay[:, cut(b)], r.ends, r.totals, ahead_sems))
        if b < 2:
            r.pre_grad[b] = dot(r.cotangent[...], r.down[pl.ds(b * hidden_half, hidden_half), :], 1, 1)

    cotangent_share = Share(
        ahead, r.cotangent, r.cotangent_peer, r.share_send.at[0], r.share_recv.at[0], x_peer, core, other_core
    )
    normed2_share = Share(
        ahead, r.normed2, r.normed2_peer, r.share_send.at[1], r.share_recv.at[1], y_peer, core, other_core
    )
    normed1_share = Share(
        ahead, r.normed1, r.normed1_x, r.share_send.at[2], r.share_recv.at[2], x_peer, core, other_core
    )
    wide_shares = [
        Share(ahead, source, r.wide_y, r.share_send.at[3], r.share_recv.at[3], y_peer, core, other_core)
        for source in (r.middle_grad, r.normed1)
    ]

    def narrow_copy(source, n, target, peer):
        return remote(source, target, r.half_send.at[n], r.half_recv.at[n], peer)

    def key_copy():
        return narrow_copy(r.key_grad, 4, r.narrow_x, x_peer)

    def query_copy():
        return narrow_copy(r.query_grad, 4, r.narrow_x, x_peer)

    def gated_copy():
        return narrow_copy(r.gated, 5, r.narrow_y, y_peer)

    def value_copy():
        return narrow_copy(r.value_grad, 5, r.narrow_y, y_peer)

    cotangent_share.across().start()

    @pl.when(y == 1)
    def _():
        wide_shares[1].across().start()

    for b in range(blocks):
        decay, out_coef = r.decay[:, cut(b)], r.out_coef[:, cut(b)]
        skip = narrow(3)[:, features(b)]

        def carry(k, state, b=b, decay=decay, out_coef=out_coef, skip=skip):
            r.starts[k, :, cut(b)] = r.starts[k, :, cut(b)] + state
            base = pl.multiple_of(k * CHUNK, CHUNK)
            for j in range(CHUNK):
                state = decay * state
                r.part[j] = fold_states(out_coef * state)
            rows = pl.ds(base, CHUNK)
            out = r.out[rows, cut(b)] + jnp.sum(r.part[...], axis=1) + skip * r.mixed[rows, cut(b)]
            r.out[rows, cut(b)] = out
            r.gated[rows, cut(b)] = r.query[rows, cut(b)] * out
            return state

        incoming = ahead.carried(b, r.device_decay[:, cut(b)], befores[b], r.totals, ahead_sems)
        lax.fori_loop(0, chunks, carry, incoming)
    store(r.gated, r.gated_hbm)

    def core_copy(n, source, target):
        return remote(source, target, r.core_send.at[n], r.core_recv.at[n], me, other_core)

    loads[6].wait()
    merged_copies = []
    for n in range(2):
        rows = pl.ds(n * top, top)
        r.merged[rows, :] = dot(r.gated[rows, :], r.out_weight[...], 1, 0)
        copy = core_copy(n, r.merged.at[rows], r.merged_other.at[rows])
        copy.start()
        merged_copies.append(copy)

    @pl.when(y == 0)
    def _():
        gated_copy().start()

    normed1_share.across().start()
    small_start = STATE // 4
    r.small[...] = jnp.zeros_like(r.small)

    def put(k, row):
        r.small[1, pl.ds(small_start + k // 2, 1), pl.ds(k % 2 * width, width)] = row

    spreads = []
    for n, copy in enumerate(merged_copies):
        rows = pl.ds(n * top, top)
        copy.wait_recv()
        middle = r.tokens[rows, :] + (r.merged[rows, :] + r.merged_other[rows, :]) + wide(2)
        centered = middle - over_features(middle)
        inverse = lax.rsqrt(over_features(centered * centered) + EPSILON)
        scaled = centered * inverse
        r.middle[rows, :] = middle
        r.scaled[rows, :] = scaled
        r.normed2[rows, :] = scaled * wide(3) + wide(4)
        spreads.append(inverse)
    normed2_share.across().start()

    loads[7].wait()
    for n in range(2):
        part = pl.ds(n * hidden_half, hidden_half)
        pre = dot(r.normed2[...], r.up[:, part], 1, 0) + wide(6 + n)
        square = pre * pre
        curve = jnp.tanh(GELU_SCALE * (pre + 0.044715 * (square * pre)))
        r.active[n] = 0.5 * pre * (1.0 + curve)
        slope = 0.5 * (1.0 + curve) + 0.5 * pre * (1.0 - curve * curve) * (
            GELU_SCALE * (1.0 + 3 * 0.044715 * square)
        )
        pre_grad = r.pre_grad[n] * slope
        r.pre_grad[n] = pre_grad
        r.small[0, pl.ds(small_start + 6 + n, 1), :] = over_tokens(pre_grad)
    early = tokens * EARLY // 8

    def half_copies(n):
        rows = (pl.ds(0, early), pl.ds(early, tokens - early))[n]
        return (
            remote(
                r.active.at[1 - x, rows], r.active_peer.at[rows], r.half_send.at[2 * n], r.half_recv.at[2 * n], x_peer
            ),
            remote(
                r.pre_grad.at[1 - y, rows],
                r.pre_grad_peer.at[rows],
                r.half_send.at[2 * n + 1],
                r.half_recv.at[2 * n + 1],
                y_peer,
            ),
        )

    for copy in half_copies(0):
        copy.start()
    r.normed_grad[...] = dot(r.pre_grad[0], r.up[:, pl.ds(0, hidden_half)], 1, 1)
    r.normed_grad[...] = r.normed_grad[...] + dot(r.pre_grad[1], r.up[:, pl.ds(hidden_half, hidden_half)], 1, 1)
    normed_grad_copy = core_copy(2, r.normed_grad, r.normed_grad_other)
    normed_grad_copy.start()
    for n in range(2):
        feed = dot(r.active[n], r.down[pl.ds(n * hidden_half, hidden_half), :], 1, 0)
        if n == 0:
            r.feed[...] = feed
        else:
            r.feed[...] = r.feed[...] + feed
    feed_copy = core_copy(3, r.feed, r.feed_other)
    feed_copy.start()
    normed_grad_copy.wait_recv()
    for n in range(2):
        rows = pl.ds(n * top, top)
        normed_grad = r.normed_grad[rows, :] + r.normed_grad_other[rows, :]
        scaled = r.scaled[rows, :]
        scaled_grad = normed_grad * wide(3)
        centered = scaled_grad - over_features(scaled_grad) - scaled * over_features(scaled_grad * scaled)
        middle_grad = r.cotangent[rows, :] + spreads[n] * centered
        r.middle_grad[rows, :] = middle_grad
        sums = (normed_grad * scaled, normed_grad, middle_grad, r.cotangent[rows, :])
        for k, values in enumerate(sums):
            row = pl.ds(small_start + 2 + k, 1)
            if n == 0:
                r.small[0, row, :] = over_tokens(values)
            else:
                r.small[0, row, :] = r.small[0, row, :] + over_tokens(values)
        r.gated_grad[rows, :] = dot(middle_grad, r.out_weight[...], 1, 1)
    store(r.middle_grad, r.middle_grad_hbm)

    grad = r.gated_grad[...] * r.query[...]
    r.grad[...] = grad
    for b in range(blocks):
        r.grad_rows[b] = grad[:, features(b)]
    for b in range(blocks):
        decay = r.decay[:, cut(b)]

        def end(i, adjoint, b=b, decay=decay):
            base = pl.multiple_of((chunks - 1 - i) * CHUNK, CHUNK)
            for j in range(CHUNK - 1, -1, -1):
                adjoint = decay * adjoint + r.grad_rows[b, pl.ds(base + j, 1), :]
            return adjoint

        back.send_end(b, lax.fori_loop(0, chunks, end, jnp.zeros_like(decay)), r.back_ends, back_sems)
    for copy in half_copies(1):
        copy.start()
    query_grad = r.gated_grad[...] * r.out[...]
    r.query_grad[...] = query_grad
    store(r.query_grad, r.query_grad_hbm)
    put(0, over_tokens(r.grad[...] * r.mixed[...]))
    put(5, over_tokens(query_grad))
    cotangent_share.relay()
    normed1_share.relay()
    normed2_share.relay()
    feed_copy.wait_recv()
    r.block_out[...] = r.middle[...] + (r.feed[...] + r.feed_other[...]) + wide(5)
    store(r.block_out, r.block_out_hbm)
    befores = [
        back.group_total(b, r.device_decay[:, cut(b)], r.back_ends, r.back_totals, back_sems) for b in range(blocks)
    ]

    def product(left_ref, right_ref):
        return dot(left_ref[...], right_ref[...], 0, 0)

    r.down_half[...] = product(r.active.at[x], r.cotangent)

    for b in range(blocks):
        if b == 1:

            @pl.when(y == 0)
            def _():
                wide_shares[0].across().start()

            @pl.when(x == 1)
            def _():
                query_copy().start()

        decay, out_coef = r.decay[:, cut(b)], r.out_coef[:, cut(b)]
        skip = narrow(3)[:, features(b)]
        r.coef[:, cut(b)] = jnp.zeros_like(decay)
        r.slope[:, cut(b)] = jnp.zeros_like(decay)

        def chunk(i, adjoint, b=b, decay=decay, out_coef=out_coef, skip=skip):
            k = chunks - 1 - i
            base = pl.multiple_of(k * CHUNK, CHUNK)
            state = r.starts[k, :, cut(b)]
            for j in range(CHUNK):
                r.state[j] = state
                state = decay * state + r.rows[b, pl.ds(base + j, 1), :]
            coef, slope = r.coef[:, cut(b)], r.slope[:, cut(b)]
            for j in range(CHUNK - 1, -1, -1):
                adjoint = decay * adjoint + r.grad_rows[b, pl.ds(base + j, 1), :]
                r.part[j] = fold_states(out_coef * adjoint)
                coef = coef + adjoint * r.rows[b, pl.ds(base + j, 1), :]
                slope = slope + adjoint * r.state[j]
            r.coef[:, cut(b)] = coef
            r.slope[:, cut(b)] = slope
            rows = pl.ds(base, CHUNK)
            grad_mixed = jnp.sum(r.part[...], axis=1) + skip * r.grad[rows, cut(b)]
            r.shifted_grad[rows, cut(b)] = grad_mixed * r.value[rows, cut(b)]
            r.value_grad[rows, cut(b)] = grad_mixed * r.shifted[rows, cut(b)]
            return adjoint

        incoming = back.carried(b, r.device_decay[:, cut(b)], befores[b], r.back_totals, back_sems)
        lax.fori_loop(0, chunks, chunk, incoming)
    store(r.value_grad, r.value_grad_hbm)

    def head_copy():
        return remote(
            r.shifted_grad.at[pl.ds(0, 8)], r.shifted_grad.at[pl.ds(tokens, 8)], r.halo_send.at[1], r.halo_recv.at[1], me - 1
        )

    @pl.when(jnp.logical_not(first))
    def _():
        head_copy().start()

    @pl.when(y == 1)
    def _():
        value_copy().start()

    for j in range(SHIFT):
        put(1 + j, over_tokens(r.shifted_grad[pl.ds(0, tokens), :] * r.keys[pl.ds(8 - j, tokens), :]))
    put(7, over_tokens(r.value_grad[...]))
    r.up_half[...] = product(r.normed2, r.pre_grad.at[y])

    @pl.when(last)
    def _():
        r.shifted_grad[pl.ds(tokens, 8), :] = jnp.zeros((8, width), F32)

    @pl.when(jnp.logical_not(last))
    def _():
        head_copy().wait_recv()

    key_grad = tap(0) * r.shifted_grad[pl.ds(0, tokens), :]
    for j in range(1, SHIFT):
        key_grad = key_grad + tap(j) * r.shifted_grad[pl.ds(j, tokens), :]
    r.key_grad[...] = key_grad
    store(r.key_grad, r.key_grad_hbm)

    @pl.when(x == 0)
    def _():
        key_copy().start()

    put(6, over_tokens(key_grad))

    for p in range(4):
        rows = pl.ds(p * small_start, small_start)
        coef = r.coef[rows, :]
        rate_grad = r.coef_rate[rows, :] * coef - r.decay[rows, :] * r.out_coef[rows, :] * r.slope[rows, :]
        step_grad = over_tokens(r.rate[rows, :] * rate_grad)
        put(8, step_grad if p == 0 else r.small[1, pl.ds(small_start + 4, 1), pl.ds(0, width)] + step_grad)
        r.small[p, pl.ds(0, small_start), pl.ds(0, width)] = narrow(4) * rate_grad
        r.small[p, pl.ds(0, small_start), pl.ds(width, width)] = r.in_coef[rows, :] * coef
    store(r.small, r.small_hbm)
    wide_shares[0].relay()

    cotangent_share.finish()
    normed2_share.finish()
    halves = half_copies(0) + half_copies(1)
    for copy in halves[::2]:
        copy.wait()
    r.down_half[...] = r.down_half[...] + product(r.active_peer, r.cotangent_peer)
    store(r.down_half, r.down_half_hbm)
    for copy in halves[1::2]:
        copy.wait()
    r.up_half[...] = r.up_half[...] + product(r.normed2_peer, r.pre_grad_peer)
    store(r.up_half, r.up_half_hbm)
    normed1_share.finish()
    wide_shares[0].finish()
    key_copy().wait()
    gated_copy().wait()
    for copy in merged_copies + [normed_grad_copy, feed_copy]:
        copy.wait_send()
    ahead.drain(blocks, r.ends, r.totals, ahead_sems)
    back.drain(blocks, r.back_ends, r.back_totals, back_sems)

    @pl.when(jnp.logical_not(last))
    def _():
        halo_copy().wait_send()

    @pl.when(jnp.logical_not(first))
    def _():
        head_copy().wait_send()

    for copy in stores:
        copy.wait()


def front_call(span, inputs, in_hbm, outs, scratch, sems):
    names = [*inputs, *in_hbm, *outs, *scratch, *sems]
    results = pl.pallas_call(
        functools.partial(front_kernel, names, span),
        in_specs=[pl.BlockSpec(memory_space=pltpu.VMEM)] * len(inputs)
        + [pl.BlockSpec(memory_space=pltpu.HBM)] * len(in_hbm),
        out_specs=[pl.BlockSpec(memory_space=pltpu.HBM)] * len(outs),
        out_shape=[shape(*dims) for dims in outs.values()],
        scratch_shapes=[pltpu.VMEM(dims, F32) for dims in scratch.values()]
        + [pltpu.SemaphoreType.DMA(dims) for dims in sems.values()],
        compiler_params=pltpu.CompilerParams(collective_id=1, has_side_effects=True, vmem_limit_bytes=60 * 2**20),
        name="front",
    )(*inputs.values(), *in_hbm.values())
    return types.SimpleNamespace(**dict(zip(outs, results)))


MESH = pl.DeviceIdType.MESH


def is_far(i):
    return lax.rem(i, 5) == 1


class Plan:
    def __init__(self, feed_rows, mixer_rows, rows):
        self.rows = rows
        self.feed, self.mixer = feed_rows // rows, mixer_rows // 2 // rows
        self.small_rows = STATE // 4 + 8
        self.pieces = self.feed + self.mixer + -(-self.small_rows // rows)
        self.total = self.pieces * rows
        self.feed_rows, self.mixer_rows = feed_rows, mixer_rows


def sum_kernel(
    length, plan, lag,
    small_ref, gain_ref, up_half_ref, down_half_ref, normed_hbm, middle_grad_hbm, gated_hbm, query_grad_hbm, key_grad_hbm,
    value_grad_hbm, normed_x_hbm, narrow_x_hbm, wide_y_hbm, narrow_y_hbm, tokens_hbm, query_hbm, key_hbm, value_hbm,
    out_ref, input_grad_ref,
    normed_ref, middle_grad_ref, gated_ref, query_grad_ref, key_grad_ref, value_grad_ref,
    normed_x_ref, narrow_x_ref, wide_y_ref, narrow_y_ref, tokens_ref,
    sum_ref, got_ref, feed_got_ref, keep_ref, send_ref, mixer_got_ref, small_got_ref, small_sum_ref, weights_ref, local_ref,
    other_ref,
    load_sem, store_sem, chain_send, chain_recv, z_send, z_recv, side_send, side_recv, feed_send, feed_recv,
    mixer_send, mixer_recv, small_send, small_recv, core_send, core_recv
):
    me = lax.axis_index("seq")
    core = lax.axis_index("tp")
    place, quarter = me // 4, lax.rem(me, 4)
    x, y = lax.rem(quarter, 2), quarter // 2
    x_peer, y_peer = me + 1 - 2 * x, me + 2 - 4 * y
    quarter_x, quarter_y, quarter_d = quarter + 1 - 2 * x, quarter + 2 - 4 * y, 3 - quarter
    rows, pieces = plan.rows, plan.pieces
    width = gated_ref.shape[1]
    first = lag * (length - 1)
    spread = SPREAD
    started = (place, length - 1 - place)
    ahead = (me + 4, me - 4)
    behind = (me - 4, me + 4)
    side_peers = (x_peer, y_peer)
    side_bits = (x, y)
    halves = (up_half_ref, down_half_ref)
    barrier = pltpu.get_barrier_semaphore()

    def greet(peer):
        pl.semaphore_signal(barrier, inc=1, device_id={"seq": peer}, device_id_type=MESH)

    greet(x_peer)
    greet(y_peer)
    pl.semaphore_signal(barrier, inc=1, device_id={"tp": 1 - core}, device_id_type=MESH)
    pl.when(place > 0)(lambda: greet(me - 4))
    pl.when(place < length - 1)(lambda: greet(me + 4))
    pairs = [
        (half_ref.at[pl.ds(pl.multiple_of(bit * plan.feed_rows, 8), plan.feed_rows)], sum_ref.at[d, pl.ds(0, plan.feed_rows)])
        for d, (half_ref, bit) in enumerate(zip(halves, side_bits))
    ]
    pairs += [
        (normed_hbm, normed_ref),
        (query_grad_hbm, query_grad_ref),
        (key_grad_hbm, key_grad_ref),
        (normed_x_hbm, normed_x_ref),
        (narrow_x_hbm, narrow_x_ref),
        (gated_hbm, gated_ref),
        (value_grad_hbm, value_grad_ref),
        (middle_grad_hbm, middle_grad_ref),
        (wide_y_hbm, wide_y_ref),
        (narrow_y_hbm, narrow_y_ref),
        (tokens_hbm, tokens_ref),
        (query_hbm, weights_ref.at[0]),
        (key_hbm, weights_ref.at[1]),
        (value_hbm, weights_ref.at[2]),
    ]
    loads = [pltpu.make_async_copy(source, target, load_sem.at[n]) for n, (source, target) in enumerate(pairs)]
    for load in loads:
        load.start()
    pl.semaphore_wait(barrier, 3 + (place > 0).astype(jnp.int32) + (place < length - 1).astype(jnp.int32))

    def remote(source, target, send, recv, peer):
        return pltpu.make_async_remote_copy(
            src_ref=source,
            dst_ref=target,
            send_sem=send,
            recv_sem=recv,
            device_id={"seq": peer},
            device_id_type=MESH,
        )

    def at(i):
        return pl.ds(pl.multiple_of(i * rows, 8), rows)

    def feed_copy(d, i):
        source = pl.ds(pl.multiple_of((1 - side_bits[d]) * plan.feed_rows + i * rows, 8), rows)
        return remote(
            halves[d].at[source], feed_got_ref.at[d, at(i)], feed_send.at[d, i], feed_recv.at[d, i], side_peers[d]
        )

    def send_feed(i, _):
        for d in range(2):
            feed_copy(d, i).start()
        return 0

    lax.fori_loop(0, min(WINDOW, plan.feed), send_feed, 0)

    def features(ref, h):
        return ref[:, pl.ds(pl.multiple_of(h * width, LANES), width)]

    def query_or_key(h):
        narrow = jnp.where(x == 0, query_grad_ref[...], key_grad_ref[...])
        return dot(features(normed_ref, h), narrow, 0, 0) + dot(features(normed_x_ref, h), narrow_x_ref[...], 0, 0)

    def value_or_out(h):
        left = jnp.where(y == 0, features(normed_ref, h), gated_ref[...])
        right = jnp.where(y == 0, value_grad_ref[...], features(middle_grad_ref, h))
        wide, narrow = features(wide_y_ref, h), narrow_y_ref[...]
        return dot(left, right, 0, 0) + dot(jnp.where(y == 0, wide, narrow), jnp.where(y == 0, narrow, wide), 0, 0)

    mixer_copies = [
        remote(send_ref.at[n], mixer_got_ref.at[n], mixer_send.at[n], mixer_recv.at[n], peer)
        for n, peer in enumerate((y_peer, x_peer))
    ]
    for load in loads:
        load.wait()

    def send_mixer():
        send_ref[0] = query_or_key(1 - y)
        mixer_copies[0].start()
        send_ref[1] = value_or_out(1 - x)
        mixer_copies[1].start()


    def chain_copy(d, i):
        return remote(
            sum_ref.at[d, at(i)], got_ref.at[d, at(i)], chain_send.at[d, i], chain_recv.at[d, i], ahead[d]
        )

    def z_copy(d, i, k):
        ref = out_ref.at[(quarter, quarter_x, quarter_y, quarter_d)[k], d, at(i)]
        return remote(ref, ref, z_send.at[d, i, k], z_recv.at[d, i, k], behind[d])

    def side_copy(d, i, k):
        even = lax.rem(i, 2) == 0
        source = (quarter, quarter, jnp.where(even, quarter_x, quarter_y))[k]
        peer = (x_peer, y_peer, jnp.where(even, y_peer, x_peer))[k]
        ref = out_ref.at[source, d, at(i)]
        return remote(ref, ref, side_send.at[d, i, k], side_recv.at[d, i, k], peer)

    def chain_step(d, i):
        @pl.when(i < plan.feed)
        def _():
            feed_copy(d, i).wait_recv()
            sum_ref[d, at(i)] = sum_ref[d, at(i)] + feed_got_ref[d, at(i)]

        @pl.when(started[d] > 0)
        def _():
            chain_copy(d, i).wait_recv()
            sum_ref[d, at(i)] = sum_ref[d, at(i)] + got_ref[d, at(i)]

        @pl.when(started[d] < length - 1)
        def _():
            chain_copy(d, i).start()

        @pl.when(started[d] == length - 1)
        def _():
            store = pltpu.make_async_copy(sum_ref.at[d, at(i)], out_ref.at[quarter, d, at(i)], store_sem.at[d, i])
            store.start()
            store.wait()

    def kind(d, i):
        remaining = length - 1 - started[d]
        far = is_far(i)
        sideways = jnp.logical_or(jnp.logical_not(far), remaining == 0)
        onward = jnp.logical_and(far, remaining < length - 1)
        return remaining, sideways, onward

    def own_step(d, i):
        remaining, sideways, _ = kind(d, i)

        @pl.when(remaining > 0)
        def _():
            z_copy(d, i, 0).wait_recv()

        @pl.when(remaining < length - 1)
        def _():
            z_copy(d, i, 0).start()

        @pl.when(sideways)
        def _():
            side_copy(d, i, 0).start()
            side_copy(d, i, 1).start()

    def side_step(d, i):
        _, sideways, onward = kind(d, i)

        @pl.when(sideways)
        def _():
            side_copy(d, i, 0).wait_recv()
            side_copy(d, i, 1).wait_recv()
            side_copy(d, i, 2).start()

        @pl.when(jnp.logical_not(sideways))
        def _():
            z_copy(d, i, 1).wait_recv()
            z_copy(d, i, 2).wait_recv()

        @pl.when(onward)
        def _():
            z_copy(d, i, 1).start()
            z_copy(d, i, 2).start()

    def last_step(d, i):
        _, sideways, onward = kind(d, i)

        @pl.when(sideways)
        def _():
            side_copy(d, i, 2).wait_recv()

        @pl.when(jnp.logical_not(sideways))
        def _():
            z_copy(d, i, 3).wait_recv()

        @pl.when(onward)
        def _():
            z_copy(d, i, 3).start()

    def tick(t, _):
        @pl.when(t + WINDOW < plan.feed)
        def _():
            send_feed(t + WINDOW, 0)

        steps = ((chain_step, 0), (own_step, first), (last_step, first + SIDE + LAST), (side_step, first + SIDE))
        for step, late in steps:
            for d in range(2):
                passed = lag * started[d] if step is chain_step else spread * (length - 1 - started[d])
                i = t - late - passed
                pl.when(jnp.logical_and(i >= 0, i < pieces))(functools.partial(step, d, i))
        return 0

    core_copy = pltpu.make_async_remote_copy(
        src_ref=local_ref,
        dst_ref=other_ref,
        send_sem=core_send.at[0],
        recv_sem=core_recv.at[0],
        device_id={"tp": 1 - core},
        device_id_type=MESH,
    )
    small_x = remote(
        small_sum_ref.at[1 - x], small_got_ref.at[pl.ds(0, 2)], small_send.at[0], small_recv.at[0], x_peer
    )
    small_y = remote(
        small_sum_ref.at[x, 1 - y], small_got_ref.at[2], small_send.at[1], small_recv.at[1], y_peer
    )

    def normed_grad():
        local_ref[...] = (
            dot(query_grad_ref[...], weights_ref[0], 1, 1)
            + dot(key_grad_ref[...], weights_ref[1], 1, 1)
            + dot(value_grad_ref[...], weights_ref[2], 1, 1)
        )
        core_copy.start()

    def first_norm():
        core_copy.wait_recv()
        grad = local_ref[...] + other_ref[...]
        values = tokens_ref[...]
        centered = values - over_features(values)
        inverse = lax.rsqrt(over_features(centered * centered) + EPSILON)
        scaled = centered * inverse
        scaled_grad = grad * gain_ref[...].reshape(1, -1)
        scaled_grad = scaled_grad - over_features(scaled_grad) - scaled * over_features(scaled_grad * scaled)
        input_grad_ref[...] = middle_grad_ref[...] + inverse * scaled_grad
        for p in range(4):
            small_sum_ref[p // 2, p % 2] = small_ref[p]
        small_sum_ref[0, 0, pl.ds(STATE // 4, 1), :] = over_tokens(grad * scaled)
        small_sum_ref[0, 0, pl.ds(STATE // 4 + 1, 1), :] = over_tokens(grad)
        small_x.start()

    def keep_mixer():
        keep_ref[0] = query_or_key(y)
        keep_ref[1] = value_or_out(x)

    def add_small():
        small_x.wait()
        small_sum_ref[x] = small_sum_ref[x] + small_got_ref[pl.ds(0, 2)]
        small_y.start()

    def mixer_sums():
        for copy in mixer_copies:
            copy.wait_recv()
        count = plan.mixer_rows // 2
        for d in range(2):
            source, target = pl.ds(d * count, count), pl.ds(plan.feed_rows, count)
            for n in range(2):
                sum_ref[d, target, pl.ds(n * width, width)] = keep_ref[n, source, :] + mixer_got_ref[n, source, :]

    def small_sums():
        small_y.wait()
        start = plan.feed_rows + plan.mixer_rows // 2
        sum_ref[:, pl.ds(start, plan.total - start), :] = jnp.zeros((2, plan.total - start, sum_ref.shape[2]), F32)
        sum_ref[0, pl.ds(start, plan.small_rows), :] = small_sum_ref[x, y] + small_got_ref[2]

    stages = (
        (1, (send_mixer,)),
        (2, (normed_grad,)),
        (5, (first_norm,)),
        (8, (keep_mixer, add_small)),
        (plan.feed, (mixer_sums, small_sums)),
    )
    at_tick = 0
    for until, work in stages:
        lax.fori_loop(at_tick, until, tick, 0)
        at_tick = until
        for piece in work:
            piece()
    lax.fori_loop(at_tick, first + spread * (length - 1) + SIDE + LAST + pieces, tick, 0)

    def drain(i, _):
        for d in range(2):
            remaining, sideways, onward = kind(d, i)
            pl.when(i < plan.feed)(lambda: feed_copy(d, i).wait_send())
            pl.when(remaining > 0)(lambda: chain_copy(d, i).wait_send())
            pl.when(remaining < length - 1)(lambda: z_copy(d, i, 0).wait_send())

            @pl.when(onward)
            def _():
                for k in range(1, 4):
                    z_copy(d, i, k).wait_send()

            @pl.when(sideways)
            def _():
                for k in range(3):
                    side_copy(d, i, k).wait_send()

        return 0

    lax.fori_loop(0, pieces, drain, 0)
    for copy in mixer_copies + [core_copy]:
        copy.wait_send()


def summed_quarters(plan, lag, args, in_hbm, collective_id):
    length = lax.axis_size("seq") // 4
    pieces, feed = plan.pieces, plan.feed
    tokens, columns = args[4].shape
    width = args[6].shape[1]
    sems = [(16,), (2, pieces), (2, pieces), (2, pieces), (2, pieces, 4), (2, pieces, 4), (2, pieces, 3), (2, pieces, 3)]
    sems += [(2, feed), (2, feed), (2,), (2,), (2,), (2,), (1,), (1,)]
    wide, narrow = (tokens, columns), (tokens, width)
    scratch = [wide, wide, narrow, narrow, narrow, narrow, wide, narrow, wide, narrow, wide]
    scratch += [(2, plan.total, columns)] * 2 + [(2, plan.feed_rows, columns)] + [(2, plan.mixer_rows, width)] * 3
    scratch += [(3, plan.small_rows, columns), (2, 2, plan.small_rows, columns), (3, columns, width)] + [(tokens, columns)] * 2
    return pl.pallas_call(
        functools.partial(sum_kernel, length, plan, lag),
        out_shape=[shape(4, 2, plan.total, columns), shape(tokens, columns)],
        in_specs=[pl.BlockSpec(memory_space=pltpu.HBM if n in in_hbm else pltpu.VMEM) for n in range(len(args))],
        out_specs=[pl.BlockSpec(memory_space=pltpu.HBM), pl.BlockSpec(memory_space=pltpu.VMEM)],
        scratch_shapes=[pltpu.VMEM(dims, F32) for dims in scratch] + [pltpu.SemaphoreType.DMA(dims) for dims in sems],
        compiler_params=pltpu.CompilerParams(
            collective_id=collective_id, has_side_effects=True, vmem_limit_bytes=60 * 2**20
        ),
        name="gradient_sums",
    )(*args)


def unpack_kernel(plan, sums_hbm, block_hbm, grad_hbm, *refs):
    (
        up_ref, down_ref, query_ref, key_ref, value_ref, out_ref, rate_ref, state_out_ref, block_out_ref, input_grad_ref,
        *vector_refs, sums_ref, rows_ref, load_sem, store_sem
    ) = refs
    columns, width = up_ref.shape[0], query_ref.shape[1]
    feed, count, state = plan.feed_rows, plan.mixer_rows // 2, STATE // 4
    loads, stores = [], []

    def load(source, target):
        loads.append(pltpu.make_async_copy(source, target, load_sem.at[len(loads)]))
        loads[-1].start()

    def store(source, target):
        stores.append(pltpu.make_async_copy(source, target, store_sem.at[len(stores)]))
        stores[-1].start()

    def span(start, size):
        return pl.ds(start, size)

    quarters = [(x, y, 2 * y + x) for x in range(2) for y in range(2)]
    for part in (span(feed, plan.total - feed), span(0, feed)):
        for _, _, q in quarters:
            for d in range(2):
                load(sums_hbm.at[q, d, part], sums_ref.at[q, d, part])
    load(block_hbm, rows_ref.at[0])
    load(grad_hbm, rows_ref.at[1])
    waiting = iter(loads)
    for x, y, q in quarters:
        for d in range(2):
            next(waiting).wait()
            mixer = sums_ref.at[q, d, span(feed, count)]
            target = (query_ref, key_ref)[x]
            store(mixer.at[:, span(0, width)], target.at[span((2 * y + d) * count, count)])
            if y == 0:
                target = value_ref.at[span((2 * x + d) * count, count)]
            else:
                target = out_ref.at[span(d * count, count), span(x * width, width)]
            store(mixer.at[:, span(width, width)], target)
        rows = span((2 * x + y) * state, state)
        last = sums_ref.at[q, 0, span(feed + count, state)]
        store(last.at[:, span(0, width)], rate_ref.at[rows])
        store(last.at[:, span(width, width)], state_out_ref.at[rows])
    for x, y, q in quarters:
        next(waiting).wait()
        store(sums_ref.at[q, 0, span(0, feed)], up_ref.at[span(x * feed, feed), span(y * columns, columns)])
        next(waiting).wait()
        store(sums_ref.at[q, 1, span(0, feed)], down_ref.at[span((2 * x + y) * feed, feed)])
    for n, target in enumerate((block_out_ref, input_grad_ref)):
        next(waiting).wait()
        store(rows_ref.at[n], target)
    *wide_refs, up_bias_ref, skip_ref, taps_ref, query_bias_ref, key_bias_ref, value_bias_ref, step_ref = vector_refs
    row = feed + count + state

    def narrow(k):
        return sums_ref[2, 0, row + k // 2, pl.ds(k % 2 * width, width)]

    for k, ref in enumerate(wide_refs):
        ref[...] = sums_ref[0, 0, row + k, :]
    for k in range(2):
        up_bias_ref[pl.ds(k * columns, columns)] = sums_ref[0, 0, row + 6 + k, :]
    for k in range(SHIFT):
        taps_ref[k, :] = narrow(1 + k)
    for k, ref in ((0, skip_ref), (5, query_bias_ref), (6, key_bias_ref), (7, value_bias_ref), (8, step_ref)):
        ref[...] = narrow(k)
    for item in stores:
        item.wait()


def unpacked(plan, args, matrices, vectors):
    return pl.pallas_call(
        functools.partial(unpack_kernel, plan),
        out_shape=[shape(*out.shape) for out in (*matrices, *args[1:], *vectors)],
        in_specs=[pl.BlockSpec(memory_space=pltpu.HBM)] * 3,
        out_specs=[pl.BlockSpec(memory_space=pltpu.HBM)] * (len(matrices) + 2)
        + [pl.BlockSpec(memory_space=pltpu.VMEM)] * len(vectors),
        scratch_shapes=[
            pltpu.VMEM(args[0].shape, F32),
            pltpu.VMEM((2, *args[1].shape), F32),
            pltpu.SemaphoreType.DMA((18,)),
            pltpu.SemaphoreType.DMA((34,)),
        ],
        compiler_params=pltpu.CompilerParams(vmem_limit_bytes=60 * 2**20),
        name="unpack",
    )(*args)


def on_device(
    tokens,
    cotangent,
    norm1_gain,
    norm1_bias,
    query_weight,
    query_bias,
    key_weight,
    key_bias,
    value_weight,
    value_bias,
    shift_kernel,
    log_step,
    state_rate,
    state_out,
    skip_gain,
    out_weight,
    out_bias,
    norm2_gain,
    norm2_bias,
    up_weight,
    up_bias,
    down_weight,
    down_bias,
):
    rows, columns = tokens.shape
    width = query_weight.shape[1]
    hidden = up_weight.shape[1]
    span = lax.axis_size("seq") // SEQS
    blocks, groups = width // LANES, span // 4
    plan = Plan(columns // 2, width, PIECE_ROWS)
    tok, wide_tok, state, row_blocks = (rows, width), (rows, columns), (STATE, width), (blocks, rows, LANES)
    hidden_tok = (rows, hidden // 2)
    ends, totals = (4, STATE, width), (groups, STATE, width)
    end_sems, total_sems = (blocks, 3), (blocks, max(1, groups - 1))
    front = front_call(
        span,
        dict(
            norm1_gain=norm1_gain,
            norm1_bias=norm1_bias,
            query_bias=query_bias,
            key_bias=key_bias,
            value_bias=value_bias,
            taps=shift_kernel,
            log_step=log_step,
            state_rate=state_rate,
            state_out=state_out,
            skip_gain=skip_gain,
            out_bias=out_bias,
            norm2_gain=norm2_gain,
            norm2_bias=norm2_bias,
            up_bias=up_bias,
            down_bias=down_bias,
        ),
        dict(
            tokens_hbm=tokens,
            key_hbm=key_weight,
            value_hbm=value_weight,
            query_hbm=query_weight,
            cotangent_hbm=cotangent,
            down_hbm=down_weight,
            out_hbm=out_weight,
            up_hbm=up_weight,
        ),
        dict(
            block_out_hbm=wide_tok,
            middle_grad_hbm=wide_tok,
            normed1_hbm=wide_tok,
            gated_hbm=tok,
            query_grad_hbm=tok,
            key_grad_hbm=tok,
            value_grad_hbm=tok,
            small_hbm=(4, plan.small_rows, columns),
            down_half_hbm=(hidden // 2, columns),
            up_half_hbm=(columns, hidden // 2),
            normed1_x=wide_tok,
            narrow_x=tok,
            wide_y=wide_tok,
            narrow_y=tok,
        ),
        dict(
            tokens=wide_tok,
            cotangent=wide_tok,
            key_weight=key_weight.shape,
            value_weight=value_weight.shape,
            query_weight=query_weight.shape,
            out_weight=out_weight.shape,
            up=up_weight.shape,
            down=down_weight.shape,
            normed1=wide_tok,
            keys=(rows + 8, width),
            value=tok,
            query=tok,
            shifted=tok,
            mixed=tok,
            out=tok,
            gated=tok,
            rows=row_blocks,
            grad_rows=row_blocks,
            starts=(rows // CHUNK, STATE, width),
            part=(CHUNK, 8, LANES),
            state=(CHUNK, STATE, LANES),
            ends=ends,
            totals=totals,
            back_ends=ends,
            back_totals=totals,
            merged=wide_tok,
            merged_other=wide_tok,
            middle=wide_tok,
            scaled=wide_tok,
            normed2=wide_tok,
            active=(2, *hidden_tok),
            pre_grad=(2, *hidden_tok),
            normed_grad=wide_tok,
            normed_grad_other=wide_tok,
            feed=wide_tok,
            feed_other=wide_tok,
            active_peer=hidden_tok,
            pre_grad_peer=hidden_tok,
            cotangent_peer=wide_tok,
            normed2_peer=wide_tok,
            middle_grad=wide_tok,
            gated_grad=tok,
            grad=tok,
            query_grad=tok,
            key_grad=tok,
            value_grad=tok,
            shifted_grad=(rows + 8, width),
            coef=state,
            slope=state,
            wide=(8, columns),
            narrow=(16, width),
            rate=state,
            decay=state,
            in_coef=state,
            out_coef=state,
            device_decay=state,
            coef_rate=state,
            small=(4, plan.small_rows, columns),
            block_out=wide_tok,
            down_half=(hidden // 2, columns),
            up_half=(columns, hidden // 2),
        ),
        dict(
            end_send=end_sems,
            end_recv=end_sems,
            total_send=total_sems,
            total_recv=total_sems,
            back_end_send=end_sems,
            back_end_recv=end_sems,
            back_total_send=total_sems,
            back_total_recv=total_sems,
            halo_send=(2,),
            halo_recv=(2,),
            load_sem=(8,),
            store_sem=(10,),
            core_send=(4,),
            core_recv=(4,),
            half_send=(6,),
            half_recv=(6,),
            share_send=(4, 2),
            share_recv=(4, 2),
        ),
    )
    sums, input_grad = summed_quarters(
        plan,
        LAG,
        (front.small_hbm, norm1_gain, front.up_half_hbm, front.down_half_hbm, front.normed1_hbm)
        + (front.middle_grad_hbm, front.gated_hbm, front.query_grad_hbm, front.key_grad_hbm, front.value_grad_hbm)
        + (front.normed1_x, front.narrow_x, front.wide_y, front.narrow_y, tokens, query_weight, key_weight, value_weight),
        range(2, 18),
        3,
    )
    (
        grad_up_weight,
        grad_down_weight,
        grad_query_weight,
        grad_key_weight,
        grad_value_weight,
        grad_out_weight,
        grad_state_rate,
        grad_state_out,
        block_out,
        input_grad,
        grad_norm1_gain,
        grad_norm1_bias,
        grad_norm2_gain,
        grad_norm2_bias,
        grad_out_bias,
        grad_down_bias,
        grad_up_bias,
        grad_skip_gain,
        grad_shift_kernel,
        grad_query_bias,
        grad_key_bias,
        grad_value_bias,
        grad_log_step,
    ) = unpacked(
        plan,
        (sums, front.block_out_hbm, input_grad),
        (up_weight, down_weight, query_weight, key_weight, value_weight, out_weight, state_rate, state_out),
        (norm1_gain, norm1_bias, norm2_gain, norm2_bias, out_bias, down_bias, up_bias, skip_gain, shift_kernel)
        + (query_bias, key_bias, value_bias, log_step),
    )
    return (
        block_out,
        input_grad,
        grad_norm1_gain,
        grad_norm1_bias,
        grad_query_weight,
        grad_query_bias,
        grad_key_weight,
        grad_key_bias,
        grad_value_weight,
        grad_value_bias,
        grad_shift_kernel,
        grad_log_step,
        grad_state_rate,
        grad_state_out,
        grad_skip_gain,
        grad_out_weight,
        grad_out_bias,
        grad_norm2_gain,
        grad_norm2_bias,
        grad_up_weight,
        grad_up_bias,
        grad_down_weight,
        grad_down_bias,
    )


def solution(mesh):
    return jax.shard_map(
        on_device,
        mesh=mesh,
        in_specs=(
            P("seq", None),
            P("seq", None),
            P(),
            P(),
            P(None, "tp"),
            P("tp"),
            P(None, "tp"),
            P("tp"),
            P(None, "tp"),
            P("tp"),
            P(None, "tp"),
            P("tp"),
            P(None, "tp"),
            P(None, "tp"),
            P("tp"),
            P("tp", None),
            P(),
            P(),
            P(),
            P(None, "tp"),
            P("tp"),
            P("tp", None),
            P(),
        ),
        out_specs=(
            P("seq", None),
            P("seq", None),
            P(),
            P(),
            P(None, "tp"),
            P("tp"),
            P(None, "tp"),
            P("tp"),
            P(None, "tp"),
            P("tp"),
            P(None, "tp"),
            P("tp"),
            P(None, "tp"),
            P(None, "tp"),
            P("tp"),
            P("tp", None),
            P(),
            P(),
            P(),
            P(None, "tp"),
            P("tp"),
            P("tp", None),
            P(),
        ),
        check_vma=False,
    )
```

```python
import functools
import types

import jax
import jax.numpy as jnp
from jax import lax
from jax.experimental import pallas as pl
from jax.experimental.pallas import tpu as pltpu
from jax.sharding import PartitionSpec as P

SHIFT = 4
SEQS = 2
STATE = 64
LANES = 128
CHUNK = 32
PIECE_ROWS = 24
LAG = 2
SPREAD = 2
SIDE = 4
LAST = 6
WINDOW = 3
EARLY = 2
GELU_SCALE = (2.0 / 3.141592653589793) ** 0.5

EPSILON = 1e-05
F32 = jnp.float32
PRECISION = lax.Precision.HIGH


def shape(*dims):
    return jax.ShapeDtypeStruct(dims, F32)


def fold_states(values):
    return jnp.sum(values.reshape(STATE // 8, 8, LANES), axis=0)


def cut(block):
    return pl.ds(block * LANES, LANES)


class Sequence:
    def __init__(self, span, backward):
        self.me = lax.axis_index("seq")
        self.span = span
        self.place = lax.rem(self.me, span)
        self.start = self.me - self.place
        self.groups = span // 4
        self.quarter, self.group = lax.rem(self.place, 4), self.place // 4
        if backward:
            self.rank, self.turn = 3 - self.quarter, self.groups - 1 - self.group
        else:
            self.rank, self.turn = self.quarter, self.group
        self.backward = backward

    def greet(self, other_core):
        barrier = pltpu.get_barrier_semaphore()
        for k in range(1, self.span):
            peer = self.start + lax.rem(self.place + k, self.span)
            pl.semaphore_signal(barrier, inc=1, device_id={"seq": peer}, device_id_type=pl.DeviceIdType.MESH)
        pl.semaphore_signal(barrier, inc=1, device_id={"tp": other_core}, device_id_type=pl.DeviceIdType.MESH)

    def greeted(self):
        pl.semaphore_wait(pltpu.get_barrier_semaphore(), self.span)

    def remote(self, source, target, send, recv, peer, core=None):
        return pltpu.make_async_remote_copy(
            src_ref=source,
            dst_ref=target,
            send_sem=send,
            recv_sem=recv,
            device_id={"seq": peer} if core is None else {"tp": core},
            device_id_type=pl.DeviceIdType.MESH,
        )

    def end_copy(self, b, k, ends_ref, sems):
        other = lax.rem(self.quarter + k, 4)
        peer = self.me - self.quarter + other
        ref = ends_ref.at[self.rank, :, cut(b)]
        return self.remote(ref, ref, sems[0].at[b, k - 1], sems[1].at[b, k - 1], peer)

    def total_copy(self, b, k, totals_ref, sems):
        peer = self.me - 4 * k if self.backward else self.me + 4 * k
        ref = totals_ref.at[self.turn, :, cut(b)]
        return self.remote(ref, ref, sems[2].at[b, k - 1], sems[3].at[b, k - 1], peer)

    def send_end(self, b, end, ends_ref, sems):
        ends_ref[self.rank, :, cut(b)] = end
        for k in range(1, 4):
            self.end_copy(b, k, ends_ref, sems).start()

    def group_total(self, b, decay, ends_ref, totals_ref, sems):
        for k in range(1, 4):
            self.end_copy(b, k, ends_ref, sems).wait_recv()
        before = jnp.zeros_like(decay)
        total = ends_ref[0, :, cut(b)]
        for r in range(3):
            before = jnp.where(self.rank > r, before * decay + ends_ref[r, :, cut(b)], before)
            total = total * decay + ends_ref[r + 1, :, cut(b)]
        if self.groups > 1:
            totals_ref[self.turn, :, cut(b)] = total
            for k in range(1, self.groups):
                pl.when(self.turn + k < self.groups)(lambda: self.total_copy(b, k, totals_ref, sems).start())
        return before

    def carried(self, b, decay, before, totals_ref, sems):
        if self.groups == 1:
            return before
        square = decay * decay
        fourth = square * square
        carry = jnp.zeros_like(decay)
        for h in range(self.groups - 1):
            for k in range(1, self.groups - h):
                pl.when(self.turn == h + k)(lambda: self.total_copy(b, k, totals_ref, sems).wait_recv())
        for h in range(self.groups - 1):
            carry = jnp.where(self.turn > h, carry * fourth + totals_ref[h, :, cut(b)], carry)
        for r in range(3):
            carry = jnp.where(self.rank > r, carry * decay, carry)
        return before + carry

    def drain(self, blocks, ends_ref, totals_ref, sems):
        for b in range(blocks):
            for k in range(1, 4):
                self.end_copy(b, k, ends_ref, sems).wait_send()
            for k in range(1, self.groups):
                pl.when(self.turn + k < self.groups)(lambda: self.total_copy(b, k, totals_ref, sems).wait_send())


def dot(left, right, left_axis, right_axis):
    return lax.dot_general(
        left, right, (((left_axis,), (right_axis,)), ((), ())), precision=PRECISION, preferred_element_type=F32
    )


def over_tokens(values):
    return jnp.sum(values, axis=0, keepdims=True)


def over_features(values):
    return jnp.mean(values, axis=1, keepdims=True)


class Share:
    def __init__(self, seq, source_ref, target_ref, send, recv, peer, core, other_core):
        self.source_ref, self.target_ref, self.send, self.recv = source_ref, target_ref, send, recv
        self.seq, self.peer, self.core, self.other_core = seq, peer, core, other_core
        size = source_ref.shape[0] // 2
        self.mine = pl.ds(pl.multiple_of(core * size, 8), size)

    def across(self):
        return self.seq.remote(
            self.source_ref.at[self.mine], self.target_ref.at[self.mine], self.send.at[0], self.recv.at[0], self.peer
        )

    def between(self):
        ref = self.target_ref.at[self.mine]
        return self.seq.remote(ref, ref, self.send.at[1], self.recv.at[1], self.seq.me, self.other_core)

    def relay(self):
        self.across().wait_recv()
        self.between().start()

    def finish(self):
        self.between().wait_recv()
        self.across().wait_send()
        self.between().wait_send()


def one_less_exp(values):
    series = jnp.ones_like(values)
    for k in range(8, 1, -1):
        series = 1.0 - values * series * (1.0 / k)
    return jnp.where(values < 0.25, values * series, 1.0 - jnp.exp(-values))


def front_kernel(names, span, *refs):
    r = types.SimpleNamespace(**dict(zip(names, refs)))
    tokens, width = r.gated.shape
    hidden_half = r.up.shape[1] // 2
    blocks, chunks, top = width // LANES, tokens // CHUNK, tokens // 2
    ahead, back = Sequence(span, False), Sequence(span, True)
    ahead_sems = (r.end_send, r.end_recv, r.total_send, r.total_recv)
    back_sems = (r.back_end_send, r.back_end_recv, r.back_total_send, r.back_total_recv)
    me, remote = ahead.me, ahead.remote
    x, y = lax.rem(me, 2), lax.rem(me // 2, 2)
    x_peer, y_peer = me + 1 - 2 * x, me + 2 - 4 * y
    core = lax.axis_index("tp")
    other_core = 1 - core
    first, last = ahead.place == 0, ahead.place == span - 1

    pairs = (
        (r.tokens_hbm, r.tokens),
        (r.key_hbm, r.key_weight),
        (r.value_hbm, r.value_weight),
        (r.query_hbm, r.query_weight),
        (r.cotangent_hbm, r.cotangent),
        (r.down_hbm, r.down),
        (r.out_hbm, r.out_weight),
        (r.up_hbm, r.up),
    )
    loads = [pltpu.make_async_copy(source, target, r.load_sem.at[n]) for n, (source, target) in enumerate(pairs)]
    for load in loads:
        load.start()
    ahead.greet(other_core)
    vectors = (r.norm1_gain, r.norm1_bias, r.out_bias, r.norm2_gain, r.norm2_bias, r.down_bias)
    for k, vector in enumerate(vectors):
        r.wide[k : k + 1, :] = vector[...].reshape(1, -1)
    for k in range(2):
        r.wide[6 + k : 7 + k, :] = r.up_bias[pl.ds(k * hidden_half, hidden_half)].reshape(1, -1)
    for k, vector in enumerate((r.query_bias, r.key_bias, r.value_bias, r.skip_gain)):
        r.narrow[k : k + 1, :] = vector[...].reshape(1, -1)
    step = jnp.exp(r.log_step[...].reshape(1, -1))
    r.narrow[4:5, :] = step
    r.narrow[5 : 5 + SHIFT, :] = r.taps[...]
    rate = step * r.state_rate[...]
    decay = jnp.exp(-rate)
    in_coef = jnp.sqrt(one_less_exp(2.0 * rate))
    out_coef = in_coef * r.state_out[...]
    r.rate[...] = rate
    r.decay[...] = decay
    r.in_coef[...] = in_coef
    r.out_coef[...] = out_coef
    r.device_decay[...] = jnp.exp(-rate * tokens)
    r.coef_rate[...] = decay * decay / in_coef * r.state_out[...]
    stores = []

    def store(source, target):
        stores.append(pltpu.make_async_copy(source, target, r.store_sem.at[len(stores)]))
        stores[-1].start()

    def wide(k):
        return r.wide[k : k + 1, :]

    def narrow(k):
        return r.narrow[k : k + 1, :]

    def tap(j):
        return narrow(5 + j)

    def features(b):
        return slice(b * LANES, (b + 1) * LANES)

    loads[0].wait()
    values = r.tokens[...]
    centered = values - over_features(values)
    normed = centered * lax.rsqrt(over_features(centered * centered) + EPSILON) * wide(0) + wide(1)
    r.normed1[...] = normed
    store(r.normed1, r.normed1_hbm)
    loads[1].wait()
    r.keys[pl.ds(8, tokens), :] = dot(r.normed1[...], r.key_weight[...], 1, 0) + narrow(1)
    ahead.greeted()

    def halo_copy():
        return remote(
            r.keys.at[pl.ds(tokens, 8)], r.keys.at[pl.ds(0, 8)], r.halo_send.at[0], r.halo_recv.at[0], me + 1
        )

    @pl.when(jnp.logical_not(last))
    def _():
        halo_copy().start()

    loads[2].wait()
    r.value[...] = dot(r.normed1[...], r.value_weight[...], 1, 0) + narrow(2)

    def mix(start, count):
        total = tap(0) * r.keys[pl.ds(8 + start, count), :]
        for j in range(1, SHIFT):
            total = total + tap(j) * r.keys[pl.ds(8 + start - j, count), :]
        r.shifted[pl.ds(start, count), :] = total
        mixed = total * r.value[pl.ds(start, count), :]
        r.mixed[pl.ds(start, count), :] = mixed
        for b in range(blocks):
            r.rows[b, pl.ds(start, count), :] = mixed[:, features(b)]

    mix(8, tokens - 8)

    @pl.when(first)
    def _():
        r.keys[pl.ds(0, 8), :] = jnp.zeros((8, width), F32)

    @pl.when(jnp.logical_not(first))
    def _():
        halo_copy().wait_recv()

    mix(0, 8)

    for b in range(blocks):
        decay, out_coef = r.decay[:, cut(b)], r.out_coef[:, cut(b)]

        def scan(k, state, b=b, decay=decay, out_coef=out_coef):
            r.starts[k, :, cut(b)] = state
            base = pl.multiple_of(k * CHUNK, CHUNK)
            for j in range(CHUNK):
                state = decay * state + r.rows[b, pl.ds(base + j, 1), :]
                r.part[j] = fold_states(out_coef * state)
            r.out[pl.ds(base, CHUNK), cut(b)] = jnp.sum(r.part[...], axis=1)
            return state

        ahead.send_end(b, lax.fori_loop(0, chunks, scan, jnp.zeros_like(decay)), r.ends, ahead_sems)
    loads[3].wait()
    r.query[...] = dot(r.normed1[...], r.query_weight[...], 1, 0) + narrow(0)
    loads[4].wait()
    loads[5].wait()
    befores = []
    for b in range(blocks):
        befores.append(ahead.group_total(b, r.device_decay[:, cut(b)], r.ends, r.totals, ahead_sems))
        if b < 2:
            r.pre_grad[b] = dot(r.cotangent[...], r.down[pl.ds(b * hidden_half, hidden_half), :], 1, 1)

    cotangent_share = Share(
        ahead, r.cotangent, r.cotangent_peer, r.share_send.at[0], r.share_recv.at[0], x_peer, core, other_core
    )
    normed2_share = Share(
        ahead, r.normed2, r.normed2_peer, r.share_send.at[1], r.share_recv.at[1], y_peer, core, other_core
    )
    normed1_share = Share(
        ahead, r.normed1, r.normed1_x, r.share_send.at[2], r.share_recv.at[2], x_peer, core, other_core
    )
    wide_shares = [
        Share(ahead, source, r.wide_y, r.share_send.at[3], r.share_recv.at[3], y_peer, core, other_core)
        for source in (r.middle_grad, r.normed1)
    ]

    def narrow_copy(source, n, target, peer):
        return remote(source, target, r.half_send.at[n], r.half_recv.at[n], peer)

    def key_copy():
        return narrow_copy(r.key_grad, 4, r.narrow_x, x_peer)

    def query_copy():
        return narrow_copy(r.query_grad, 4, r.narrow_x, x_peer)

    def gated_copy():
        return narrow_copy(r.gated, 5, r.narrow_y, y_peer)

    def value_copy():
        return narrow_copy(r.value_grad, 5, r.narrow_y, y_peer)

    cotangent_share.across().start()

    @pl.when(y == 1)
    def _():
        wide_shares[1].across().start()

    for b in range(blocks):
        decay, out_coef = r.decay[:, cut(b)], r.out_coef[:, cut(b)]
        skip = narrow(3)[:, features(b)]

        def carry(k, state, b=b, decay=decay, out_coef=out_coef, skip=skip):
            r.starts[k, :, cut(b)] = r.starts[k, :, cut(b)] + state
            base = pl.multiple_of(k * CHUNK, CHUNK)
            for j in range(CHUNK):
                state = decay * state
                r.part[j] = fold_states(out_coef * state)
            rows = pl.ds(base, CHUNK)
            out = r.out[rows, cut(b)] + jnp.sum(r.part[...], axis=1) + skip * r.mixed[rows, cut(b)]
            r.out[rows, cut(b)] = out
            r.gated[rows, cut(b)] = r.query[rows, cut(b)] * out
            return state

        incoming = ahead.carried(b, r.device_decay[:, cut(b)], befores[b], r.totals, ahead_sems)
        lax.fori_loop(0, chunks, carry, incoming)
    store(r.gated, r.gated_hbm)

    def core_copy(n, source, target):
        return remote(source, target, r.core_send.at[n], r.core_recv.at[n], me, other_core)

    loads[6].wait()
    merged_copies = []
    for n in range(2):
        rows = pl.ds(n * top, top)
        r.merged[rows, :] = dot(r.gated[rows, :], r.out_weight[...], 1, 0)
        copy = core_copy(n, r.merged.at[rows], r.merged_other.at[rows])
        copy.start()
        merged_copies.append(copy)

    @pl.when(y == 0)
    def _():
        gated_copy().start()

    normed1_share.across().start()
    small_start = STATE // 4
    r.small[...] = jnp.zeros_like(r.small)

    def put(k, row):
        r.small[1, pl.ds(small_start + k // 2, 1), pl.ds(k % 2 * width, width)] = row

    spreads = []
    for n, copy in enumerate(merged_copies):
        rows = pl.ds(n * top, top)
        copy.wait_recv()
        middle = r.tokens[rows, :] + (r.merged[rows, :] + r.merged_other[rows, :]) + wide(2)
        centered = middle - over_features(middle)
        inverse = lax.rsqrt(over_features(centered * centered) + EPSILON)
        scaled = centered * inverse
        r.middle[rows, :] = middle
        r.scaled[rows, :] = scaled
        r.normed2[rows, :] = scaled * wide(3) + wide(4)
        spreads.append(inverse)
    normed2_share.across().start()

    loads[7].wait()
    for n in range(2):
        part = pl.ds(n * hidden_half, hidden_half)
        pre = dot(r.normed2[...], r.up[:, part], 1, 0) + wide(6 + n)
        square = pre * pre
        curve = jnp.tanh(GELU_SCALE * (pre + 0.044715 * (square * pre)))
        r.active[n] = 0.5 * pre * (1.0 + curve)
        slope = 0.5 * (1.0 + curve) + 0.5 * pre * (1.0 - curve * curve) * (
            GELU_SCALE * (1.0 + 3 * 0.044715 * square)
        )
        pre_grad = r.pre_grad[n] * slope
        r.pre_grad[n] = pre_grad
        r.small[0, pl.ds(small_start + 6 + n, 1), :] = over_tokens(pre_grad)
    early = tokens * EARLY // 8

    def half_copies(n):
        rows = (pl.ds(0, early), pl.ds(early, tokens - early))[n]
        return (
            remote(
                r.active.at[1 - x, rows], r.active_peer.at[rows], r.half_send.at[2 * n], r.half_recv.at[2 * n], x_peer
            ),
            remote(
                r.pre_grad.at[1 - y, rows],
                r.pre_grad_peer.at[rows],
                r.half_send.at[2 * n + 1],
                r.half_recv.at[2 * n + 1],
                y_peer,
            ),
        )

    for copy in half_copies(0):
        copy.start()
    r.normed_grad[...] = dot(r.pre_grad[0], r.up[:, pl.ds(0, hidden_half)], 1, 1)
    r.normed_grad[...] = r.normed_grad[...] + dot(r.pre_grad[1], r.up[:, pl.ds(hidden_half, hidden_half)], 1, 1)
    normed_grad_copy = core_copy(2, r.normed_grad, r.normed_grad_other)
    normed_grad_copy.start()
    for n in range(2):
        feed = dot(r.active[n], r.down[pl.ds(n * hidden_half, hidden_half), :], 1, 0)
        if n == 0:
            r.feed[...] = feed
        else:
            r.feed[...] = r.feed[...] + feed
    feed_copy = core_copy(3, r.feed, r.feed_other)
    feed_copy.start()
    normed_grad_copy.wait_recv()
    for n in range(2):
        rows = pl.ds(n * top, top)
        normed_grad = r.normed_grad[rows, :] + r.normed_grad_other[rows, :]
        scaled = r.scaled[rows, :]
        scaled_grad = normed_grad * wide(3)
        centered = scaled_grad - over_features(scaled_grad) - scaled * over_features(scaled_grad * scaled)
        middle_grad = r.cotangent[rows, :] + spreads[n] * centered
        r.middle_grad[rows, :] = middle_grad
        sums = (normed_grad * scaled, normed_grad, middle_grad, r.cotangent[rows, :])
        for k, values in enumerate(sums):
            row = pl.ds(small_start + 2 + k, 1)
            if n == 0:
                r.small[0, row, :] = over_tokens(values)
            else:
                r.small[0, row, :] = r.small[0, row, :] + over_tokens(values)
        r.gated_grad[rows, :] = dot(middle_grad, r.out_weight[...], 1, 1)
    store(r.middle_grad, r.middle_grad_hbm)

    grad = r.gated_grad[...] * r.query[...]
    r.grad[...] = grad
    for b in range(blocks):
        r.grad_rows[b] = grad[:, features(b)]
    for b in range(blocks):
        decay = r.decay[:, cut(b)]

        def end(i, adjoint, b=b, decay=decay):
            base = pl.multiple_of((chunks - 1 - i) * CHUNK, CHUNK)
            for j in range(CHUNK - 1, -1, -1):
                adjoint = decay * adjoint + r.grad_rows[b, pl.ds(base + j, 1), :]
            return adjoint

        back.send_end(b, lax.fori_loop(0, chunks, end, jnp.zeros_like(decay)), r.back_ends, back_sems)
    for copy in half_copies(1):
        copy.start()
    query_grad = r.gated_grad[...] * r.out[...]
    r.query_grad[...] = query_grad
    store(r.query_grad, r.query_grad_hbm)
    put(0, over_tokens(r.grad[...] * r.mixed[...]))
    put(5, over_tokens(query_grad))
    cotangent_share.relay()
    normed1_share.relay()
    normed2_share.relay()
    feed_copy.wait_recv()
    r.block_out[...] = r.middle[...] + (r.feed[...] + r.feed_other[...]) + wide(5)
    store(r.block_out, r.block_out_hbm)
    befores = [
        back.group_total(b, r.device_decay[:, cut(b)], r.back_ends, r.back_totals, back_sems) for b in range(blocks)
    ]

    def product(left_ref, right_ref):
        return dot(left_ref[...], right_ref[...], 0, 0)

    r.down_half[...] = product(r.active.at[x], r.cotangent)

    for b in range(blocks):
        if b == 1:

            @pl.when(y == 0)
            def _():
                wide_shares[0].across().start()

            @pl.when(x == 1)
            def _():
                query_copy().start()

        decay, out_coef = r.decay[:, cut(b)], r.out_coef[:, cut(b)]
        skip = narrow(3)[:, features(b)]
        r.coef[:, cut(b)] = jnp.zeros_like(decay)
        r.slope[:, cut(b)] = jnp.zeros_like(decay)

        def chunk(i, adjoint, b=b, decay=decay, out_coef=out_coef, skip=skip):
            k = chunks - 1 - i
            base = pl.multiple_of(k * CHUNK, CHUNK)
            state = r.starts[k, :, cut(b)]
            for j in range(CHUNK):
                r.state[j] = state
                state = decay * state + r.rows[b, pl.ds(base + j, 1), :]
            coef, slope = r.coef[:, cut(b)], r.slope[:, cut(b)]
            for j in range(CHUNK - 1, -1, -1):
                adjoint = decay * adjoint + r.grad_rows[b, pl.ds(base + j, 1), :]
                r.part[j] = fold_states(out_coef * adjoint)
                coef = coef + adjoint * r.rows[b, pl.ds(base + j, 1), :]
                slope = slope + adjoint * r.state[j]
            r.coef[:, cut(b)] = coef
            r.slope[:, cut(b)] = slope
            rows = pl.ds(base, CHUNK)
            grad_mixed = jnp.sum(r.part[...], axis=1) + skip * r.grad[rows, cut(b)]
            r.shifted_grad[rows, cut(b)] = grad_mixed * r.value[rows, cut(b)]
            r.value_grad[rows, cut(b)] = grad_mixed * r.shifted[rows, cut(b)]
            return adjoint

        incoming = back.carried(b, r.device_decay[:, cut(b)], befores[b], r.back_totals, back_sems)
        lax.fori_loop(0, chunks, chunk, incoming)
    store(r.value_grad, r.value_grad_hbm)

    def head_copy():
        return remote(
            r.shifted_grad.at[pl.ds(0, 8)], r.shifted_grad.at[pl.ds(tokens, 8)], r.halo_send.at[1], r.halo_recv.at[1], me - 1
        )

    @pl.when(jnp.logical_not(first))
    def _():
        head_copy().start()

    @pl.when(y == 1)
    def _():
        value_copy().start()

    for j in range(SHIFT):
        put(1 + j, over_tokens(r.shifted_grad[pl.ds(0, tokens), :] * r.keys[pl.ds(8 - j, tokens), :]))
    put(7, over_tokens(r.value_grad[...]))
    r.up_half[...] = product(r.normed2, r.pre_grad.at[y])

    @pl.when(last)
    def _():
        r.shifted_grad[pl.ds(tokens, 8), :] = jnp.zeros((8, width), F32)

    @pl.when(jnp.logical_not(last))
    def _():
        head_copy().wait_recv()

    key_grad = tap(0) * r.shifted_grad[pl.ds(0, tokens), :]
    for j in range(1, SHIFT):
        key_grad = key_grad + tap(j) * r.shifted_grad[pl.ds(j, tokens), :]
    r.key_grad[...] = key_grad
    store(r.key_grad, r.key_grad_hbm)

    @pl.when(x == 0)
    def _():
        key_copy().start()

    put(6, over_tokens(key_grad))

    for p in range(4):
        rows = pl.ds(p * small_start, small_start)
        coef = r.coef[rows, :]
        rate_grad = r.coef_rate[rows, :] * coef - r.decay[rows, :] * r.out_coef[rows, :] * r.slope[rows, :]
        step_grad = over_tokens(r.rate[rows, :] * rate_grad)
        put(8, step_grad if p == 0 else r.small[1, pl.ds(small_start + 4, 1), pl.ds(0, width)] + step_grad)
        r.small[p, pl.ds(0, small_start), pl.ds(0, width)] = narrow(4) * rate_grad
        r.small[p, pl.ds(0, small_start), pl.ds(width, width)] = r.in_coef[rows, :] * coef
    store(r.small, r.small_hbm)
    wide_shares[0].relay()

    cotangent_share.finish()
    normed2_share.finish()
    halves = half_copies(0) + half_copies(1)
    for copy in halves[::2]:
        copy.wait()
    r.down_half[...] = r.down_half[...] + product(r.active_peer, r.cotangent_peer)
    store(r.down_half, r.down_half_hbm)
    for copy in halves[1::2]:
        copy.wait()
    r.up_half[...] = r.up_half[...] + product(r.normed2_peer, r.pre_grad_peer)
    store(r.up_half, r.up_half_hbm)
    normed1_share.finish()
    wide_shares[0].finish()
    key_copy().wait()
    gated_copy().wait()
    for copy in merged_copies + [normed_grad_copy, feed_copy]:
        copy.wait_send()
    ahead.drain(blocks, r.ends, r.totals, ahead_sems)
    back.drain(blocks, r.back_ends, r.back_totals, back_sems)

    @pl.when(jnp.logical_not(last))
    def _():
        halo_copy().wait_send()

    @pl.when(jnp.logical_not(first))
    def _():
        head_copy().wait_send()

    for copy in stores:
        copy.wait()


def front_call(span, inputs, in_hbm, outs, scratch, sems):
    names = [*inputs, *in_hbm, *outs, *scratch, *sems]
    results = pl.pallas_call(
        functools.partial(front_kernel, names, span),
        in_specs=[pl.BlockSpec(memory_space=pltpu.VMEM)] * len(inputs)
        + [pl.BlockSpec(memory_space=pltpu.HBM)] * len(in_hbm),
        out_specs=[pl.BlockSpec(memory_space=pltpu.HBM)] * len(outs),
        out_shape=[shape(*dims) for dims in outs.values()],
        scratch_shapes=[pltpu.VMEM(dims, F32) for dims in scratch.values()]
        + [pltpu.SemaphoreType.DMA(dims) for dims in sems.values()],
        compiler_params=pltpu.CompilerParams(collective_id=1, has_side_effects=True, vmem_limit_bytes=60 * 2**20),
        name="front",
    )(*inputs.values(), *in_hbm.values())
    return types.SimpleNamespace(**dict(zip(outs, results)))


MESH = pl.DeviceIdType.MESH


def is_far(i):
    return lax.rem(i, 5) == 1


class Plan:
    def __init__(self, feed_rows, mixer_rows, rows):
        self.rows = rows
        self.feed, self.mixer = feed_rows // rows, mixer_rows // 2 // rows
        self.small_rows = STATE // 4 + 8
        self.pieces = self.feed + self.mixer + -(-self.small_rows // rows)
        self.total = self.pieces * rows
        self.counts = (self.pieces, self.feed + self.mixer)
        self.feed_rows, self.mixer_rows = feed_rows, mixer_rows


def sum_kernel(
    length, plan, lag,
    small_ref, gain_ref, up_half_ref, down_half_ref, normed_hbm, middle_grad_hbm, gated_hbm, query_grad_hbm, key_grad_hbm,
    value_grad_hbm, normed_x_hbm, narrow_x_hbm, wide_y_hbm, narrow_y_hbm, tokens_hbm, query_hbm, key_hbm, value_hbm,
    out_ref, input_grad_ref,
    normed_ref, middle_grad_ref, gated_ref, query_grad_ref, key_grad_ref, value_grad_ref,
    normed_x_ref, narrow_x_ref, wide_y_ref, narrow_y_ref, tokens_ref,
    sum_ref, got_ref, feed_got_ref, keep_ref, send_ref, mixer_got_ref, small_got_ref, small_sum_ref, weights_ref, local_ref,
    other_ref,
    load_sem, store_sem, chain_send, chain_recv, z_send, z_recv, side_send, side_recv, feed_send, feed_recv,
    mixer_send, mixer_recv, small_send, small_recv, core_send, core_recv
):
    me = lax.axis_index("seq")
    core = lax.axis_index("tp")
    place, quarter = me // 4, lax.rem(me, 4)
    x, y = lax.rem(quarter, 2), quarter // 2
    x_peer, y_peer = me + 1 - 2 * x, me + 2 - 4 * y
    quarter_x, quarter_y, quarter_d = quarter + 1 - 2 * x, quarter + 2 - 4 * y, 3 - quarter
    rows, pieces = plan.rows, plan.pieces
    width = gated_ref.shape[1]
    first = lag * (length - 1)
    spread = SPREAD
    started = (place, length - 1 - place)
    ahead = (me + 4, me - 4)
    behind = (me - 4, me + 4)
    side_peers = (x_peer, y_peer)
    side_bits = (x, y)
    halves = (up_half_ref, down_half_ref)
    barrier = pltpu.get_barrier_semaphore()

    def greet(peer):
        pl.semaphore_signal(barrier, inc=1, device_id={"seq": peer}, device_id_type=MESH)

    greet(x_peer)
    greet(y_peer)
    pl.semaphore_signal(barrier, inc=1, device_id={"tp": 1 - core}, device_id_type=MESH)
    pl.when(place > 0)(lambda: greet(me - 4))
    pl.when(place < length - 1)(lambda: greet(me + 4))
    pairs = [
        (half_ref.at[pl.ds(pl.multiple_of(bit * plan.feed_rows, 8), plan.feed_rows)], sum_ref.at[d, pl.ds(0, plan.feed_rows)])
        for d, (half_ref, bit) in enumerate(zip(halves, side_bits))
    ]
    pairs += [
        (normed_hbm, normed_ref),
        (query_grad_hbm, query_grad_ref),
        (key_grad_hbm, key_grad_ref),
        (normed_x_hbm, normed_x_ref),
        (narrow_x_hbm, narrow_x_ref),
        (gated_hbm, gated_ref),
        (value_grad_hbm, value_grad_ref),
        (middle_grad_hbm, middle_grad_ref),
        (wide_y_hbm, wide_y_ref),
        (narrow_y_hbm, narrow_y_ref),
        (tokens_hbm, tokens_ref),
        (query_hbm, weights_ref.at[0]),
        (key_hbm, weights_ref.at[1]),
        (value_hbm, weights_ref.at[2]),
    ]
    loads = [pltpu.make_async_copy(source, target, load_sem.at[n]) for n, (source, target) in enumerate(pairs)]
    for load in loads:
        load.start()
    pl.semaphore_wait(barrier, 3 + (place > 0).astype(jnp.int32) + (place < length - 1).astype(jnp.int32))

    def remote(source, target, send, recv, peer):
        return pltpu.make_async_remote_copy(
            src_ref=source,
            dst_ref=target,
            send_sem=send,
            recv_sem=recv,
            device_id={"seq": peer},
            device_id_type=MESH,
        )

    def at(i):
        return pl.ds(pl.multiple_of(i * rows, 8), rows)

    def feed_copy(d, i):
        source = pl.ds(pl.multiple_of((1 - side_bits[d]) * plan.feed_rows + i * rows, 8), rows)
        return remote(
            halves[d].at[source], feed_got_ref.at[d, at(i)], feed_send.at[d, i], feed_recv.at[d, i], side_peers[d]
        )

    def send_feed(i, _):
        for d in range(2):
            feed_copy(d, i).start()
        return 0

    lax.fori_loop(0, min(WINDOW, plan.feed), send_feed, 0)

    def features(ref, h):
        return ref[:, pl.ds(pl.multiple_of(h * width, LANES), width)]

    def query_or_key(h):
        narrow = jnp.where(x == 0, query_grad_ref[...], key_grad_ref[...])
        return dot(features(normed_ref, h), narrow, 0, 0) + dot(features(normed_x_ref, h), narrow_x_ref[...], 0, 0)

    def value_or_out(h):
        left = jnp.where(y == 0, features(normed_ref, h), gated_ref[...])
        right = jnp.where(y == 0, value_grad_ref[...], features(middle_grad_ref, h))
        wide, narrow = features(wide_y_ref, h), narrow_y_ref[...]
        return dot(left, right, 0, 0) + dot(jnp.where(y == 0, wide, narrow), jnp.where(y == 0, narrow, wide), 0, 0)

    mixer_copies = [
        remote(send_ref.at[n], mixer_got_ref.at[n], mixer_send.at[n], mixer_recv.at[n], peer)
        for n, peer in enumerate((y_peer, x_peer))
    ]
    for load in loads:
        load.wait()

    def send_mixer():
        send_ref[0] = query_or_key(1 - y)
        mixer_copies[0].start()
        send_ref[1] = value_or_out(1 - x)
        mixer_copies[1].start()


    def chain_copy(d, i):
        return remote(
            sum_ref.at[d, at(i)], got_ref.at[d, at(i)], chain_send.at[d, i], chain_recv.at[d, i], ahead[d]
        )

    def z_copy(d, i, k):
        ref = out_ref.at[(quarter, quarter_x, quarter_y, quarter_d)[k], d, at(i)]
        return remote(ref, ref, z_send.at[d, i, k], z_recv.at[d, i, k], behind[d])

    def side_copy(d, i, k):
        even = lax.rem(i, 2) == 0
        source = (quarter, quarter, jnp.where(even, quarter_x, quarter_y))[k]
        peer = (x_peer, y_peer, jnp.where(even, y_peer, x_peer))[k]
        ref = out_ref.at[source, d, at(i)]
        return remote(ref, ref, side_send.at[d, i, k], side_recv.at[d, i, k], peer)

    def chain_step(d, i):
        @pl.when(i < plan.feed)
        def _():
            feed_copy(d, i).wait_recv()
            sum_ref[d, at(i)] = sum_ref[d, at(i)] + feed_got_ref[d, at(i)]

        @pl.when(started[d] > 0)
        def _():
            chain_copy(d, i).wait_recv()
            sum_ref[d, at(i)] = sum_ref[d, at(i)] + got_ref[d, at(i)]

        @pl.when(started[d] < length - 1)
        def _():
            chain_copy(d, i).start()

        @pl.when(started[d] == length - 1)
        def _():
            store = pltpu.make_async_copy(sum_ref.at[d, at(i)], out_ref.at[quarter, d, at(i)], store_sem.at[d, i])
            store.start()
            store.wait()

    def kind(d, i):
        remaining = length - 1 - started[d]
        far = is_far(i)
        sideways = jnp.logical_or(jnp.logical_not(far), remaining == 0)
        onward = jnp.logical_and(far, remaining < length - 1)
        return remaining, sideways, onward

    def own_step(d, i):
        remaining, sideways, _ = kind(d, i)

        @pl.when(remaining > 0)
        def _():
            z_copy(d, i, 0).wait_recv()

        @pl.when(remaining < length - 1)
        def _():
            z_copy(d, i, 0).start()

        @pl.when(sideways)
        def _():
            side_copy(d, i, 0).start()
            side_copy(d, i, 1).start()

    def side_step(d, i):
        _, sideways, onward = kind(d, i)

        @pl.when(sideways)
        def _():
            side_copy(d, i, 0).wait_recv()
            side_copy(d, i, 1).wait_recv()
            side_copy(d, i, 2).start()

        @pl.when(jnp.logical_not(sideways))
        def _():
            z_copy(d, i, 1).wait_recv()
            z_copy(d, i, 2).wait_recv()

        @pl.when(onward)
        def _():
            z_copy(d, i, 1).start()
            z_copy(d, i, 2).start()

    def last_step(d, i):
        _, sideways, onward = kind(d, i)

        @pl.when(sideways)
        def _():
            side_copy(d, i, 2).wait_recv()

        @pl.when(jnp.logical_not(sideways))
        def _():
            z_copy(d, i, 3).wait_recv()

        @pl.when(onward)
        def _():
            z_copy(d, i, 3).start()

    def tick(t, _):
        @pl.when(t + WINDOW < plan.feed)
        def _():
            send_feed(t + WINDOW, 0)

        steps = ((chain_step, 0), (own_step, first), (last_step, first + SIDE + LAST), (side_step, first + SIDE))
        for step, late in steps:
            for d in range(2):
                passed = lag * started[d] if step is chain_step else spread * (length - 1 - started[d])
                i = t - late - passed
                pl.when(jnp.logical_and(i >= 0, i < plan.counts[d]))(functools.partial(step, d, i))
        return 0

    core_copy = pltpu.make_async_remote_copy(
        src_ref=local_ref,
        dst_ref=other_ref,
        send_sem=core_send.at[0],
        recv_sem=core_recv.at[0],
        device_id={"tp": 1 - core},
        device_id_type=MESH,
    )
    small_x = remote(
        small_sum_ref.at[1 - x], small_got_ref.at[pl.ds(0, 2)], small_send.at[0], small_recv.at[0], x_peer
    )
    small_y = remote(
        small_sum_ref.at[x, 1 - y], small_got_ref.at[2], small_send.at[1], small_recv.at[1], y_peer
    )

    def normed_grad():
        local_ref[...] = (
            dot(query_grad_ref[...], weights_ref[0], 1, 1)
            + dot(key_grad_ref[...], weights_ref[1], 1, 1)
            + dot(value_grad_ref[...], weights_ref[2], 1, 1)
        )
        core_copy.start()

    def first_norm():
        core_copy.wait_recv()
        grad = local_ref[...] + other_ref[...]
        values = tokens_ref[...]
        centered = values - over_features(values)
        inverse = lax.rsqrt(over_features(centered * centered) + EPSILON)
        scaled = centered * inverse
        scaled_grad = grad * gain_ref[...].reshape(1, -1)
        scaled_grad = scaled_grad - over_features(scaled_grad) - scaled * over_features(scaled_grad * scaled)
        input_grad_ref[...] = middle_grad_ref[...] + inverse * scaled_grad
        for p in range(4):
            small_sum_ref[p // 2, p % 2] = small_ref[p]
        small_sum_ref[0, 0, pl.ds(STATE // 4, 1), :] = over_tokens(grad * scaled)
        small_sum_ref[0, 0, pl.ds(STATE // 4 + 1, 1), :] = over_tokens(grad)
        small_x.start()

    def keep_mixer():
        keep_ref[0] = query_or_key(y)
        keep_ref[1] = value_or_out(x)

    def add_small():
        small_x.wait()
        small_sum_ref[x] = small_sum_ref[x] + small_got_ref[pl.ds(0, 2)]
        small_y.start()

    def mixer_sums():
        for copy in mixer_copies:
            copy.wait_recv()
        count = plan.mixer_rows // 2
        for d in range(2):
            source, target = pl.ds(d * count, count), pl.ds(plan.feed_rows, count)
            for n in range(2):
                sum_ref[d, target, pl.ds(n * width, width)] = keep_ref[n, source, :] + mixer_got_ref[n, source, :]

    def small_sums():
        small_y.wait()
        start = plan.feed_rows + plan.mixer_rows // 2
        sum_ref[:, pl.ds(start, plan.total - start), :] = jnp.zeros((2, plan.total - start, sum_ref.shape[2]), F32)
        sum_ref[0, pl.ds(start, plan.small_rows), :] = small_sum_ref[x, y] + small_got_ref[2]

    stages = (
        (1, (send_mixer,)),
        (2, (normed_grad,)),
        (5, (first_norm,)),
        (8, (keep_mixer, add_small)),
        (plan.feed, (mixer_sums, small_sums)),
    )
    at_tick = 0
    for until, work in stages:
        lax.fori_loop(at_tick, until, tick, 0)
        at_tick = until
        for piece in work:
            piece()
    lax.fori_loop(at_tick, first + spread * (length - 1) + SIDE + LAST + pieces, tick, 0)

    def drain(d, i, _):
        remaining, sideways, onward = kind(d, i)
        pl.when(i < plan.feed)(lambda: feed_copy(d, i).wait_send())
        pl.when(remaining > 0)(lambda: chain_copy(d, i).wait_send())
        pl.when(remaining < length - 1)(lambda: z_copy(d, i, 0).wait_send())

        @pl.when(onward)
        def _():
            for k in range(1, 4):
                z_copy(d, i, k).wait_send()

        @pl.when(sideways)
        def _():
            for k in range(3):
                side_copy(d, i, k).wait_send()

        return 0

    for d in range(2):
        lax.fori_loop(0, plan.counts[d], functools.partial(drain, d), 0)
    for copy in mixer_copies + [core_copy]:
        copy.wait_send()


def summed_quarters(plan, lag, args, in_hbm, collective_id):
    length = lax.axis_size("seq") // 4
    pieces, feed = plan.pieces, plan.feed
    tokens, columns = args[4].shape
    width = args[6].shape[1]
    sems = [(16,), (2, pieces), (2, pieces), (2, pieces), (2, pieces, 4), (2, pieces, 4), (2, pieces, 3), (2, pieces, 3)]
    sems += [(2, feed), (2, feed), (2,), (2,), (2,), (2,), (1,), (1,)]
    wide, narrow = (tokens, columns), (tokens, width)
    scratch = [wide, wide, narrow, narrow, narrow, narrow, wide, narrow, wide, narrow, wide]
    scratch += [(2, plan.total, columns)] * 2 + [(2, plan.feed_rows, columns)] + [(2, plan.mixer_rows, width)] * 3
    scratch += [(3, plan.small_rows, columns), (2, 2, plan.small_rows, columns), (3, columns, width)] + [(tokens, columns)] * 2
    return pl.pallas_call(
        functools.partial(sum_kernel, length, plan, lag),
        out_shape=[shape(4, 2, plan.total, columns), shape(tokens, columns)],
        in_specs=[pl.BlockSpec(memory_space=pltpu.HBM if n in in_hbm else pltpu.VMEM) for n in range(len(args))],
        out_specs=[pl.BlockSpec(memory_space=pltpu.HBM), pl.BlockSpec(memory_space=pltpu.VMEM)],
        scratch_shapes=[pltpu.VMEM(dims, F32) for dims in scratch] + [pltpu.SemaphoreType.DMA(dims) for dims in sems],
        compiler_params=pltpu.CompilerParams(
            collective_id=collective_id, has_side_effects=True, vmem_limit_bytes=60 * 2**20
        ),
        name="gradient_sums",
    )(*args)


def unpack_kernel(plan, sums_hbm, block_hbm, grad_hbm, *refs):
    (
        up_ref, down_ref, query_ref, key_ref, value_ref, out_ref, rate_ref, state_out_ref, block_out_ref, input_grad_ref,
        *vector_refs, sums_ref, rows_ref, load_sem, store_sem
    ) = refs
    columns, width = up_ref.shape[0], query_ref.shape[1]
    feed, count, state = plan.feed_rows, plan.mixer_rows // 2, STATE // 4
    loads, stores = [], []

    def load(source, target):
        loads.append(pltpu.make_async_copy(source, target, load_sem.at[len(loads)]))
        loads[-1].start()

    def store(source, target):
        stores.append(pltpu.make_async_copy(source, target, store_sem.at[len(stores)]))
        stores[-1].start()

    def span(start, size):
        return pl.ds(start, size)

    quarters = [(x, y, 2 * y + x) for x in range(2) for y in range(2)]
    for start in (feed, 0):
        for _, _, q in quarters:
            for d in range(2):
                part = span(start, plan.counts[d] * plan.rows - feed if start else feed)
                load(sums_hbm.at[q, d, part], sums_ref.at[q, d, part])
    load(block_hbm, rows_ref.at[0])
    load(grad_hbm, rows_ref.at[1])
    waiting = iter(loads)
    for x, y, q in quarters:
        for d in range(2):
            next(waiting).wait()
            mixer = sums_ref.at[q, d, span(feed, count)]
            target = (query_ref, key_ref)[x]
            store(mixer.at[:, span(0, width)], target.at[span((2 * y + d) * count, count)])
            if y == 0:
                target = value_ref.at[span((2 * x + d) * count, count)]
            else:
                target = out_ref.at[span(d * count, count), span(x * width, width)]
            store(mixer.at[:, span(width, width)], target)
        rows = span((2 * x + y) * state, state)
        last = sums_ref.at[q, 0, span(feed + count, state)]
        store(last.at[:, span(0, width)], rate_ref.at[rows])
        store(last.at[:, span(width, width)], state_out_ref.at[rows])
    for x, y, q in quarters:
        next(waiting).wait()
        store(sums_ref.at[q, 0, span(0, feed)], up_ref.at[span(x * feed, feed), span(y * columns, columns)])
        next(waiting).wait()
        store(sums_ref.at[q, 1, span(0, feed)], down_ref.at[span((2 * x + y) * feed, feed)])
    for n, target in enumerate((block_out_ref, input_grad_ref)):
        next(waiting).wait()
        store(rows_ref.at[n], target)
    *wide_refs, up_bias_ref, skip_ref, taps_ref, query_bias_ref, key_bias_ref, value_bias_ref, step_ref = vector_refs
    row = feed + count + state

    def narrow(k):
        return sums_ref[2, 0, row + k // 2, pl.ds(k % 2 * width, width)]

    for k, ref in enumerate(wide_refs):
        ref[...] = sums_ref[0, 0, row + k, :]
    for k in range(2):
        up_bias_ref[pl.ds(k * columns, columns)] = sums_ref[0, 0, row + 6 + k, :]
    for k in range(SHIFT):
        taps_ref[k, :] = narrow(1 + k)
    for k, ref in ((0, skip_ref), (5, query_bias_ref), (6, key_bias_ref), (7, value_bias_ref), (8, step_ref)):
        ref[...] = narrow(k)
    for item in stores:
        item.wait()


def unpacked(plan, args, matrices, vectors):
    return pl.pallas_call(
        functools.partial(unpack_kernel, plan),
        out_shape=[shape(*out.shape) for out in (*matrices, *args[1:], *vectors)],
        in_specs=[pl.BlockSpec(memory_space=pltpu.HBM)] * 3,
        out_specs=[pl.BlockSpec(memory_space=pltpu.HBM)] * (len(matrices) + 2)
        + [pl.BlockSpec(memory_space=pltpu.VMEM)] * len(vectors),
        scratch_shapes=[
            pltpu.VMEM(args[0].shape, F32),
            pltpu.VMEM((2, *args[1].shape), F32),
            pltpu.SemaphoreType.DMA((18,)),
            pltpu.SemaphoreType.DMA((34,)),
        ],
        compiler_params=pltpu.CompilerParams(vmem_limit_bytes=60 * 2**20),
        name="unpack",
    )(*args)


def on_device(
    tokens,
    cotangent,
    norm1_gain,
    norm1_bias,
    query_weight,
    query_bias,
    key_weight,
    key_bias,
    value_weight,
    value_bias,
    shift_kernel,
    log_step,
    state_rate,
    state_out,
    skip_gain,
    out_weight,
    out_bias,
    norm2_gain,
    norm2_bias,
    up_weight,
    up_bias,
    down_weight,
    down_bias,
):
    rows, columns = tokens.shape
    width = query_weight.shape[1]
    hidden = up_weight.shape[1]
    span = lax.axis_size("seq") // SEQS
    blocks, groups = width // LANES, span // 4
    plan = Plan(columns // 2, width, PIECE_ROWS)
    tok, wide_tok, state, row_blocks = (rows, width), (rows, columns), (STATE, width), (blocks, rows, LANES)
    hidden_tok = (rows, hidden // 2)
    ends, totals = (4, STATE, width), (groups, STATE, width)
    end_sems, total_sems = (blocks, 3), (blocks, max(1, groups - 1))
    front = front_call(
        span,
        dict(
            norm1_gain=norm1_gain,
            norm1_bias=norm1_bias,
            query_bias=query_bias,
            key_bias=key_bias,
            value_bias=value_bias,
            taps=shift_kernel,
            log_step=log_step,
            state_rate=state_rate,
            state_out=state_out,
            skip_gain=skip_gain,
            out_bias=out_bias,
            norm2_gain=norm2_gain,
            norm2_bias=norm2_bias,
            up_bias=up_bias,
            down_bias=down_bias,
        ),
        dict(
            tokens_hbm=tokens,
            key_hbm=key_weight,
            value_hbm=value_weight,
            query_hbm=query_weight,
            cotangent_hbm=cotangent,
            down_hbm=down_weight,
            out_hbm=out_weight,
            up_hbm=up_weight,
        ),
        dict(
            block_out_hbm=wide_tok,
            middle_grad_hbm=wide_tok,
            normed1_hbm=wide_tok,
            gated_hbm=tok,
            query_grad_hbm=tok,
            key_grad_hbm=tok,
            value_grad_hbm=tok,
            small_hbm=(4, plan.small_rows, columns),
            down_half_hbm=(hidden // 2, columns),
            up_half_hbm=(columns, hidden // 2),
            normed1_x=wide_tok,
            narrow_x=tok,
            wide_y=wide_tok,
            narrow_y=tok,
        ),
        dict(
            tokens=wide_tok,
            cotangent=wide_tok,
            key_weight=key_weight.shape,
            value_weight=value_weight.shape,
            query_weight=query_weight.shape,
            out_weight=out_weight.shape,
            up=up_weight.shape,
            down=down_weight.shape,
            normed1=wide_tok,
            keys=(rows + 8, width),
            value=tok,
            query=tok,
            shifted=tok,
            mixed=tok,
            out=tok,
            gated=tok,
            rows=row_blocks,
            grad_rows=row_blocks,
            starts=(rows // CHUNK, STATE, width),
            part=(CHUNK, 8, LANES),
            state=(CHUNK, STATE, LANES),
            ends=ends,
            totals=totals,
            back_ends=ends,
            back_totals=totals,
            merged=wide_tok,
            merged_other=wide_tok,
            middle=wide_tok,
            scaled=wide_tok,
            normed2=wide_tok,
            active=(2, *hidden_tok),
            pre_grad=(2, *hidden_tok),
            normed_grad=wide_tok,
            normed_grad_other=wide_tok,
            feed=wide_tok,
            feed_other=wide_tok,
            active_peer=hidden_tok,
            pre_grad_peer=hidden_tok,
            cotangent_peer=wide_tok,
            normed2_peer=wide_tok,
            middle_grad=wide_tok,
            gated_grad=tok,
            grad=tok,
            query_grad=tok,
            key_grad=tok,
            value_grad=tok,
            shifted_grad=(rows + 8, width),
            coef=state,
            slope=state,
            wide=(8, columns),
            narrow=(16, width),
            rate=state,
            decay=state,
            in_coef=state,
            out_coef=state,
            device_decay=state,
            coef_rate=state,
            small=(4, plan.small_rows, columns),
            block_out=wide_tok,
            down_half=(hidden // 2, columns),
            up_half=(columns, hidden // 2),
        ),
        dict(
            end_send=end_sems,
            end_recv=end_sems,
            total_send=total_sems,
            total_recv=total_sems,
            back_end_send=end_sems,
            back_end_recv=end_sems,
            back_total_send=total_sems,
            back_total_recv=total_sems,
            halo_send=(2,),
            halo_recv=(2,),
            load_sem=(8,),
            store_sem=(10,),
            core_send=(4,),
            core_recv=(4,),
            half_send=(6,),
            half_recv=(6,),
            share_send=(4, 2),
            share_recv=(4, 2),
        ),
    )
    sums, input_grad = summed_quarters(
        plan,
        LAG,
        (front.small_hbm, norm1_gain, front.up_half_hbm, front.down_half_hbm, front.normed1_hbm)
        + (front.middle_grad_hbm, front.gated_hbm, front.query_grad_hbm, front.key_grad_hbm, front.value_grad_hbm)
        + (front.normed1_x, front.narrow_x, front.wide_y, front.narrow_y, tokens, query_weight, key_weight, value_weight),
        range(2, 18),
        3,
    )
    (
        grad_up_weight,
        grad_down_weight,
        grad_query_weight,
        grad_key_weight,
        grad_value_weight,
        grad_out_weight,
        grad_state_rate,
        grad_state_out,
        block_out,
        input_grad,
        grad_norm1_gain,
        grad_norm1_bias,
        grad_norm2_gain,
        grad_norm2_bias,
        grad_out_bias,
        grad_down_bias,
        grad_up_bias,
        grad_skip_gain,
        grad_shift_kernel,
        grad_query_bias,
        grad_key_bias,
        grad_value_bias,
        grad_log_step,
    ) = unpacked(
        plan,
        (sums, front.block_out_hbm, input_grad),
        (up_weight, down_weight, query_weight, key_weight, value_weight, out_weight, state_rate, state_out),
        (norm1_gain, norm1_bias, norm2_gain, norm2_bias, out_bias, down_bias, up_bias, skip_gain, shift_kernel)
        + (query_bias, key_bias, value_bias, log_step),
    )
    return (
        block_out,
        input_grad,
        grad_norm1_gain,
        grad_norm1_bias,
        grad_query_weight,
        grad_query_bias,
        grad_key_weight,
        grad_key_bias,
        grad_value_weight,
        grad_value_bias,
        grad_shift_kernel,
        grad_log_step,
        grad_state_rate,
        grad_state_out,
        grad_skip_gain,
        grad_out_weight,
        grad_out_bias,
        grad_norm2_gain,
        grad_norm2_bias,
        grad_up_weight,
        grad_up_bias,
        grad_down_weight,
        grad_down_bias,
    )


def solution(mesh):
    return jax.shard_map(
        on_device,
        mesh=mesh,
        in_specs=(
            P("seq", None),
            P("seq", None),
            P(),
            P(),
            P(None, "tp"),
            P("tp"),
            P(None, "tp"),
            P("tp"),
            P(None, "tp"),
            P("tp"),
            P(None, "tp"),
            P("tp"),
            P(None, "tp"),
            P(None, "tp"),
            P("tp"),
            P("tp", None),
            P(),
            P(),
            P(),
            P(None, "tp"),
            P("tp"),
            P("tp", None),
            P(),
        ),
        out_specs=(
            P("seq", None),
            P("seq", None),
            P(),
            P(),
            P(None, "tp"),
            P("tp"),
            P(None, "tp"),
            P("tp"),
            P(None, "tp"),
            P("tp"),
            P(None, "tp"),
            P("tp"),
            P(None, "tp"),
            P(None, "tp"),
            P("tp"),
            P("tp", None),
            P(),
            P(),
            P(),
            P(None, "tp"),
            P("tp"),
            P("tp", None),
            P(),
        ),
        check_vma=False,
    )
```
